256 devices in a mesh: wrap: 128 (over z, x_lo, y, core), span: 2 (over x_hi).
Axes of the slice: x: 4 (x_hi: 2, x_lo: 2; x = x_hi * 2 + x_lo), y: 4, z: 8, core: 2. Of those that a mesh axis runs over, the one named last changes fastest.
Arguments:
- cell_xyz: float32 [3, 4096, 16, 128], P(None, 'wrap', 'span'), may hold values from -6 to 6
- panel_xyz: float32 [3, 65536], P(None, 'wrap'), may hold values from -6 to 6
- panel_size: float32 [65536], P('wrap'), may hold values from 1 to 3
- block_lists: int32 [4096, 16, 8], P('wrap', 'span'), may hold values from 0 to 511
- nu_field: float32 [4096, 16, 128], P('wrap', 'span'), may hold values from 0.05 to 1
- vorticity: float32 [4096, 16, 128], P('wrap', 'span'), may hold values from 0.5 to 5
Outputs:
- nu_next: float32 [4096, 16, 128], P('wrap', 'span')
- wall_dist: float32 [4096, 16, 128], P('wrap', 'span')
The draws below stay inside these ranges and needn't reach their ends.
Inputs may be any that keep to these rules, and one draw needn't show every extreme that they name: `block_lists`: each entry names a panel block.
All inputs are finite; a program needn't handle non-finite values.
Results may differ from the reference program's by a relative error of at most 0.00002.
Values sent between devices are 32-bit elements; how exact they have to be, the bound alone decides.
No kernel may reach another device: no remote copies, remote signals or barrier semaphores. Data moves between devices by JAX's collectives and lax.ppermute only.
A program may use at most 64 MiB of HBM per device.

```python
import math
import jax
import jax.numpy as jnp
from jax import lax

J = 128
PBS = 128
NB = 8
W = 4096
K = 16
P_SIZE = 65536
PB = 512


def plant(values, rng, low, top_value):
    index_at = [jax.random.randint(jax.random.fold_in(rng, axis), (), 0, length) for axis, length in enumerate(values.shape)]
    widest = values.shape.index(max(values.shape))
    beside = index_at[:widest] + [(index_at[widest] + 1) % values.shape[widest]] + index_at[widest + 1:]
    return values.at[tuple(index_at)].set(low).at[tuple(beside)].set(top_value)


def block_levels(key, shape, pieces, low, largest):
    level, own = 1.0, jax.random.fold_in(key, 6)
    for dim, blocks in pieces:
        steps = jnp.exp(jax.random.uniform(jax.random.fold_in(own, dim), (blocks,), jnp.float32, low / len(pieces), largest / len(pieces)))
        level = level * jnp.repeat(steps, shape[dim] // blocks).reshape([-1 if axis == dim else 1 for axis in range(len(shape))])
    return level


def bell_draw(stream_key, dims, deviation, bound, pieces=(), dtype=jnp.bfloat16):
    level = block_levels(stream_key, dims, pieces, -0.22, 0.18) if pieces else 1.0
    entries = jax.random.normal(stream_key, dims, jnp.float32) * deviation * level
    return jnp.minimum(jnp.maximum(entries, -bound), bound).astype(dtype)


def setup_inputs(seed: int = 0) -> dict:
    key_list = jax.random.split(jax.random.key(seed), 7)
    return {
        "cell_xyz": bell_draw(key_list[0], (3, W, K, J), 1.0, 6.0, ((1, 128), (2, 2)), jnp.float32),
        "panel_xyz": bell_draw(key_list[1], (3, P_SIZE), 1.0, 6.0, ((1, 128),), jnp.float32),
        "panel_size": jnp.clip(jnp.exp(math.log(3.0) - 1.0986123 * jax.random.uniform(key_list[2], (P_SIZE,), jnp.float32) ** block_levels(key_list[2], (P_SIZE,), ((0, 128),), -0.2, 0.2)), 1.0, 3.0),
        "block_lists": plant(jax.random.randint(key_list[3], (W, K, NB), 0, PB), jax.random.fold_in(key_list[3], 1), 0, PB - 1).astype(jnp.int32),
        "nu_field": jnp.clip(jnp.exp(math.log(1.0) - 2.9957323 * jax.random.uniform(key_list[4], (W, K, J), jnp.float32) ** block_levels(key_list[4], (W, K, J), ((0, 128), (1, 2)), -0.2, 0.2)), 0.05, 1.0),
        "vorticity": jnp.clip(jnp.exp(math.log(5.0) - 2.3025851 * jax.random.uniform(key_list[5], (W, K, J), jnp.float32) ** block_levels(key_list[5], (W, K, J), ((0, 128), (1, 2)), -0.2, 0.2)), 0.5, 5.0),
    }


coef_cb1 = 0.1355
coef_cb2 = 0.622
coef_sigma = 2.0 / 3.0
coef_kappa = 0.41
coef_cw2 = 0.3
coef_cw3 = 2.0
viscous = 1.0
time_step = 0.03
coef_cw1 = coef_cb1 / coef_kappa ** 2 + (1.0 + coef_cb2) / coef_sigma

def line_squares(cells, blocks_xyz, blocks_size, listed):
    line_count = listed.shape[0]
    chosen = blocks_xyz[:, listed, :].reshape(3, line_count, 1, -1)
    radius = blocks_size[listed, :].reshape(line_count, 1, -1)
    summed = radius * radius
    for component in range(3):
        offset = cells[component][:, :, None] - chosen[component]
        summed = summed + offset * offset
    return lax.optimization_barrier(jnp.min(summed, axis=2))

def update_rate(current, neighbours, squares, vorticity):
    face_flux = jnp.zeros_like(current)
    for beside in neighbours:
        change = beside - current
        face_flux = face_flux + (1.0 + coef_cb2) * (viscous + 0.5 * (current + beside)) * change - coef_cb2 * (viscous + current) * change
    diffusion = face_flux / coef_sigma
    scaled = coef_kappa ** 2 * squares
    modified = vorticity + current / scaled
    wall_ratio = current / (modified * scaled)
    shaped = wall_ratio + coef_cw2 * (wall_ratio ** 6 - wall_ratio)
    factor = shaped * ((1.0 + coef_cw3 ** 6) / (shaped ** 6 + coef_cw3 ** 6)) ** (1.0 / 6.0)
    return diffusion + coef_cb1 * modified * current - coef_cw1 * factor * current * current / squares

def reference_rate(current, squares, vorticity):
    extent = current.shape[0]
    positions = jnp.arange(extent)
    in_wake = (positions < extent // 4) | (positions >= extent - extent // 4)
    ghost_row = jnp.where(in_wake[:, None], current[::-1, :, 0], -current[:, :, 0])
    neighbours = (jnp.concatenate([current[:1], current[:-1]], axis=0), jnp.concatenate([current[1:], current[-1:]], axis=0), jnp.concatenate([current[:, :1], current[:, :-1]], axis=1), jnp.concatenate([current[:, 1:], current[:, -1:]], axis=1), jnp.concatenate([ghost_row[:, :, None], current[:, :, :-1]], axis=2), jnp.concatenate([current[:, :, 1:], current[:, :, -1:]], axis=2))
    return update_rate(current, neighbours, squares, vorticity)

def reference(cell_xyz, panel_xyz, panel_size, block_lists, nu_field, vorticity):
    blocks_xyz = panel_xyz.reshape(3, -1, PBS)
    blocks_size = panel_size.reshape(-1, PBS)

    def per_index(packed):
        return line_squares(packed[0], blocks_xyz, blocks_size, packed[1])
    squares = lax.map(per_index, (jnp.moveaxis(cell_xyz, 1, 0), block_lists))
    middle = nu_field + 0.5 * time_step * reference_rate(nu_field, squares, vorticity)
    nu_next = nu_field + time_step * reference_rate(middle, squares, vorticity)
    return (nu_next, jnp.sqrt(squares))
```

```python
import functools

import jax
import jax.numpy as jnp
from jax import lax
from jax.experimental import pallas as pl
from jax.experimental.pallas import tpu as pltpu
from jax.sharding import PartitionSpec as P

BF = jnp.bfloat16
F32 = jnp.float32
PBS = 128
FEATS = 48
LINES_PER_STEP = 32
STAGES = ((6, 5), (4, 3), (2, 1), (0,))

coef_cb1 = 0.1355
coef_cb2 = 0.622
coef_sigma = 2.0 / 3.0
coef_kappa = 0.41
coef_cw2 = 0.3
coef_cw3 = 2.0
viscous = 1.0
time_step = 0.03
coef_cw1 = coef_cb1 / coef_kappa**2 + (1.0 + coef_cb2) / coef_sigma


def split_rows(rows):
    high = rows.astype(BF).astype(F32)
    rest = rows - high
    mid = rest.astype(BF).astype(F32)
    return high, mid, rest - mid


def panel_features(rows):
    high, mid, low = split_rows(rows)
    return jnp.concatenate([high, high, high, mid, mid, low], 0).astype(BF)


def cell_features(rows):
    high, mid, low = split_rows(rows)
    return jnp.concatenate([high, mid, low, high, mid, high], 0).astype(BF)


def cells_kernel(rows_ref, out_ref):
    lines = rows_ref.shape[0]
    per_step = 8

    def body(step, carry):
        for part in range(per_step):
            line = step * per_step + part
            feats = cell_features(rows_ref[line])
            out_ref[pl.ds(pl.multiple_of(line * 128, 128), 128), :] = feats.T
        return carry

    lax.fori_loop(0, lines // per_step, body, 0)


def squares_kernel(place_ref, panels_ref, cells_ref, norm_ref, squares_ref, dist_ref, table_ref):
    blocks = table_ref.shape[0]
    per_step = 4

    def build(step, carry):
        for part in range(per_step):
            pair = step * per_step + part
            rows = panels_ref[pl.ds(pl.multiple_of(pair * 8, 8), 8), :]
            table_ref[pair * 2] = panel_features(rows)
            table_ref[pair * 2 + 1] = panel_features(jnp.concatenate([rows[4:], rows[:4]], 0))
        return carry

    lax.fori_loop(0, blocks // 2 // per_step, build, 0)
    tiles = squares_ref.shape[0]
    tiles_per_step = LINES_PER_STEP // 8

    def body(step, carry):
        for part in range(tiles_per_step):
            tile = step * tiles_per_step + part
            found = []
            for sub in range(8):
                line = tile * 8 + sub
                cells = cells_ref[pl.ds(pl.multiple_of(line * 128, 128), 128), :]
                nearest = None
                for slot in range(0, 8, 2):
                    first = place_ref[line * 8 + slot]
                    second = place_ref[line * 8 + slot + 1]
                    panels = jnp.concatenate([table_ref[first], table_ref[second]], 1)
                    value = jnp.dot(cells, panels, preferred_element_type=F32)
                    value = jnp.minimum(value[:, :128], value[:, 128:])
                    nearest = value if nearest is None else jnp.minimum(nearest, value)
                turned = jnp.min(nearest.T.reshape(16, 8, 128), axis=0)
                found.append(jnp.min(turned, axis=0, keepdims=True))
            squares = jnp.concatenate(found, 0) + norm_ref[tile]
            squares_ref[tile] = squares
            dist_ref[tile] = jnp.sqrt(squares)
        return carry

    lax.fori_loop(0, tiles // tiles_per_step, body, 0)


def section_kernel(
    step_size,
    flags_ref,
    current_ref,
    lower_ref,
    upper_ref,
    beside_ref,
    ghost_ref,
    squares_ref,
    vorticity_ref,
    base_ref,
    out_ref,
):
    rows = current_ref.shape[0]
    at_first = flags_ref[0] == 1
    at_last = flags_ref[1] == 1
    at_low_span = flags_ref[2] == 1
    in_wake = flags_ref[3] == 1
    lane = lax.broadcasted_iota(jnp.int32, (8, 128), 1)
    sub = lax.broadcasted_iota(jnp.int32, (8, 128), 0)

    for row in range(rows):
        value = current_ref[row]
        if row == 0:
            below = jnp.where(at_first, value, lower_ref[0])
        else:
            below = current_ref[row - 1]
        if row == rows - 1:
            above = jnp.where(at_last, value, upper_ref[0])
        else:
            above = current_ref[row + 1]
        across = jnp.broadcast_to(beside_ref[row : row + 1, :], (8, 128))
        span_low = jnp.where(at_low_span, value, across)
        span_high = jnp.where(at_low_span, across, value)
        span_below = jnp.where(sub == 0, span_low, pltpu.roll(value, 1, 0))
        span_above = jnp.where(sub == 7, span_high, pltpu.roll(value, 7, 0))
        ghost = jnp.where(in_wake, ghost_ref[row], -value)
        normal_below = jnp.where(lane == 0, ghost, pltpu.roll(value, 1, 1))
        normal_above = jnp.where(lane == 127, value, pltpu.roll(value, 127, 1))
        sums = jnp.zeros_like(value)
        squared = jnp.zeros_like(value)
        for other in (below, above, span_below, span_above, normal_below, normal_above):
            change = other - value
            sums = sums + change
            squared = squared + change * change
        flux = (viscous + value) * sums + (0.5 * (1.0 + coef_cb2)) * squared
        squares = squares_ref[row]
        scaled = coef_kappa**2 * squares
        modified = vorticity_ref[row] + value / scaled
        ratio = value / (modified * scaled)
        ratio2 = ratio * ratio
        shaped = ratio + coef_cw2 * (ratio2 * ratio2 * ratio2 - ratio)
        shaped2 = shaped * shaped
        base = (1.0 + coef_cw3**6) / (shaped2 * shaped2 * shaped2 + coef_cw3**6)
        factor = shaped * jnp.exp(jnp.log(base) * (1.0 / 6.0))
        rate = (
            flux / coef_sigma
            + coef_cb1 * modified * value
            - coef_cw1 * factor * value * value / squares
        )
        out_ref[row] = base_ref[row] + step_size * rate


def section(step_size, flags, current, base, squares, vorticity):
    devices = lax.axis_size("wrap")
    rows = current.shape[0]
    low_span = lax.axis_index("span") == 0
    lower = lax.ppermute(current[-1:], "wrap", [(i, i + 1) for i in range(devices - 1)])
    upper = lax.ppermute(current[:1], "wrap", [(i + 1, i) for i in range(devices - 1)])
    sent = jnp.where(low_span, current[:, -1], current[:, 0])
    beside = lax.ppermute(sent, "span", [(0, 1), (1, 0)])
    partner = lax.ppermute(
        current[:, :, 0], "wrap", [(i, devices - 1 - i) for i in range(devices)]
    )[::-1]
    ghost = jnp.broadcast_to(partner[:, :, None], current.shape)
    smem = pl.BlockSpec(memory_space=pltpu.SMEM)
    vmem = pl.BlockSpec(memory_space=pltpu.VMEM)
    return pl.pallas_call(
        functools.partial(section_kernel, step_size),
        out_shape=jax.ShapeDtypeStruct(current.shape, F32),
        in_specs=[smem] + [vmem] * 8,
        out_specs=vmem,
        name="section",
    )(flags, current, lower, upper, beside, ghost, squares, vorticity, base)


def gather(shard):
    devices = lax.axis_size("wrap")
    for bits in STAGES:
        parts = [shard]
        for choice in range(1, 1 << len(bits)):
            mask = sum(((choice >> n) & 1) << bit for n, bit in enumerate(bits))
            parts.append(lax.ppermute(shard, "wrap", [(i, i ^ mask) for i in range(devices)]))
        shard = jnp.concatenate(parts, 0)
    return shard


def slot_of(device):
    mask = device ^ lax.axis_index("wrap")
    order = [bit for bits in STAGES for bit in bits]
    return sum(((mask >> bit) & 1) << place for place, bit in enumerate(order))


def shards(cell_xyz, panel_xyz, panel_size, block_lists, nu_field, vorticity):
    devices = lax.axis_size("wrap")
    wrap_place = lax.axis_index("wrap")
    local_wrap, local_span, normal_cells = nu_field.shape
    lines = local_wrap * local_span
    own_blocks = panel_size.shape[0] // PBS

    offset = jnp.sum(panel_xyz * panel_xyz, axis=0) + panel_size * panel_size
    packed = jnp.concatenate([panel_xyz, offset[None]], 0).reshape(4, own_blocks, PBS)
    panels = gather(jnp.swapaxes(packed, 0, 1).reshape(own_blocks * 4, PBS))

    places = slot_of(block_lists // own_blocks) * own_blocks + block_lists % own_blocks
    places = places.reshape(lines * block_lists.shape[2])

    norm = jnp.sum(cell_xyz * cell_xyz, axis=0)
    flat = cell_xyz.reshape(3, lines, normal_cells)
    filler = jnp.zeros_like(flat[0])
    cell_rows = jnp.stack(
        [-2.0 * flat[0], -2.0 * flat[1], -2.0 * flat[2], filler + 1.0] + [filler] * 4, 1
    )
    smem = pl.BlockSpec(memory_space=pltpu.SMEM)
    vmem = pl.BlockSpec(memory_space=pltpu.VMEM)
    cells = pl.pallas_call(
        cells_kernel,
        out_shape=jax.ShapeDtypeStruct((lines * normal_cells, FEATS), BF),
        in_specs=[vmem],
        out_specs=vmem,
        compiler_params=pltpu.CompilerParams(vmem_limit_bytes=24 * 2**20),
        name="cells",
    )(cell_rows)
    like = jax.ShapeDtypeStruct(nu_field.shape, F32)
    squares, dist = pl.pallas_call(
        squares_kernel,
        out_shape=(like, like),
        in_specs=[smem, vmem, vmem, vmem],
        out_specs=(vmem, vmem),
        scratch_shapes=[pltpu.VMEM((devices * own_blocks, FEATS, PBS), BF)],
        compiler_params=pltpu.CompilerParams(vmem_limit_bytes=32 * 2**20),
        name="squares",
    )(places, panels, cells, norm)

    wake = (wrap_place < devices // 4) | (wrap_place >= devices - devices // 4)
    flags = jnp.stack(
        [wrap_place == 0, wrap_place == devices - 1, lax.axis_index("span") == 0, wake]
    ).astype(jnp.int32)
    middle = section(0.5 * time_step, flags, nu_field, nu_field, squares, vorticity)
    nu_next = section(time_step, flags, middle, nu_field, squares, vorticity)
    return (nu_next, dist)


def solution(mesh):
    in_specs = (
        P(None, "wrap", "span", None),
        P(None, "wrap"),
        P("wrap"),
        P("wrap", "span", None),
        P("wrap", "span", None),
        P("wrap", "span", None),
    )
    out_specs = (P("wrap", "span", None), P("wrap", "span", None))
    return jax.shard_map(shards, mesh=mesh, in_specs=in_specs, out_specs=out_specs, check_vma=False)
```

```python
import functools

import jax
import jax.numpy as jnp
from jax import lax
from jax.experimental import pallas as pl
from jax.experimental.pallas import tpu as pltpu
from jax.sharding import PartitionSpec as P

BF = jnp.bfloat16
F32 = jnp.float32
PBS = 128
FEATS = 48
LINES_PER_STEP = 32
STAGES = ((6, 5), (4, 3), (2, 1), (0,))

coef_cb1 = 0.1355
coef_cb2 = 0.622
coef_sigma = 2.0 / 3.0
coef_kappa = 0.41
coef_cw2 = 0.3
coef_cw3 = 2.0
viscous = 1.0
time_step = 0.03
coef_cw1 = coef_cb1 / coef_kappa**2 + (1.0 + coef_cb2) / coef_sigma

SMEM = pl.BlockSpec(memory_space=pltpu.SMEM)
VMEM = pl.BlockSpec(memory_space=pltpu.VMEM)


def tile_iota(dim):
    return lax.broadcasted_iota(jnp.int32, (8, 128), dim)


def split_rows(rows):
    high = rows.astype(BF).astype(F32)
    rest = rows - high
    mid = rest.astype(BF).astype(F32)
    return high, mid, rest - mid


def panel_features(rows):
    high, mid, low = split_rows(rows)
    return jnp.concatenate([high, high, high, mid, mid, low], 0).astype(BF)


def cell_features(rows):
    high, mid, low = split_rows(rows)
    return jnp.concatenate([high, mid, low, high, mid, high], 0).astype(BF)


def edge_row(value, low_span):
    return jnp.where(low_span, value[7:8], value[0:1])


def first_column(value):
    return jnp.broadcast_to(value[:, 0:1], (8, 128))


def prep_kernel(xyz_ref, size_ref, nu_ref, message_ref, last_ref, first_ref, beside_ref, column_ref):
    low_span = lax.axis_index("span") == 0
    own_blocks = size_ref.shape[1] // PBS
    for block in range(own_blocks):
        lanes = slice(block * PBS, (block + 1) * PBS)
        xyz = xyz_ref[:, lanes]
        size = size_ref[:, lanes]
        offset = jnp.sum(xyz * xyz, axis=0, keepdims=True) + size * size
        message_ref[block * 4 : block * 4 + 3, :] = xyz
        message_ref[block * 4 + 3 : block * 4 + 4, :] = offset
    rows = nu_ref.shape[0]
    last_ref[...] = nu_ref[rows - 1]
    first_ref[...] = nu_ref[0]
    lane = tile_iota(1)
    column = jnp.zeros((8, 128), F32)
    for row in range(rows):
        value = nu_ref[row]
        beside_ref[row : row + 1, :] = edge_row(value, low_span)
        column = jnp.where(lane == row, first_column(value), column)
    column_ref[...] = column


class Halo:
    def __init__(self, nu_ref, last_ref, first_ref, beside_ref, column_ref, padded_ref, ghost_ref):
        devices = lax.axis_size("wrap")
        place = lax.axis_index("wrap")
        rows = nu_ref.shape[0]
        self.rows = rows
        self.low_span = lax.axis_index("span") == 0
        self.padded, self.ghost, self.beside = padded_ref, ghost_ref, beside_ref
        padded_ref[0] = jnp.where(place == 0, nu_ref[0], last_ref[...])
        padded_ref[rows + 1] = jnp.where(place == devices - 1, nu_ref[rows - 1], first_ref[...])
        in_wake = (place < devices // 4) | (place >= devices - devices // 4)
        column = column_ref[...]
        for row in range(rows):
            value = nu_ref[row]
            padded_ref[row + 1] = value
            partner = jnp.broadcast_to(column[:, rows - 1 - row : rows - row], (8, 128))
            ghost_ref[row] = jnp.where(in_wake, partner, -value)

    def rate(self, row, squares, vorticity):
        value = self.padded[row + 1]
        sub, lane = tile_iota(0), tile_iota(1)
        across = jnp.broadcast_to(self.beside[pl.ds(row, 1), :], (8, 128))
        span_low = jnp.where(self.low_span, value, across)
        span_high = jnp.where(self.low_span, across, value)
        others = (
            self.padded[row],
            self.padded[row + 2],
            jnp.where(sub == 0, span_low, pltpu.roll(value, 1, 0)),
            jnp.where(sub == 7, span_high, pltpu.roll(value, 7, 0)),
            jnp.where(lane == 0, self.ghost[row], pltpu.roll(value, 1, 1)),
            jnp.where(lane == 127, value, pltpu.roll(value, 127, 1)),
        )
        sums = jnp.zeros_like(value)
        squared = jnp.zeros_like(value)
        for other in others:
            change = other - value
            sums = sums + change
            squared = squared + change * change
        flux = (viscous + value) * sums + (0.5 * (1.0 + coef_cb2)) * squared
        scaled = coef_kappa**2 * squares
        modified = vorticity + value / scaled
        ratio = value / (modified * scaled)
        ratio2 = ratio * ratio
        shaped = ratio + coef_cw2 * (ratio2 * ratio2 * ratio2 - ratio)
        shaped2 = shaped * shaped
        base = (1.0 + coef_cw3**6) / (shaped2 * shaped2 * shaped2 + coef_cw3**6)
        factor = shaped * jnp.exp(jnp.log(base) * (1.0 / 6.0))
        return (
            flux / coef_sigma
            + coef_cb1 * modified * value
            - coef_cw1 * factor * value * value / squares
        )


def build_table(halves, table_ref):
    place = lax.axis_index("wrap")
    order = [bit for bits in STAGES for bit in bits]
    own_blocks = table_ref.shape[0] // lax.axis_size("wrap")
    slots = halves[0].shape[0] // (4 * own_blocks)
    top = len(order) - 1

    def body(slot, carry):
        for half, ref in enumerate(halves):
            mask = half << order[top]
            for n in range(top):
                mask = mask | (((slot >> n) & 1) << order[n])
            base = (place ^ mask) * own_blocks
            for pair in range(own_blocks // 2):
                start = pl.multiple_of(slot * own_blocks * 4 + pair * 8, 8)
                rows = ref[pl.ds(start, 8), :]
                table_ref[base + pair * 2] = panel_features(rows)
                table_ref[base + pair * 2 + 1] = panel_features(pltpu.roll(rows, 4, 0))
        return carry

    lax.fori_loop(0, slots, body, 0)


def nearest_tile(tile, list_ref, cell_ref, table_ref):
    sub = tile_iota(0)
    unit = jnp.where(sub == 3, 1.0, 0.0)
    xyz = [cell_ref[component, tile] for component in range(3)]
    twice = [-2.0 * part for part in xyz]
    found = []
    for line in range(8):
        rows = unit
        for component in range(3):
            spread = jnp.broadcast_to(twice[component][line : line + 1], (8, 128))
            rows = jnp.where(sub == component, spread, rows)
        cells = cell_features(rows).T
        nearest = None
        for slot in range(0, 8, 2):
            first = list_ref[(tile * 8 + line) * 8 + slot]
            second = list_ref[(tile * 8 + line) * 8 + slot + 1]
            panels = jnp.concatenate([table_ref[first], table_ref[second]], 1)
            value = jnp.dot(cells, panels, preferred_element_type=F32)
            value = jnp.minimum(value[:, :128], value[:, 128:])
            nearest = value if nearest is None else jnp.minimum(nearest, value)
        turned = jnp.min(nearest.T.reshape(16, 8, 128), axis=0)
        found.append(jnp.min(turned, axis=0, keepdims=True))
    norm = xyz[0] * xyz[0] + xyz[1] * xyz[1] + xyz[2] * xyz[2]
    return jnp.concatenate(found, 0) + norm


def main_kernel(
    list_ref,
    own_ref,
    other_ref,
    cell_ref,
    nu_ref,
    vorticity_ref,
    last_ref,
    first_ref,
    beside_ref,
    column_ref,
    dist_ref,
    squares_ref,
    middle_ref,
    last_out,
    first_out,
    beside_out,
    column_out,
    table_ref,
    padded_ref,
    ghost_ref,
):
    halo = Halo(nu_ref, last_ref, first_ref, beside_ref, column_ref, padded_ref, ghost_ref)
    build_table((own_ref, other_ref), table_ref)
    tiles = nu_ref.shape[0]
    per_step = LINES_PER_STEP // 8

    def body(step, column):
        lane = tile_iota(1)
        for part in range(per_step):
            tile = step * per_step + part
            squares = nearest_tile(tile, list_ref, cell_ref, table_ref)
            squares_ref[tile] = squares
            dist_ref[tile] = jnp.sqrt(squares)
            rate = halo.rate(tile, squares, vorticity_ref[tile])
            middle = nu_ref[tile] + 0.5 * time_step * rate
            middle_ref[tile] = middle
            beside_out[pl.ds(tile, 1), :] = edge_row(middle, halo.low_span)
            column = jnp.where(lane == tile, first_column(middle), column)
        return column

    column_out[...] = lax.fori_loop(0, tiles // per_step, body, jnp.zeros((8, 128), F32))
    last_out[...] = middle_ref[tiles - 1]
    first_out[...] = middle_ref[0]


def last_kernel(
    middle_ref,
    nu_ref,
    squares_ref,
    vorticity_ref,
    last_ref,
    first_ref,
    beside_ref,
    column_ref,
    next_ref,
    padded_ref,
    ghost_ref,
):
    halo = Halo(middle_ref, last_ref, first_ref, beside_ref, column_ref, padded_ref, ghost_ref)
    for row in range(nu_ref.shape[0]):
        rate = halo.rate(row, squares_ref[row], vorticity_ref[row])
        next_ref[row] = nu_ref[row] + time_step * rate


def exchange(last, first, beside, column):
    devices = lax.axis_size("wrap")
    column = lax.ppermute(column, "wrap", [(i, devices - 1 - i) for i in range(devices)])
    last = lax.ppermute(last, "wrap", [(i, i + 1) for i in range(devices - 1)])
    first = lax.ppermute(first, "wrap", [(i + 1, i) for i in range(devices - 1)])
    beside = lax.ppermute(beside, "span", [(0, 1), (1, 0)])
    return last, first, beside, column


def gather(shard):
    devices = lax.axis_size("wrap")
    for bits in STAGES[:-1]:
        parts = [shard]
        for choice in range(1, 1 << len(bits)):
            mask = sum(((choice >> n) & 1) << bit for n, bit in enumerate(bits))
            parts.append(lax.ppermute(shard, "wrap", [(i, i ^ mask) for i in range(devices)]))
        shard = jnp.concatenate(parts, 0)
    mask = 1 << STAGES[-1][0]
    return shard, lax.ppermute(shard, "wrap", [(i, i ^ mask) for i in range(devices)])


def shards(cell_xyz, panel_xyz, panel_size, block_lists, nu_field, vorticity):
    devices = lax.axis_size("wrap")
    rows, span, cells = nu_field.shape
    own_blocks = panel_size.shape[0] // PBS
    tile = jax.ShapeDtypeStruct((span, cells), F32)
    field = jax.ShapeDtypeStruct(nu_field.shape, F32)
    side = jax.ShapeDtypeStruct((rows, cells), F32)
    edges = (tile, tile, side, tile)
    scratch = [pltpu.VMEM((rows + 2, span, cells), F32), pltpu.VMEM(nu_field.shape, F32)]

    message, *sent = pl.pallas_call(
        prep_kernel,
        out_shape=(jax.ShapeDtypeStruct((4 * own_blocks, PBS), F32),) + edges,
        in_specs=[VMEM] * 3,
        out_specs=(VMEM,) * 5,
        compiler_params=pltpu.CompilerParams(vmem_limit_bytes=4 * 2**20),
        name="prep",
    )(panel_xyz, panel_size[None], nu_field)
    own, other = gather(message)
    halos = exchange(*sent)

    dist, squares, middle, *sent = pl.pallas_call(
        main_kernel,
        out_shape=(field, field, field) + edges,
        in_specs=[SMEM] + [VMEM] * 9,
        out_specs=(VMEM,) * 7,
        scratch_shapes=[pltpu.VMEM((devices * own_blocks, FEATS, PBS), BF)] + scratch,
        compiler_params=pltpu.CompilerParams(vmem_limit_bytes=24 * 2**20),
        cost_estimate=pl.CostEstimate(
            flops=2 * 128 * rows * span * cells * block_lists.shape[2] * PBS,
            bytes_accessed=4 * 2**20,
            transcendentals=0,
        ),
        name="main",
    )(block_lists.reshape(-1), own, other, cell_xyz, nu_field, vorticity, *halos)
    halos = exchange(*sent)

    nu_next = pl.pallas_call(
        last_kernel,
        out_shape=field,
        in_specs=[VMEM] * 8,
        out_specs=VMEM,
        scratch_shapes=scratch,
        compiler_params=pltpu.CompilerParams(vmem_limit_bytes=8 * 2**20),
        name="last",
    )(middle, nu_field, squares, vorticity, *halos)
    return (nu_next, dist)


def solution(mesh):
    in_specs = (
        P(None, "wrap", "span", None),
        P(None, "wrap"),
        P("wrap"),
        P("wrap", "span", None),
        P("wrap", "span", None),
        P("wrap", "span", None),
    )
    out_specs = (P("wrap", "span", None), P("wrap", "span", None))
    return jax.shard_map(shards, mesh=mesh, in_specs=in_specs, out_specs=out_specs, check_vma=False)
```

```python
import functools

import jax
import jax.numpy as jnp
from jax import lax
from jax.experimental import pallas as pl
from jax.experimental.pallas import tpu as pltpu
from jax.sharding import PartitionSpec as P

BF = jnp.bfloat16
F32 = jnp.float32
PBS = 128
FEATS = 48
LINES_PER_STEP = 32
STAGES = ((6, 5), (4, 3), (2, 1), (0,))

coef_cb1 = 0.1355
coef_cb2 = 0.622
coef_sigma = 2.0 / 3.0
coef_kappa = 0.41
coef_cw2 = 0.3
coef_cw3 = 2.0
viscous = 1.0
time_step = 0.03
coef_cw1 = coef_cb1 / coef_kappa**2 + (1.0 + coef_cb2) / coef_sigma

SMEM = pl.BlockSpec(memory_space=pltpu.SMEM)
VMEM = pl.BlockSpec(memory_space=pltpu.VMEM)


def tile_iota(dim):
    return lax.broadcasted_iota(jnp.int32, (8, 128), dim)


def split_rows(rows):
    high = rows.astype(BF).astype(F32)
    rest = rows - high
    mid = rest.astype(BF).astype(F32)
    return high, mid, rest - mid


def panel_features(rows):
    high, mid, low = split_rows(rows)
    return jnp.concatenate([high, high, high, mid, mid, low], 0).astype(BF)


def cell_features(rows):
    high, mid, low = split_rows(rows)
    return jnp.concatenate([high, mid, low, high, mid, high], 0).astype(BF)


def edge_row(value, low_span):
    return jnp.where(low_span, value[7:8], value[0:1])


def first_column(value):
    return jnp.broadcast_to(value[:, 0:1], (8, 128))


def message_kernel(xyz_hbm, size_hbm, message_ref, xyz_ref, size_ref, sems):
    copies = [
        pltpu.make_async_copy(xyz_hbm, xyz_ref, sems.at[0]),
        pltpu.make_async_copy(size_hbm, size_ref, sems.at[1]),
    ]
    for copy in copies:
        copy.start()
    for copy in copies:
        copy.wait()
    for block in range(size_ref.shape[1] // PBS):
        lanes = slice(block * PBS, (block + 1) * PBS)
        xyz = xyz_ref[:, lanes]
        size = size_ref[:, lanes]
        offset = jnp.sum(xyz * xyz, axis=0, keepdims=True) + size * size
        message_ref[block * 4 : block * 4 + 3, :] = xyz
        message_ref[block * 4 + 3 : block * 4 + 4, :] = offset


def even_place():
    return lax.rem(lax.axis_index("wrap"), 2) == 0


def put_edges(first, last, pair_ref, next_ref):
    pair_ref[...] = jnp.where(even_place(), last, first)
    next_ref[...] = jnp.where(even_place(), first, last)


def edges_kernel(nu_ref, pair_ref, next_ref, beside_ref, column_ref):
    low_span = lax.axis_index("span") == 0
    rows = nu_ref.shape[0]
    put_edges(nu_ref[0], nu_ref[rows - 1], pair_ref, next_ref)
    lane = tile_iota(1)
    column = jnp.zeros((8, 128), F32)
    for row in range(rows):
        value = nu_ref[row]
        beside_ref[row : row + 1, :] = edge_row(value, low_span)
        column = jnp.where(lane == row, first_column(value), column)
    column_ref[...] = column


class Halo:
    def __init__(self, nu_ref, pair, after, beside_ref, column, padded_ref, ghost_ref):
        devices = lax.axis_size("wrap")
        place = lax.axis_index("wrap")
        rows = nu_ref.shape[0]
        self.rows = rows
        self.low_span = lax.axis_index("span") == 0
        self.padded, self.ghost, self.beside = padded_ref, ghost_ref, beside_ref
        lower = jnp.where(even_place(), after, pair)
        upper = jnp.where(even_place(), pair, after)
        padded_ref[0] = jnp.where(place == 0, nu_ref[0], lower)
        padded_ref[rows + 1] = jnp.where(place == devices - 1, nu_ref[rows - 1], upper)
        in_wake = (place < devices // 4) | (place >= devices - devices // 4)
        for row in range(rows):
            value = nu_ref[row]
            padded_ref[row + 1] = value
            partner = jnp.broadcast_to(column[:, rows - 1 - row : rows - row], (8, 128))
            ghost_ref[row] = jnp.where(in_wake, partner, -value)

    def rate(self, row, squares, vorticity):
        value = self.padded[row + 1]
        sub, lane = tile_iota(0), tile_iota(1)
        across = jnp.broadcast_to(self.beside[pl.ds(row, 1), :], (8, 128))
        span_low = jnp.where(self.low_span, value, across)
        span_high = jnp.where(self.low_span, across, value)
        others = (
            self.padded[row],
            self.padded[row + 2],
            jnp.where(sub == 0, span_low, pltpu.roll(value, 1, 0)),
            jnp.where(sub == 7, span_high, pltpu.roll(value, 7, 0)),
            jnp.where(lane == 0, self.ghost[row], pltpu.roll(value, 1, 1)),
            jnp.where(lane == 127, value, pltpu.roll(value, 127, 1)),
        )
        sums = jnp.zeros_like(value)
        squared = jnp.zeros_like(value)
        for other in others:
            change = other - value
            sums = sums + change
            squared = squared + change * change
        flux = (viscous + value) * sums + (0.5 * (1.0 + coef_cb2)) * squared
        scaled = coef_kappa**2 * squares
        modified = vorticity + value / scaled
        ratio = value / (modified * scaled)
        ratio2 = ratio * ratio
        shaped = ratio + coef_cw2 * (ratio2 * ratio2 * ratio2 - ratio)
        shaped2 = shaped * shaped
        base = (1.0 + coef_cw3**6) / (shaped2 * shaped2 * shaped2 + coef_cw3**6)
        factor = shaped * jnp.exp(jnp.log(base) * (1.0 / 6.0))
        return (
            flux / coef_sigma
            + coef_cb1 * modified * value
            - coef_cw1 * factor * value * value / squares
        )


def build_table(halves, table_ref):
    place = lax.axis_index("wrap")
    order = [bit for bits in STAGES for bit in bits]
    own_blocks = table_ref.shape[0] // lax.axis_size("wrap")
    slots = halves[0].shape[0] // (4 * own_blocks)
    top = len(order) - 1

    def body(slot, carry):
        for half, ref in enumerate(halves):
            mask = half << order[top]
            for n in range(top):
                mask = mask | (((slot >> n) & 1) << order[n])
            base = (place ^ mask) * own_blocks
            for pair in range(own_blocks // 2):
                start = pl.multiple_of(slot * own_blocks * 4 + pair * 8, 8)
                rows = ref[pl.ds(start, 8), :]
                table_ref[base + pair * 2] = panel_features(rows)
                table_ref[base + pair * 2 + 1] = panel_features(pltpu.roll(rows, 4, 0))
        return carry

    lax.fori_loop(0, slots, body, 0)


def nearest_tile(tile, list_ref, cell_ref, table_ref):
    sub = tile_iota(0)
    unit = jnp.where(sub == 3, 1.0, 0.0)
    xyz = [cell_ref[component, tile] for component in range(3)]
    twice = [-2.0 * part for part in xyz]
    found = []
    for line in range(8):
        rows = unit
        for component in range(3):
            spread = jnp.broadcast_to(twice[component][line : line + 1], (8, 128))
            rows = jnp.where(sub == component, spread, rows)
        cells = cell_features(rows).T
        nearest = None
        for slot in range(0, 8, 2):
            first = list_ref[(tile * 8 + line) * 8 + slot]
            second = list_ref[(tile * 8 + line) * 8 + slot + 1]
            panels = jnp.concatenate([table_ref[first], table_ref[second]], 1)
            value = jnp.dot(cells, panels, preferred_element_type=F32)
            value = jnp.minimum(value[:, :128], value[:, 128:])
            nearest = value if nearest is None else jnp.minimum(nearest, value)
        turned = jnp.min(nearest.T.reshape(16, 8, 128), axis=0)
        found.append(jnp.min(turned, axis=0, keepdims=True))
    norm = xyz[0] * xyz[0] + xyz[1] * xyz[1] + xyz[2] * xyz[2]
    return jnp.concatenate(found, 0) + norm


def main_kernel(
    list_ref,
    own_ref,
    other_ref,
    cell_ref,
    nu_ref,
    vorticity_ref,
    next_ref,
    beside_ref,
    dist_ref,
    squares_ref,
    middle_ref,
    pair_out,
    next_out,
    beside_out,
    column_out,
    table_ref,
    padded_ref,
    ghost_ref,
):
    panel_rows = own_ref.shape[0]
    column = other_ref[panel_rows : panel_rows + 8]
    pair = other_ref[panel_rows + 8 : panel_rows + 16]
    halo = Halo(nu_ref, pair, next_ref[...], beside_ref, column, padded_ref, ghost_ref)
    build_table((own_ref, other_ref), table_ref)
    tiles = nu_ref.shape[0]
    per_step = LINES_PER_STEP // 8

    def body(step, column):
        lane = tile_iota(1)
        for part in range(per_step):
            tile = step * per_step + part
            squares = nearest_tile(tile, list_ref, cell_ref, table_ref)
            squares_ref[tile] = squares
            dist_ref[tile] = jnp.sqrt(squares)
            rate = halo.rate(tile, squares, vorticity_ref[tile])
            middle = nu_ref[tile] + 0.5 * time_step * rate
            middle_ref[tile] = middle
            beside_out[pl.ds(tile, 1), :] = edge_row(middle, halo.low_span)
            column = jnp.where(lane == tile, first_column(middle), column)
        return column

    column_out[...] = lax.fori_loop(0, tiles // per_step, body, jnp.zeros((8, 128), F32))
    put_edges(middle_ref[0], middle_ref[tiles - 1], pair_out, next_out)


def last_kernel(
    middle_ref,
    nu_ref,
    squares_ref,
    vorticity_ref,
    pair_ref,
    next_ref,
    beside_ref,
    column_ref,
    out_ref,
    padded_ref,
    ghost_ref,
):
    halo = Halo(
        middle_ref, pair_ref[...], next_ref[...], beside_ref, column_ref[...], padded_ref, ghost_ref
    )
    for row in range(nu_ref.shape[0]):
        rate = halo.rate(row, squares_ref[row], vorticity_ref[row])
        out_ref[row] = nu_ref[row] + time_step * rate


def swap_mask(block, mask):
    return lax.ppermute(block, "wrap", [(i, i ^ mask) for i in range(lax.axis_size("wrap"))])


def swap_next(block):
    devices = lax.axis_size("wrap")
    pairs = [(i, i + 1) for i in range(1, devices - 1, 2)]
    return lax.ppermute(block, "wrap", pairs + [(j, i) for i, j in pairs])


def swap_span(block):
    return lax.ppermute(block, "span", [(0, 1), (1, 0)])


def gather(shard, pair, after, beside, column):
    size = shard.shape[0]
    for stage, bits in enumerate(STAGES[:-1]):
        if stage == len(STAGES) - 2:
            shard, after, beside = lax.optimization_barrier((shard, after, beside))
            after, beside = swap_next(after), swap_span(beside)
        parts = [shard]
        for choice in range(1, 1 << len(bits)):
            mask = sum(((choice >> n) & 1) << bit for n, bit in enumerate(bits))
            if choice == (1 << len(bits)) - 1:
                both = swap_mask(jnp.concatenate([shard, column], 0), mask)
                parts.append(both[:size])
                column = both[size:]
            else:
                parts.append(swap_mask(shard, mask))
        shard = jnp.concatenate(parts, 0)
        size = shard.shape[0]
    shard, after, beside = lax.optimization_barrier((shard, after, beside))
    other = swap_mask(jnp.concatenate([shard, column, pair], 0), 1 << STAGES[-1][0])
    return shard, other, after, beside


def shards(cell_xyz, panel_xyz, panel_size, block_lists, nu_field, vorticity):
    devices = lax.axis_size("wrap")
    rows, span, cells = nu_field.shape
    own_blocks = panel_size.shape[0] // PBS
    tile = jax.ShapeDtypeStruct((span, cells), F32)
    field = jax.ShapeDtypeStruct(nu_field.shape, F32)
    side = jax.ShapeDtypeStruct((rows, cells), F32)
    edges = (tile, tile, side, tile)
    scratch = [pltpu.VMEM((rows + 2, span, cells), F32), pltpu.VMEM(nu_field.shape, F32)]

    message = pl.pallas_call(
        message_kernel,
        out_shape=jax.ShapeDtypeStruct((4 * own_blocks, PBS), F32),
        in_specs=[pl.BlockSpec(memory_space=pltpu.HBM)] * 2,
        out_specs=VMEM,
        scratch_shapes=[
            pltpu.VMEM(panel_xyz.shape, F32),
            pltpu.VMEM((1,) + panel_size.shape, F32),
            pltpu.SemaphoreType.DMA((2,)),
        ],
        compiler_params=pltpu.CompilerParams(vmem_limit_bytes=2**20),
        name="message",
    )(panel_xyz, panel_size[None])
    sent = pl.pallas_call(
        edges_kernel,
        out_shape=edges,
        in_specs=[VMEM],
        out_specs=(VMEM,) * 4,
        compiler_params=pltpu.CompilerParams(vmem_limit_bytes=4 * 2**20),
        name="edges",
    )(nu_field)
    own, other, after, beside = gather(message, *sent)

    dist, squares, middle, pair, next_pair, sides, column = pl.pallas_call(
        main_kernel,
        out_shape=(field, field, field) + edges,
        in_specs=[SMEM] + [VMEM] * 7,
        out_specs=(VMEM,) * 7,
        scratch_shapes=[pltpu.VMEM((devices * own_blocks, FEATS, PBS), BF)] + scratch,
        compiler_params=pltpu.CompilerParams(vmem_limit_bytes=24 * 2**20),
        cost_estimate=pl.CostEstimate(
            flops=2 * 128 * rows * span * cells * block_lists.shape[2] * PBS,
            bytes_accessed=4 * 2**20,
            transcendentals=0,
        ),
        name="main",
    )(block_lists.reshape(-1), own, other, cell_xyz, nu_field, vorticity, after, beside)
    column = swap_mask(column, devices - 1)
    next_pair = swap_next(next_pair)
    sides = swap_span(sides)
    pair = swap_mask(pair, 1)

    nu_next = pl.pallas_call(
        last_kernel,
        out_shape=field,
        in_specs=[VMEM] * 8,
        out_specs=VMEM,
        scratch_shapes=scratch,
        compiler_params=pltpu.CompilerParams(vmem_limit_bytes=8 * 2**20),
        name="last",
    )(middle, nu_field, squares, vorticity, pair, next_pair, sides, column)
    return (nu_next, dist)


def solution(mesh):
    in_specs = (
        P(None, "wrap", "span", None),
        P(None, "wrap"),
        P("wrap"),
        P("wrap", "span", None),
        P("wrap", "span", None),
        P("wrap", "span", None),
    )
    out_specs = (P("wrap", "span", None), P("wrap", "span", None))
    return jax.shard_map(shards, mesh=mesh, in_specs=in_specs, out_specs=out_specs, check_vma=False)
```

```python
import functools

import jax
import jax.numpy as jnp
from jax import lax
from jax.experimental import pallas as pl
from jax.experimental.pallas import tpu as pltpu
from jax.sharding import PartitionSpec as P

BF = jnp.bfloat16
F32 = jnp.float32
PBS = 128
FEATS = 48
LINES_PER_STEP = 32
STAGES = ((6, 5), (4, 3), (2, 1), (0,))

coef_cb1 = 0.1355
coef_cb2 = 0.622
coef_sigma = 2.0 / 3.0
coef_kappa = 0.41
coef_cw2 = 0.3
coef_cw3 = 2.0
viscous = 1.0
time_step = 0.03
coef_cw1 = coef_cb1 / coef_kappa**2 + (1.0 + coef_cb2) / coef_sigma

SMEM = pl.BlockSpec(memory_space=pltpu.SMEM)
VMEM = pl.BlockSpec(memory_space=pltpu.VMEM)


def tile_iota(dim):
    return lax.broadcasted_iota(jnp.int32, (8, 128), dim)


def split_rows(rows):
    high = rows.astype(BF).astype(F32)
    rest = rows - high
    mid = rest.astype(BF).astype(F32)
    return high, mid, rest - mid


def panel_features(rows):
    high, mid, low = split_rows(rows)
    return jnp.concatenate([high, high, high, mid, mid, low], 0).astype(BF)


def cell_features(rows):
    high, mid, low = split_rows(rows)
    return jnp.concatenate([high, mid, low, high, mid, high], 0).astype(BF)


def edge_row(value, low_span):
    return jnp.where(low_span, value[7:8], value[0:1])


def first_column(value):
    return jnp.broadcast_to(value[:, 0:1], (8, 128))


def message_kernel(xyz_hbm, size_hbm, message_ref, xyz_ref, size_ref, sems):
    copies = [
        pltpu.make_async_copy(xyz_hbm, xyz_ref, sems.at[0]),
        pltpu.make_async_copy(size_hbm, size_ref, sems.at[1]),
    ]
    for copy in copies:
        copy.start()
    for copy in copies:
        copy.wait()
    for block in range(size_ref.shape[1] // PBS):
        lanes = slice(block * PBS, (block + 1) * PBS)
        xyz = xyz_ref[:, lanes]
        size = size_ref[:, lanes]
        offset = jnp.sum(xyz * xyz, axis=0, keepdims=True) + size * size
        message_ref[block * 4 : block * 4 + 3, :] = xyz
        message_ref[block * 4 + 3 : block * 4 + 4, :] = offset


def even_place():
    return lax.rem(lax.axis_index("wrap"), 2) == 0


def put_edges(first, last, pair_ref, next_ref):
    pair_ref[...] = jnp.where(even_place(), last, first)
    next_ref[...] = jnp.where(even_place(), first, last)


def edges_kernel(nu_ref, pair_ref, next_ref, beside_ref, column_ref):
    low_span = lax.axis_index("span") == 0
    rows = nu_ref.shape[0]
    put_edges(nu_ref[0], nu_ref[rows - 1], pair_ref, next_ref)
    lane = tile_iota(1)
    column = jnp.zeros((8, 128), F32)
    for row in range(rows):
        value = nu_ref[row]
        beside_ref[row : row + 1, :] = edge_row(value, low_span)
        column = jnp.where(lane == row, first_column(value), column)
    column_ref[...] = column


class Halo:
    def __init__(self, nu_ref, pair, after, beside_ref, column, padded_ref, ghost_ref):
        devices = lax.axis_size("wrap")
        place = lax.axis_index("wrap")
        rows = nu_ref.shape[0]
        self.rows = rows
        self.low_span = lax.axis_index("span") == 0
        self.padded, self.ghost, self.beside = padded_ref, ghost_ref, beside_ref
        lower = jnp.where(even_place(), after, pair)
        upper = jnp.where(even_place(), pair, after)
        padded_ref[0] = jnp.where(place == 0, nu_ref[0], lower)
        padded_ref[rows + 1] = jnp.where(place == devices - 1, nu_ref[rows - 1], upper)
        in_wake = (place < devices // 4) | (place >= devices - devices // 4)
        for row in range(rows):
            value = nu_ref[row]
            padded_ref[row + 1] = value
            partner = jnp.broadcast_to(column[:, rows - 1 - row : rows - row], (8, 128))
            ghost_ref[row] = jnp.where(in_wake, partner, -value)

    def rate(self, row, squares, vorticity):
        value = self.padded[row + 1]
        sub, lane = tile_iota(0), tile_iota(1)
        across = jnp.broadcast_to(self.beside[pl.ds(row, 1), :], (8, 128))
        span_low = jnp.where(self.low_span, value, across)
        span_high = jnp.where(self.low_span, across, value)
        others = (
            self.padded[row],
            self.padded[row + 2],
            jnp.where(sub == 0, span_low, pltpu.roll(value, 1, 0)),
            jnp.where(sub == 7, span_high, pltpu.roll(value, 7, 0)),
            jnp.where(lane == 0, self.ghost[row], pltpu.roll(value, 1, 1)),
            jnp.where(lane == 127, value, pltpu.roll(value, 127, 1)),
        )
        sums = jnp.zeros_like(value)
        squared = jnp.zeros_like(value)
        for other in others:
            change = other - value
            sums = sums + change
            squared = squared + change * change
        flux = (viscous + value) * sums + (0.5 * (1.0 + coef_cb2)) * squared
        scaled = coef_kappa**2 * squares
        modified = vorticity + value / scaled
        ratio = value / (modified * scaled)
        ratio2 = ratio * ratio
        shaped = ratio + coef_cw2 * (ratio2 * ratio2 * ratio2 - ratio)
        shaped2 = shaped * shaped
        base = (1.0 + coef_cw3**6) / (shaped2 * shaped2 * shaped2 + coef_cw3**6)
        factor = shaped * jnp.exp(jnp.log(base) * (1.0 / 6.0))
        return (
            flux / coef_sigma
            + coef_cb1 * modified * value
            - coef_cw1 * factor * value * value / squares
        )


def build_table(halves, table_ref):
    place = lax.axis_index("wrap")
    order = [bit for bits in STAGES for bit in bits]
    own_blocks = table_ref.shape[0] // lax.axis_size("wrap")
    slots = halves[0].shape[0] // (4 * own_blocks)
    top = len(order) - 1

    def body(slot, carry):
        for half, ref in enumerate(halves):
            mask = half << order[top]
            for n in range(top):
                mask = mask | (((slot >> n) & 1) << order[n])
            base = (place ^ mask) * own_blocks
            for pair in range(own_blocks // 2):
                start = pl.multiple_of(slot * own_blocks * 4 + pair * 8, 8)
                rows = ref[pl.ds(start, 8), :]
                table_ref[base + pair * 2] = panel_features(rows)
                table_ref[base + pair * 2 + 1] = panel_features(pltpu.roll(rows, 4, 0))
        return carry

    lax.fori_loop(0, slots, body, 0)


def nearest_tile(tile, list_ref, cell_ref, table_ref):
    sub = tile_iota(0)
    unit = jnp.where(sub == 3, 1.0, 0.0)
    xyz = [cell_ref[component, tile] for component in range(3)]
    twice = [-2.0 * part for part in xyz]
    found = []
    for line in range(8):
        rows = unit
        for component in range(3):
            spread = jnp.broadcast_to(twice[component][line : line + 1], (8, 128))
            rows = jnp.where(sub == component, spread, rows)
        cells = cell_features(rows).T
        nearest = None
        for slot in range(0, 8, 2):
            first = list_ref[(tile * 8 + line) * 8 + slot]
            second = list_ref[(tile * 8 + line) * 8 + slot + 1]
            panels = jnp.concatenate([table_ref[first], table_ref[second]], 1)
            value = jnp.dot(cells, panels, preferred_element_type=F32)
            value = jnp.minimum(value[:, :128], value[:, 128:])
            nearest = value if nearest is None else jnp.minimum(nearest, value)
        turned = jnp.min(nearest.T.reshape(16, 8, 128), axis=0)
        found.append(jnp.min(turned, axis=0, keepdims=True))
    norm = xyz[0] * xyz[0] + xyz[1] * xyz[1] + xyz[2] * xyz[2]
    return jnp.concatenate(found, 0) + norm


def main_kernel(
    list_ref,
    own_ref,
    other_ref,
    cell_ref,
    nu_ref,
    vorticity_ref,
    next_ref,
    beside_ref,
    dist_ref,
    squares_ref,
    middle_ref,
    pair_out,
    next_out,
    beside_out,
    column_out,
    table_ref,
    padded_ref,
    ghost_ref,
):
    panel_rows = own_ref.shape[0]
    column = other_ref[panel_rows : panel_rows + 8]
    pair = other_ref[panel_rows + 8 : panel_rows + 16]
    halo = Halo(nu_ref, pair, next_ref[...], beside_ref, column, padded_ref, ghost_ref)
    build_table((own_ref, other_ref), table_ref)
    tiles = nu_ref.shape[0]
    per_step = LINES_PER_STEP // 8

    def body(step, column):
        lane = tile_iota(1)
        for part in range(per_step):
            tile = step * per_step + part
            squares = nearest_tile(tile, list_ref, cell_ref, table_ref)
            squares_ref[tile] = squares
            dist_ref[tile] = jnp.sqrt(squares)
            rate = halo.rate(tile, squares, vorticity_ref[tile])
            middle = nu_ref[tile] + 0.5 * time_step * rate
            middle_ref[tile] = middle
            beside_out[pl.ds(tile, 1), :] = edge_row(middle, halo.low_span)
            column = jnp.where(lane == tile, first_column(middle), column)
        return column

    column_out[...] = lax.fori_loop(0, tiles // per_step, body, jnp.zeros((8, 128), F32))
    put_edges(middle_ref[0], middle_ref[tiles - 1], pair_out, next_out)


def last_kernel(
    middle_ref,
    nu_ref,
    squares_ref,
    vorticity_ref,
    pair_ref,
    next_ref,
    beside_ref,
    column_ref,
    out_ref,
    padded_ref,
    ghost_ref,
):
    halo = Halo(
        middle_ref, pair_ref[...], next_ref[...], beside_ref, column_ref[...], padded_ref, ghost_ref
    )
    for row in range(nu_ref.shape[0]):
        rate = halo.rate(row, squares_ref[row], vorticity_ref[row])
        out_ref[row] = nu_ref[row] + time_step * rate


def swap_mask(block, mask):
    return lax.ppermute(block, "wrap", [(i, i ^ mask) for i in range(lax.axis_size("wrap"))])


def swap_next(block):
    devices = lax.axis_size("wrap")
    pairs = [(i, (i + 1) % devices) for i in range(1, devices, 2)]
    return lax.ppermute(block, "wrap", pairs + [(j, i) for i, j in pairs])


def swap_span(block):
    return lax.ppermute(block, "span", [(0, 1), (1, 0)])


def gather(shard, pair, after, beside, column):
    size = shard.shape[0]
    for stage, bits in enumerate(STAGES[:-1]):
        if stage == len(STAGES) - 2:
            shard, after, beside = lax.optimization_barrier((shard, after, beside))
            after, beside = swap_next(after), swap_span(beside)
        parts = [shard]
        for choice in range(1, 1 << len(bits)):
            mask = sum(((choice >> n) & 1) << bit for n, bit in enumerate(bits))
            if choice == (1 << len(bits)) - 1:
                both = swap_mask(jnp.concatenate([shard, column], 0), mask)
                parts.append(both[:size])
                column = both[size:]
            else:
                parts.append(swap_mask(shard, mask))
        shard = jnp.concatenate(parts, 0)
        size = shard.shape[0]
    shard, after, beside = lax.optimization_barrier((shard, after, beside))
    other = swap_mask(jnp.concatenate([shard, column, pair], 0), 1 << STAGES[-1][0])
    return shard, other, after, beside


def shards(cell_xyz, panel_xyz, panel_size, block_lists, nu_field, vorticity):
    devices = lax.axis_size("wrap")
    rows, span, cells = nu_field.shape
    own_blocks = panel_size.shape[0] // PBS
    tile = jax.ShapeDtypeStruct((span, cells), F32)
    field = jax.ShapeDtypeStruct(nu_field.shape, F32)
    side = jax.ShapeDtypeStruct((rows, cells), F32)
    edges = (tile, tile, side, tile)
    scratch = [pltpu.VMEM((rows + 2, span, cells), F32), pltpu.VMEM(nu_field.shape, F32)]

    message = pl.pallas_call(
        message_kernel,
        out_shape=jax.ShapeDtypeStruct((4 * own_blocks, PBS), F32),
        in_specs=[pl.BlockSpec(memory_space=pltpu.HBM)] * 2,
        out_specs=VMEM,
        scratch_shapes=[
            pltpu.VMEM(panel_xyz.shape, F32),
            pltpu.VMEM((1,) + panel_size.shape, F32),
            pltpu.SemaphoreType.DMA((2,)),
        ],
        compiler_params=pltpu.CompilerParams(vmem_limit_bytes=2**20),
        name="message",
    )(panel_xyz, panel_size[None])
    sent = pl.pallas_call(
        edges_kernel,
        out_shape=edges,
        in_specs=[VMEM],
        out_specs=(VMEM,) * 4,
        compiler_params=pltpu.CompilerParams(vmem_limit_bytes=4 * 2**20),
        name="edges",
    )(nu_field)
    own, other, after, beside = gather(message, *sent)

    dist, squares, middle, pair, next_pair, sides, column = pl.pallas_call(
        main_kernel,
        out_shape=(field, field, field) + edges,
        in_specs=[SMEM] + [VMEM] * 7,
        out_specs=(VMEM,) * 7,
        scratch_shapes=[pltpu.VMEM((devices * own_blocks, FEATS, PBS), BF)] + scratch,
        compiler_params=pltpu.CompilerParams(vmem_limit_bytes=24 * 2**20),
        cost_estimate=pl.CostEstimate(
            flops=2 * 128 * rows * span * cells * block_lists.shape[2] * PBS,
            bytes_accessed=4 * 2**20,
            transcendentals=0,
        ),
        name="main",
    )(block_lists.reshape(-1), own, other, cell_xyz, nu_field, vorticity, after, beside)
    column = swap_mask(column, devices - 1)
    next_pair = swap_next(next_pair)
    sides = swap_span(sides)
    pair = swap_mask(pair, 1)

    nu_next = pl.pallas_call(
        last_kernel,
        out_shape=field,
        in_specs=[VMEM] * 8,
        out_specs=VMEM,
        scratch_shapes=scratch,
        compiler_params=pltpu.CompilerParams(vmem_limit_bytes=8 * 2**20),
        name="last",
    )(middle, nu_field, squares, vorticity, pair, next_pair, sides, column)
    return (nu_next, dist)


def solution(mesh):
    in_specs = (
        P(None, "wrap", "span", None),
        P(None, "wrap"),
        P("wrap"),
        P("wrap", "span", None),
        P("wrap", "span", None),
        P("wrap", "span", None),
    )
    out_specs = (P("wrap", "span", None), P("wrap", "span", None))
    return jax.shard_map(shards, mesh=mesh, in_specs=in_specs, out_specs=out_specs, check_vma=False)
```

```python
import functools

import jax
import jax.numpy as jnp
from jax import lax
from jax.experimental import pallas as pl
from jax.experimental.pallas import tpu as pltpu
from jax.sharding import PartitionSpec as P

BF = jnp.bfloat16
F32 = jnp.float32
PBS = 128
FEATS = 48
LINES_PER_STEP = 32
GROUP_BIT = 3
Y_MASKS = (2, 6, 4)

coef_cb1 = 0.1355
coef_cb2 = 0.622
coef_sigma = 2.0 / 3.0
coef_kappa = 0.41
coef_cw2 = 0.3
coef_cw3 = 2.0
viscous = 1.0
time_step = 0.03
coef_cw1 = coef_cb1 / coef_kappa**2 + (1.0 + coef_cb2) / coef_sigma

SMEM = pl.BlockSpec(memory_space=pltpu.SMEM)
VMEM = pl.BlockSpec(memory_space=pltpu.VMEM)


def tile_iota(dim):
    return lax.broadcasted_iota(jnp.int32, (8, 128), dim)


def split_rows(rows):
    high = rows.astype(BF).astype(F32)
    rest = rows - high
    mid = rest.astype(BF).astype(F32)
    return high, mid, rest - mid


def panel_features(rows):
    high, mid, low = split_rows(rows)
    return jnp.concatenate([high, high, high, mid, mid, low], 0).astype(BF)


def cell_features(rows):
    high, mid, low = split_rows(rows)
    return jnp.concatenate([high, mid, low, high, mid, high], 0).astype(BF)


def edge_row(value, low_span):
    return jnp.where(low_span, value[7:8], value[0:1])


def first_column(value):
    return jnp.broadcast_to(value[:, 0:1], (8, 128))


def even_place():
    return lax.rem(lax.axis_index("wrap"), 2) == 0


def put_edges(first, last, pair_ref, next_ref):
    pair_ref[...] = jnp.where(even_place(), last, first)
    next_ref[...] = jnp.where(even_place(), first, last)


def prep_kernel(
    xyz_hbm, size_hbm, nu_hbm, chunks_ref, pair_ref, beside_ref, xyz_ref, size_ref, nu_ref, sems
):
    pairs = ((xyz_hbm, xyz_ref), (size_hbm, size_ref), (nu_hbm, nu_ref))
    copies = [pltpu.make_async_copy(*pair, sems.at[n]) for n, pair in enumerate(pairs)]
    for copy in copies:
        copy.start()
    for copy in copies:
        copy.wait()
    parts = []
    for block in range(size_ref.shape[1] // PBS):
        lanes = slice(block * PBS, (block + 1) * PBS)
        xyz = xyz_ref[:, lanes]
        size = size_ref[:, lanes]
        parts += [xyz, jnp.sum(xyz * xyz, axis=0, keepdims=True) + size * size]
    low_span = lax.axis_index("span") == 0
    rows = nu_ref.shape[0]
    lane = tile_iota(1)
    column = jnp.zeros((8, 128), F32)
    for row in range(rows):
        value = nu_ref[row]
        beside_ref[row : row + 1, :] = edge_row(value, low_span)
        column = jnp.where(lane == row, first_column(value), column)
    first, last = nu_ref[0], nu_ref[rows - 1]
    pair_ref[...] = jnp.where(even_place(), last, first)
    parts += [column, jnp.where(even_place(), first, last)]
    chunk = jnp.concatenate(parts, 0)
    for n in range(chunks_ref.shape[0]):
        chunks_ref[n] = chunk


class Halo:
    def __init__(self, nu_ref, pair, after, beside_ref, column, padded_ref, ghost_ref):
        devices = lax.axis_size("wrap")
        place = lax.axis_index("wrap")
        rows = nu_ref.shape[0]
        self.rows = rows
        self.low_span = lax.axis_index("span") == 0
        self.padded, self.ghost, self.beside = padded_ref, ghost_ref, beside_ref
        lower = jnp.where(even_place(), after, pair)
        upper = jnp.where(even_place(), pair, after)
        padded_ref[0] = jnp.where(place == 0, nu_ref[0], lower)
        padded_ref[rows + 1] = jnp.where(place == devices - 1, nu_ref[rows - 1], upper)
        in_wake = (place < devices // 4) | (place >= devices - devices // 4)
        for row in range(rows):
            value = nu_ref[row]
            padded_ref[row + 1] = value
            partner = jnp.broadcast_to(column[:, rows - 1 - row : rows - row], (8, 128))
            ghost_ref[row] = jnp.where(in_wake, partner, -value)

    def rate(self, row, squares, vorticity):
        value = self.padded[row + 1]
        sub, lane = tile_iota(0), tile_iota(1)
        across = jnp.broadcast_to(self.beside[pl.ds(row, 1), :], (8, 128))
        span_low = jnp.where(self.low_span, value, across)
        span_high = jnp.where(self.low_span, across, value)
        others = (
            self.padded[row],
            self.padded[row + 2],
            jnp.where(sub == 0, span_low, pltpu.roll(value, 1, 0)),
            jnp.where(sub == 7, span_high, pltpu.roll(value, 7, 0)),
            jnp.where(lane == 0, self.ghost[row], pltpu.roll(value, 1, 1)),
            jnp.where(lane == 127, value, pltpu.roll(value, 127, 1)),
        )
        sums = jnp.zeros_like(value)
        squared = jnp.zeros_like(value)
        for other in others:
            change = other - value
            sums = sums + change
            squared = squared + change * change
        flux = (viscous + value) * sums + (0.5 * (1.0 + coef_cb2)) * squared
        scaled = coef_kappa**2 * squares
        modified = vorticity + value / scaled
        ratio = value / (modified * scaled)
        ratio2 = ratio * ratio
        shaped = ratio + coef_cw2 * (ratio2 * ratio2 * ratio2 - ratio)
        shaped2 = shaped * shaped
        base = (1.0 + coef_cw3**6) / (shaped2 * shaped2 * shaped2 + coef_cw3**6)
        factor = shaped * jnp.exp(jnp.log(base) * (1.0 / 6.0))
        return (
            flux / coef_sigma
            + coef_cb1 * modified * value
            - coef_cw1 * factor * value * value / squares
        )


def build_table(halves, table_ref):
    place = lax.axis_index("wrap")
    own_blocks = table_ref.shape[0] // lax.axis_size("wrap")
    groups = lax.axis_size("wrap") >> GROUP_BIT
    slots = groups * (len(Y_MASKS) + 1)

    def body(slot, carry):
        choice = slot // groups
        near = jnp.where(choice == 0, 0, Y_MASKS[0])
        for n in range(1, len(Y_MASKS)):
            near = jnp.where(choice == n + 1, Y_MASKS[n], near)
        low = (place & ((1 << GROUP_BIT) - 1)) ^ near
        skip = jnp.where(choice >= 2, 8, 0) + jnp.where(choice >= 3, 16, 0)
        for half, ref in enumerate(halves):
            base = (((slot % groups) << GROUP_BIT) | (low ^ half)) * own_blocks
            for pair in range(own_blocks // 2):
                start = pl.multiple_of(slot * own_blocks * 4 + skip + pair * 8, 8)
                rows = ref[pl.ds(start, 8), :]
                table_ref[base + pair * 2] = panel_features(rows)
                table_ref[base + pair * 2 + 1] = panel_features(pltpu.roll(rows, 4, 0))
        return carry

    lax.fori_loop(0, slots, body, 0)


def nearest_tile(tile, list_ref, cell_ref, table_ref):
    sub = tile_iota(0)
    unit = jnp.where(sub == 3, 1.0, 0.0)
    xyz = [cell_ref[component, tile] for component in range(3)]
    twice = [-2.0 * part for part in xyz]
    found = []
    for line in range(8):
        rows = unit
        for component in range(3):
            spread = jnp.broadcast_to(twice[component][line : line + 1], (8, 128))
            rows = jnp.where(sub == component, spread, rows)
        cells = cell_features(rows).T
        nearest = None
        for slot in range(0, 8, 2):
            first = list_ref[(tile * 8 + line) * 8 + slot]
            second = list_ref[(tile * 8 + line) * 8 + slot + 1]
            panels = jnp.concatenate([table_ref[first], table_ref[second]], 1)
            value = jnp.dot(cells, panels, preferred_element_type=F32)
            value = jnp.minimum(value[:, :128], value[:, 128:])
            nearest = value if nearest is None else jnp.minimum(nearest, value)
        turned = jnp.min(nearest.T.reshape(16, 8, 128), axis=0)
        found.append(jnp.min(turned, axis=0, keepdims=True))
    norm = xyz[0] * xyz[0] + xyz[1] * xyz[1] + xyz[2] * xyz[2]
    return jnp.concatenate(found, 0) + norm


def main_kernel(
    list_ref,
    own_ref,
    other_ref,
    cell_ref,
    nu_ref,
    vorticity_ref,
    beside_ref,
    dist_ref,
    squares_ref,
    middle_ref,
    pair_out,
    next_out,
    beside_out,
    column_out,
    table_ref,
    padded_ref,
    ghost_ref,
):
    place = lax.axis_index("wrap")
    total = (other_ref.shape[0] - 32) // 4
    in_first = (((place >> 1) + (place ^ 1)) & 1) == 0
    first_edge = other_ref[2 * total : 2 * total + 8]
    second_edge = other_ref[3 * total + 8 : 3 * total + 16]
    after = jnp.where(in_first, first_edge, second_edge)
    column = other_ref[3 * total + 16 : 3 * total + 24]
    pair = other_ref[4 * total + 24 : 4 * total + 32]
    halo = Halo(nu_ref, pair, after, beside_ref, column, padded_ref, ghost_ref)
    build_table((own_ref, other_ref), table_ref)
    tiles = nu_ref.shape[0]
    per_step = LINES_PER_STEP // 8

    def body(step, column):
        lane = tile_iota(1)
        for part in range(per_step):
            tile = step * per_step + part
            squares = nearest_tile(tile, list_ref, cell_ref, table_ref)
            squares_ref[tile] = squares
            dist_ref[tile] = jnp.sqrt(squares)
            rate = halo.rate(tile, squares, vorticity_ref[tile])
            middle = nu_ref[tile] + 0.5 * time_step * rate
            middle_ref[tile] = middle
            beside_out[pl.ds(tile, 1), :] = edge_row(middle, halo.low_span)
            column = jnp.where(lane == tile, first_column(middle), column)
        return column

    column_out[...] = lax.fori_loop(0, tiles // per_step, body, jnp.zeros((8, 128), F32))
    put_edges(middle_ref[0], middle_ref[tiles - 1], pair_out, next_out)


def last_kernel(
    middle_ref,
    nu_ref,
    squares_ref,
    vorticity_ref,
    pair_ref,
    next_ref,
    beside_ref,
    column_ref,
    out_ref,
    padded_ref,
    ghost_ref,
):
    halo = Halo(
        middle_ref, pair_ref[...], next_ref[...], beside_ref, column_ref[...], padded_ref, ghost_ref
    )
    for row in range(nu_ref.shape[0]):
        rate = halo.rate(row, squares_ref[row], vorticity_ref[row])
        out_ref[row] = nu_ref[row] + time_step * rate


def swap_mask(block, mask):
    return lax.ppermute(block, "wrap", [(i, i ^ mask) for i in range(lax.axis_size("wrap"))])


def swap_next(block):
    devices = lax.axis_size("wrap")
    pairs = [(i, (i + 1) % devices) for i in range(1, devices, 2)]
    return lax.ppermute(block, "wrap", pairs + [(j, i) for i, j in pairs])


def swap_span(block):
    return lax.ppermute(block, "span", [(0, 1), (1, 0)])


def gather(chunks, pair, beside):
    devices = lax.axis_size("wrap")
    place = lax.axis_index("wrap")
    groups, rows, lanes = chunks.shape
    size = rows - 16
    members = [[low + (n << GROUP_BIT) for n in range(groups)] for low in range(devices // groups)]
    chunks = lax.all_to_all(chunks, "wrap", 0, 0, tiled=True, axis_index_groups=members)
    chunks, beside = lax.optimization_barrier((chunks, beside))
    beside = swap_span(beside)
    shard = chunks[:, :size].reshape(groups * size, lanes)
    group, y, core = place >> GROUP_BIT, (place >> 1) & 3, place & 1
    column = lax.dynamic_slice(chunks, (groups - 1 - group, size, 0), (1, 8, lanes))[0]
    step = jnp.where(core == 1, jnp.where(y == 3, -1, 0), jnp.where(y == 0, 1, 0))
    source = (group + step) & (groups - 1)
    after = lax.dynamic_slice(chunks, (source, size + 8, 0), (1, 8, lanes))[0]
    first = swap_mask(jnp.concatenate([shard, after], 0), Y_MASKS[0])
    second = swap_mask(jnp.concatenate([shard, after, column], 0), Y_MASKS[1])
    third = swap_mask(shard, Y_MASKS[2])
    shard = jnp.concatenate([shard, first, second, third, pair], 0)
    shard, beside = lax.optimization_barrier((shard, beside))
    return shard, swap_mask(shard, 1), beside


def shards(cell_xyz, panel_xyz, panel_size, block_lists, nu_field, vorticity):
    devices = lax.axis_size("wrap")
    rows, span, cells = nu_field.shape
    own_blocks = panel_size.shape[0] // PBS
    tile = jax.ShapeDtypeStruct((span, cells), F32)
    field = jax.ShapeDtypeStruct(nu_field.shape, F32)
    side = jax.ShapeDtypeStruct((rows, cells), F32)
    edges = (tile, tile, side, tile)
    scratch = [pltpu.VMEM((rows + 2, span, cells), F32), pltpu.VMEM(nu_field.shape, F32)]

    groups = devices >> GROUP_BIT
    chunks, pair, beside = pl.pallas_call(
        prep_kernel,
        out_shape=(jax.ShapeDtypeStruct((groups, 4 * own_blocks + 16, PBS), F32), tile, side),
        in_specs=[pl.BlockSpec(memory_space=pltpu.HBM)] * 3,
        out_specs=(VMEM,) * 3,
        scratch_shapes=[
            pltpu.VMEM(panel_xyz.shape, F32),
            pltpu.VMEM((1,) + panel_size.shape, F32),
            pltpu.VMEM(nu_field.shape, F32),
            pltpu.SemaphoreType.DMA((3,)),
        ],
        compiler_params=pltpu.CompilerParams(vmem_limit_bytes=60 * 2**20),
        name="prep",
    )(panel_xyz, panel_size[None], nu_field)
    own, other, beside = gather(chunks, pair, beside)

    dist, squares, middle, pair, next_pair, sides, column = pl.pallas_call(
        main_kernel,
        out_shape=(field, field, field) + edges,
        in_specs=[SMEM] + [VMEM] * 6,
        out_specs=(VMEM,) * 7,
        scratch_shapes=[pltpu.VMEM((devices * own_blocks, FEATS, PBS), BF)] + scratch,
        compiler_params=pltpu.CompilerParams(vmem_limit_bytes=24 * 2**20),
        cost_estimate=pl.CostEstimate(
            flops=2 * 128 * rows * span * cells * block_lists.shape[2] * PBS,
            bytes_accessed=4 * 2**20,
            transcendentals=0,
        ),
        name="main",
    )(block_lists.reshape(-1), own, other, cell_xyz, nu_field, vorticity, beside)
    column = swap_mask(column, devices - 1)
    next_pair = swap_next(next_pair)
    sides = swap_span(sides)
    pair = swap_mask(pair, 1)

    nu_next = pl.pallas_call(
        last_kernel,
        out_shape=field,
        in_specs=[VMEM] * 8,
        out_specs=VMEM,
        scratch_shapes=scratch,
        compiler_params=pltpu.CompilerParams(vmem_limit_bytes=8 * 2**20),
        name="last",
    )(middle, nu_field, squares, vorticity, pair, next_pair, sides, column)
    return (nu_next, dist)


def solution(mesh):
    in_specs = (
        P(None, "wrap", "span", None),
        P(None, "wrap"),
        P("wrap"),
        P("wrap", "span", None),
        P("wrap", "span", None),
        P("wrap", "span", None),
    )
    out_specs = (P("wrap", "span", None), P("wrap", "span", None))
    return jax.shard_map(shards, mesh=mesh, in_specs=in_specs, out_specs=out_specs, check_vma=False)
```

```python
import functools

import jax
import jax.numpy as jnp
from jax import lax
from jax.experimental import pallas as pl
from jax.experimental.pallas import tpu as pltpu
from jax.sharding import PartitionSpec as P

BF = jnp.bfloat16
F32 = jnp.float32
PBS = 128
FEATS = 48
LINES_PER_STEP = 32
GROUP_BIT = 3
Y_MASKS = (2, 6, 4)

coef_cb1 = 0.1355
coef_cb2 = 0.622
coef_sigma = 2.0 / 3.0
coef_kappa = 0.41
coef_cw2 = 0.3
coef_cw3 = 2.0
viscous = 1.0
time_step = 0.03
coef_cw1 = coef_cb1 / coef_kappa**2 + (1.0 + coef_cb2) / coef_sigma

SMEM = pl.BlockSpec(memory_space=pltpu.SMEM)
VMEM = pl.BlockSpec(memory_space=pltpu.VMEM)


def tile_iota(dim):
    return lax.broadcasted_iota(jnp.int32, (8, 128), dim)


def split_rows(rows):
    high = rows.astype(BF).astype(F32)
    rest = rows - high
    mid = rest.astype(BF).astype(F32)
    return high, mid, rest - mid


def panel_features(rows):
    high, mid, low = split_rows(rows)
    return jnp.concatenate([high, high, high, mid, mid, low], 0).astype(BF)


def cell_features(rows):
    high, mid, low = split_rows(rows)
    return jnp.concatenate([high, mid, low, high, mid, high], 0).astype(BF)


def edge_row(value, low_span):
    return jnp.where(low_span, value[7:8], value[0:1])


def first_column(value):
    return jnp.broadcast_to(value[:, 0:1], (8, 128))


def even_place():
    return lax.rem(lax.axis_index("wrap"), 2) == 0


def put_edges(first, last, pair_ref, next_ref):
    pair_ref[...] = jnp.where(even_place(), last, first)
    next_ref[...] = jnp.where(even_place(), first, last)


def prep_kernel(
    xyz_hbm,
    size_hbm,
    nu_hbm,
    chunks_ref,
    pair_ref,
    next_ref,
    beside_ref,
    xyz_ref,
    size_ref,
    nu_ref,
    sems,
):
    pairs = ((xyz_hbm, xyz_ref), (size_hbm, size_ref), (nu_hbm, nu_ref))
    copies = [pltpu.make_async_copy(*pair, sems.at[n]) for n, pair in enumerate(pairs)]
    for copy in copies:
        copy.start()
    for copy in copies:
        copy.wait()
    parts = []
    for block in range(size_ref.shape[1] // PBS):
        lanes = slice(block * PBS, (block + 1) * PBS)
        xyz = xyz_ref[:, lanes]
        size = size_ref[:, lanes]
        parts += [xyz, jnp.sum(xyz * xyz, axis=0, keepdims=True) + size * size]
    low_span = lax.axis_index("span") == 0
    rows = nu_ref.shape[0]
    lane = tile_iota(1)
    column = jnp.zeros((8, 128), F32)
    for row in range(rows):
        value = nu_ref[row]
        beside_ref[row : row + 1, :] = edge_row(value, low_span)
        column = jnp.where(lane == row, first_column(value), column)
    put_edges(nu_ref[0], nu_ref[rows - 1], pair_ref, next_ref)
    chunk = jnp.concatenate(parts + [column], 0)
    for n in range(chunks_ref.shape[0]):
        chunks_ref[n] = chunk


class Halo:
    def __init__(self, nu_ref, pair, after, beside_ref, column, padded_ref, ghost_ref):
        devices = lax.axis_size("wrap")
        place = lax.axis_index("wrap")
        rows = nu_ref.shape[0]
        self.rows = rows
        self.low_span = lax.axis_index("span") == 0
        self.padded, self.ghost, self.beside = padded_ref, ghost_ref, beside_ref
        lower = jnp.where(even_place(), after, pair)
        upper = jnp.where(even_place(), pair, after)
        padded_ref[0] = jnp.where(place == 0, nu_ref[0], lower)
        padded_ref[rows + 1] = jnp.where(place == devices - 1, nu_ref[rows - 1], upper)
        in_wake = (place < devices // 4) | (place >= devices - devices // 4)
        for row in range(rows):
            value = nu_ref[row]
            padded_ref[row + 1] = value
            partner = jnp.broadcast_to(column[:, rows - 1 - row : rows - row], (8, 128))
            ghost_ref[row] = jnp.where(in_wake, partner, -value)

    def rate(self, row, squares, vorticity):
        value = self.padded[row + 1]
        sub, lane = tile_iota(0), tile_iota(1)
        across = jnp.broadcast_to(self.beside[pl.ds(row, 1), :], (8, 128))
        span_low = jnp.where(self.low_span, value, across)
        span_high = jnp.where(self.low_span, across, value)
        others = (
            self.padded[row],
            self.padded[row + 2],
            jnp.where(sub == 0, span_low, pltpu.roll(value, 1, 0)),
            jnp.where(sub == 7, span_high, pltpu.roll(value, 7, 0)),
            jnp.where(lane == 0, self.ghost[row], pltpu.roll(value, 1, 1)),
            jnp.where(lane == 127, value, pltpu.roll(value, 127, 1)),
        )
        sums = jnp.zeros_like(value)
        squared = jnp.zeros_like(value)
        for other in others:
            change = other - value
            sums = sums + change
            squared = squared + change * change
        flux = (viscous + value) * sums + (0.5 * (1.0 + coef_cb2)) * squared
        scaled = coef_kappa**2 * squares
        modified = vorticity + value / scaled
        ratio = value / (modified * scaled)
        ratio2 = ratio * ratio
        shaped = ratio + coef_cw2 * (ratio2 * ratio2 * ratio2 - ratio)
        shaped2 = shaped * shaped
        base = (1.0 + coef_cw3**6) / (shaped2 * shaped2 * shaped2 + coef_cw3**6)
        factor = shaped * jnp.exp(jnp.log(base) * (1.0 / 6.0))
        return (
            flux / coef_sigma
            + coef_cb1 * modified * value
            - coef_cw1 * factor * value * value / squares
        )


def build_table(halves, table_ref):
    place = lax.axis_index("wrap")
    own_blocks = table_ref.shape[0] // lax.axis_size("wrap")
    groups = lax.axis_size("wrap") >> GROUP_BIT
    slots = groups * (len(Y_MASKS) + 1)

    def body(slot, carry):
        choice = slot // groups
        near = jnp.where(choice == 0, 0, Y_MASKS[0])
        for n in range(1, len(Y_MASKS)):
            near = jnp.where(choice == n + 1, Y_MASKS[n], near)
        low = (place & ((1 << GROUP_BIT) - 1)) ^ near
        skip = jnp.where(choice == 3, 8, 0)
        for half, ref in enumerate(halves):
            base = (((slot % groups) << GROUP_BIT) | (low ^ half)) * own_blocks
            for pair in range(own_blocks // 2):
                start = pl.multiple_of(slot * own_blocks * 4 + skip + pair * 8, 8)
                rows = ref[pl.ds(start, 8), :]
                table_ref[base + pair * 2] = panel_features(rows)
                table_ref[base + pair * 2 + 1] = panel_features(pltpu.roll(rows, 4, 0))
        return carry

    lax.fori_loop(0, slots, body, 0)


def nearest_tile(tile, list_ref, cell_ref, table_ref):
    sub = tile_iota(0)
    unit = jnp.where(sub == 3, 1.0, 0.0)
    xyz = [cell_ref[component, tile] for component in range(3)]
    twice = [-2.0 * part for part in xyz]
    found = []
    for line in range(8):
        rows = unit
        for component in range(3):
            spread = jnp.broadcast_to(twice[component][line : line + 1], (8, 128))
            rows = jnp.where(sub == component, spread, rows)
        cells = cell_features(rows).T
        nearest = None
        for slot in range(0, 8, 2):
            first = list_ref[(tile * 8 + line) * 8 + slot]
            second = list_ref[(tile * 8 + line) * 8 + slot + 1]
            panels = jnp.concatenate([table_ref[first], table_ref[second]], 1)
            value = jnp.dot(cells, panels, preferred_element_type=F32)
            value = jnp.minimum(value[:, :128], value[:, 128:])
            nearest = value if nearest is None else jnp.minimum(nearest, value)
        turned = jnp.min(nearest.T.reshape(16, 8, 128), axis=0)
        found.append(jnp.min(turned, axis=0, keepdims=True))
    norm = xyz[0] * xyz[0] + xyz[1] * xyz[1] + xyz[2] * xyz[2]
    return jnp.concatenate(found, 0) + norm


def main_kernel(
    list_ref,
    own_ref,
    other_ref,
    cell_ref,
    nu_ref,
    vorticity_ref,
    next_ref,
    beside_ref,
    dist_ref,
    squares_ref,
    middle_ref,
    pair_out,
    next_out,
    beside_out,
    column_out,
    table_ref,
    padded_ref,
    ghost_ref,
):
    total = (other_ref.shape[0] - 16) // 4
    column = other_ref[3 * total : 3 * total + 8]
    pair = other_ref[4 * total + 8 : 4 * total + 16]
    halo = Halo(nu_ref, pair, next_ref[...], beside_ref, column, padded_ref, ghost_ref)
    build_table((own_ref, other_ref), table_ref)
    tiles = nu_ref.shape[0]
    per_step = LINES_PER_STEP // 8

    def body(step, column):
        lane = tile_iota(1)
        for part in range(per_step):
            tile = step * per_step + part
            squares = nearest_tile(tile, list_ref, cell_ref, table_ref)
            squares_ref[tile] = squares
            dist_ref[tile] = jnp.sqrt(squares)
            rate = halo.rate(tile, squares, vorticity_ref[tile])
            middle = nu_ref[tile] + 0.5 * time_step * rate
            middle_ref[tile] = middle
            beside_out[pl.ds(tile, 1), :] = edge_row(middle, halo.low_span)
            column = jnp.where(lane == tile, first_column(middle), column)
        return column

    column_out[...] = lax.fori_loop(0, tiles // per_step, body, jnp.zeros((8, 128), F32))
    put_edges(middle_ref[0], middle_ref[tiles - 1], pair_out, next_out)


def last_kernel(
    middle_ref,
    nu_ref,
    squares_ref,
    vorticity_ref,
    pair_ref,
    next_ref,
    beside_ref,
    column_ref,
    out_ref,
    padded_ref,
    ghost_ref,
):
    halo = Halo(
        middle_ref, pair_ref[...], next_ref[...], beside_ref, column_ref[...], padded_ref, ghost_ref
    )
    for row in range(nu_ref.shape[0]):
        rate = halo.rate(row, squares_ref[row], vorticity_ref[row])
        out_ref[row] = nu_ref[row] + time_step * rate


def swap_mask(block, mask):
    return lax.ppermute(block, "wrap", [(i, i ^ mask) for i in range(lax.axis_size("wrap"))])


def swap_next(block):
    devices = lax.axis_size("wrap")
    pairs = [(i, (i + 1) % devices) for i in range(1, devices, 2)]
    return lax.ppermute(block, "wrap", pairs + [(j, i) for i, j in pairs])


def swap_span(block):
    return lax.ppermute(block, "span", [(0, 1), (1, 0)])


def gather(chunks, pair, after, beside):
    devices = lax.axis_size("wrap")
    groups, rows, lanes = chunks.shape
    size = rows - 8
    members = [[low + (n << GROUP_BIT) for n in range(groups)] for low in range(devices // groups)]
    chunks = lax.all_to_all(chunks, "wrap", 0, 0, tiled=True, axis_index_groups=members)
    chunks, after, beside = lax.optimization_barrier((chunks, swap_next(after), swap_span(beside)))
    shard = chunks[:, :size].reshape(groups * size, lanes)
    opposite = groups - 1 - (lax.axis_index("wrap") >> GROUP_BIT)
    column = lax.dynamic_slice(chunks, (opposite, size, 0), (1, 8, lanes))[0]
    first = swap_mask(shard, Y_MASKS[0])
    second = swap_mask(jnp.concatenate([shard, column], 0), Y_MASKS[1])
    third = swap_mask(shard, Y_MASKS[2])
    shard = jnp.concatenate([shard, first, second, third, pair], 0)
    return shard, swap_mask(shard, 1), after, beside


def shards(cell_xyz, panel_xyz, panel_size, block_lists, nu_field, vorticity):
    devices = lax.axis_size("wrap")
    rows, span, cells = nu_field.shape
    own_blocks = panel_size.shape[0] // PBS
    tile = jax.ShapeDtypeStruct((span, cells), F32)
    field = jax.ShapeDtypeStruct(nu_field.shape, F32)
    side = jax.ShapeDtypeStruct((rows, cells), F32)
    edges = (tile, tile, side, tile)
    scratch = [pltpu.VMEM((rows + 2, span, cells), F32), pltpu.VMEM(nu_field.shape, F32)]

    groups = devices >> GROUP_BIT
    chunks, pair, after, beside = pl.pallas_call(
        prep_kernel,
        out_shape=(jax.ShapeDtypeStruct((groups, 4 * own_blocks + 8, PBS), F32), tile, tile, side),
        in_specs=[pl.BlockSpec(memory_space=pltpu.HBM)] * 3,
        out_specs=(VMEM,) * 4,
        scratch_shapes=[
            pltpu.VMEM(panel_xyz.shape, F32),
            pltpu.VMEM((1,) + panel_size.shape, F32),
            pltpu.VMEM(nu_field.shape, F32),
            pltpu.SemaphoreType.DMA((3,)),
        ],
        compiler_params=pltpu.CompilerParams(vmem_limit_bytes=60 * 2**20),
        name="prep",
    )(panel_xyz, panel_size[None], nu_field)
    own, other, after, beside = gather(chunks, pair, after, beside)

    dist, squares, middle, pair, next_pair, sides, column = pl.pallas_call(
        main_kernel,
        out_shape=(field, field, field) + edges,
        in_specs=[SMEM] + [VMEM] * 7,
        out_specs=(VMEM,) * 7,
        scratch_shapes=[pltpu.VMEM((devices * own_blocks, FEATS, PBS), BF)] + scratch,
        compiler_params=pltpu.CompilerParams(vmem_limit_bytes=24 * 2**20),
        cost_estimate=pl.CostEstimate(
            flops=2 * 128 * rows * span * cells * block_lists.shape[2] * PBS,
            bytes_accessed=4 * 2**20,
            transcendentals=0,
        ),
        name="main",
    )(block_lists.reshape(-1), own, other, cell_xyz, nu_field, vorticity, after, beside)
    column = swap_mask(column, devices - 1)
    next_pair = swap_next(next_pair)
    sides = swap_span(sides)
    pair = swap_mask(pair, 1)

    nu_next = pl.pallas_call(
        last_kernel,
        out_shape=field,
        in_specs=[VMEM] * 8,
        out_specs=VMEM,
        scratch_shapes=scratch,
        compiler_params=pltpu.CompilerParams(vmem_limit_bytes=8 * 2**20),
        name="last",
    )(middle, nu_field, squares, vorticity, pair, next_pair, sides, column)
    return (nu_next, dist)


def solution(mesh):
    in_specs = (
        P(None, "wrap", "span", None),
        P(None, "wrap"),
        P("wrap"),
        P("wrap", "span", None),
        P("wrap", "span", None),
        P("wrap", "span", None),
    )
    out_specs = (P("wrap", "span", None), P("wrap", "span", None))
    return jax.shard_map(shards, mesh=mesh, in_specs=in_specs, out_specs=out_specs, check_vma=False)
```

```python
import functools

import jax
import jax.numpy as jnp
from jax import lax
from jax.experimental import pallas as pl
from jax.experimental.pallas import tpu as pltpu
from jax.sharding import PartitionSpec as P

BF = jnp.bfloat16
F32 = jnp.float32
PBS = 128
FEATS = 48
LINES_PER_STEP = 64
COLUMN_ROWS = 40
GROUP_BIT = 3
Y_MASKS = (2, 6, 4)

coef_cb1 = 0.1355
coef_cb2 = 0.622
coef_sigma = 2.0 / 3.0
coef_kappa = 0.41
coef_cw2 = 0.3
coef_cw3 = 2.0
viscous = 1.0
time_step = 0.03
coef_cw1 = coef_cb1 / coef_kappa**2 + (1.0 + coef_cb2) / coef_sigma

SMEM = pl.BlockSpec(memory_space=pltpu.SMEM)
VMEM = pl.BlockSpec(memory_space=pltpu.VMEM)


def tile_iota(dim):
    return lax.broadcasted_iota(jnp.int32, (8, 128), dim)


def split_rows(rows):
    high = rows.astype(BF).astype(F32)
    rest = rows - high
    mid = rest.astype(BF).astype(F32)
    return high, mid, rest - mid


def panel_features(rows):
    high, mid, low = split_rows(rows)
    return jnp.concatenate([high, high, high, mid, mid, low], 0).astype(BF)


def cell_features(rows):
    high, mid, low = split_rows(rows)
    return jnp.concatenate([high, mid, low, high, mid, high], 0).astype(BF)


def edge_row(value, low_span):
    return jnp.where(low_span, value[7:8], value[0:1])


def first_column(value):
    return jnp.broadcast_to(value[:, 0:1], (8, 128))


def even_place():
    return lax.rem(lax.axis_index("wrap"), 2) == 0


def put_edges(first, last, pair_ref, next_ref):
    pair_ref[...] = jnp.where(even_place(), last, first)
    next_ref[...] = jnp.where(even_place(), first, last)


def prep_kernel(
    xyz_hbm,
    size_hbm,
    nu_hbm,
    chunks_ref,
    pair_ref,
    next_ref,
    beside_ref,
    xyz_ref,
    size_ref,
    nu_ref,
    sems,
):
    pairs = ((xyz_hbm, xyz_ref), (size_hbm, size_ref), (nu_hbm, nu_ref))
    copies = [pltpu.make_async_copy(*pair, sems.at[n]) for n, pair in enumerate(pairs)]
    for copy in copies:
        copy.start()
    for copy in copies:
        copy.wait()
    parts = []
    for block in range(size_ref.shape[1] // PBS):
        lanes = slice(block * PBS, (block + 1) * PBS)
        xyz = xyz_ref[:, lanes]
        size = size_ref[:, lanes]
        parts += [xyz, jnp.sum(xyz * xyz, axis=0, keepdims=True) + size * size]
    low_span = lax.axis_index("span") == 0
    rows = nu_ref.shape[0]
    lane = tile_iota(1)
    column = jnp.zeros((8, 128), F32)
    for row in range(rows):
        value = nu_ref[row]
        beside_ref[row : row + 1, :] = edge_row(value, low_span)
        column = jnp.where(lane == row, first_column(value), column)
    put_edges(nu_ref[0], nu_ref[rows - 1], pair_ref, next_ref)
    chunk = jnp.concatenate(parts + [column], 0)
    for n in range(chunks_ref.shape[0]):
        chunks_ref[n] = chunk


class Halo:
    def __init__(self, nu_ref, pair, after, beside_ref, column, padded_ref, ghost_ref):
        devices = lax.axis_size("wrap")
        place = lax.axis_index("wrap")
        rows = nu_ref.shape[0]
        self.rows = rows
        self.low_span = lax.axis_index("span") == 0
        self.padded, self.ghost, self.beside = padded_ref, ghost_ref, beside_ref
        lower = jnp.where(even_place(), after, pair)
        upper = jnp.where(even_place(), pair, after)
        padded_ref[0] = jnp.where(place == 0, nu_ref[0], lower)
        padded_ref[rows + 1] = jnp.where(place == devices - 1, nu_ref[rows - 1], upper)
        in_wake = (place < devices // 4) | (place >= devices - devices // 4)
        for row in range(rows):
            value = nu_ref[row]
            padded_ref[row + 1] = value
            partner = jnp.broadcast_to(column[:, rows - 1 - row : rows - row], (8, 128))
            ghost_ref[row] = jnp.where(in_wake, partner, -value)

    def rate(self, row, squares, vorticity):
        value = self.padded[row + 1]
        sub, lane = tile_iota(0), tile_iota(1)
        across = jnp.broadcast_to(self.beside[pl.ds(row, 1), :], (8, 128))
        span_low = jnp.where(self.low_span, value, across)
        span_high = jnp.where(self.low_span, across, value)
        others = (
            self.padded[row],
            self.padded[row + 2],
            jnp.where(sub == 0, span_low, pltpu.roll(value, 1, 0)),
            jnp.where(sub == 7, span_high, pltpu.roll(value, 7, 0)),
            jnp.where(lane == 0, self.ghost[row], pltpu.roll(value, 1, 1)),
            jnp.where(lane == 127, value, pltpu.roll(value, 127, 1)),
        )
        sums = jnp.zeros_like(value)
        squared = jnp.zeros_like(value)
        for other in others:
            change = other - value
            sums = sums + change
            squared = squared + change * change
        flux = (viscous + value) * sums + (0.5 * (1.0 + coef_cb2)) * squared
        scaled = coef_kappa**2 * squares
        modified = vorticity + value / scaled
        ratio = value / (modified * scaled)
        ratio2 = ratio * ratio
        shaped = ratio + coef_cw2 * (ratio2 * ratio2 * ratio2 - ratio)
        shaped2 = shaped * shaped
        base = (1.0 + coef_cw3**6) / (shaped2 * shaped2 * shaped2 + coef_cw3**6)
        factor = shaped * jnp.exp(jnp.log(base) * (1.0 / 6.0))
        return (
            flux / coef_sigma
            + coef_cb1 * modified * value
            - coef_cw1 * factor * value * value / squares
        )


def build_table(halves, table_ref):
    place = lax.axis_index("wrap")
    own_blocks = table_ref.shape[0] // lax.axis_size("wrap")
    groups = lax.axis_size("wrap") >> GROUP_BIT
    slots = groups * (len(Y_MASKS) + 1)

    def body(slot, carry):
        choice = slot // groups
        near = jnp.where(choice == 0, 0, Y_MASKS[0])
        for n in range(1, len(Y_MASKS)):
            near = jnp.where(choice == n + 1, Y_MASKS[n], near)
        low = (place & ((1 << GROUP_BIT) - 1)) ^ near
        skip = jnp.where(choice == 3, 16, 8)
        for half, ref in enumerate(halves):
            base = (((slot % groups) << GROUP_BIT) | (low ^ half)) * own_blocks
            for pair in range(own_blocks // 2):
                start = pl.multiple_of(slot * own_blocks * 4 + skip + pair * 8, 8)
                rows = ref[pl.ds(start, 8), :]
                table_ref[base + pair * 2] = panel_features(rows)
                table_ref[base + pair * 2 + 1] = panel_features(pltpu.roll(rows, 4, 0))
        return carry

    lax.fori_loop(0, slots, body, 0)


def nearest_tile(tile, list_ref, cell_ref, table_ref):
    sub = tile_iota(0)
    unit = jnp.where(sub == 3, 1.0, 0.0)
    xyz = [cell_ref[component, tile] for component in range(3)]
    twice = [-2.0 * part for part in xyz]
    found = []
    for line in range(8):
        rows = unit
        for component in range(3):
            spread = jnp.broadcast_to(twice[component][line : line + 1], (8, 128))
            rows = jnp.where(sub == component, spread, rows)
        cells = cell_features(rows).T
        nearest = None
        for slot in range(0, 8, 2):
            first = list_ref[(tile * 8 + line) * 8 + slot]
            second = list_ref[(tile * 8 + line) * 8 + slot + 1]
            panels = jnp.concatenate([table_ref[first], table_ref[second]], 1)
            value = jnp.dot(cells, panels, preferred_element_type=F32)
            value = jnp.minimum(value[:, :128], value[:, 128:])
            nearest = value if nearest is None else jnp.minimum(nearest, value)
        turned = jnp.min(nearest.T.reshape(16, 8, 128), axis=0)
        found.append(jnp.min(turned, axis=0, keepdims=True))
    norm = xyz[0] * xyz[0] + xyz[1] * xyz[1] + xyz[2] * xyz[2]
    return jnp.concatenate(found, 0) + norm


def main_kernel(
    list_ref,
    own_ref,
    other_ref,
    cell_ref,
    nu_ref,
    vorticity_ref,
    next_ref,
    beside_ref,
    dist_ref,
    squares_ref,
    middle_ref,
    pair_out,
    next_out,
    beside_out,
    column_out,
    table_ref,
    padded_ref,
    ghost_ref,
):
    total = (other_ref.shape[0] - 16) // 4
    column = other_ref[3 * total + 8 : 3 * total + 16]
    pair = other_ref[0:8]
    halo = Halo(nu_ref, pair, next_ref[...], beside_ref, column, padded_ref, ghost_ref)
    build_table((own_ref, other_ref), table_ref)
    tiles = nu_ref.shape[0]
    per_step = LINES_PER_STEP // 8

    def body(step, column):
        lane = tile_iota(1)
        for part in range(per_step):
            tile = step * per_step + part
            squares = nearest_tile(tile, list_ref, cell_ref, table_ref)
            squares_ref[tile] = squares
            dist_ref[tile] = jnp.sqrt(squares)
            rate = halo.rate(tile, squares, vorticity_ref[tile])
            middle = nu_ref[tile] + 0.5 * time_step * rate
            middle_ref[tile] = middle
            beside_out[pl.ds(tile, 1), :] = edge_row(middle, halo.low_span)
            column = jnp.where(lane == tile, first_column(middle), column)
        return column

    column = lax.fori_loop(0, tiles // per_step, body, jnp.zeros((8, 128), F32))
    for row in range(0, column_out.shape[0], 8):
        column_out[row : row + 8] = column
    put_edges(middle_ref[0], middle_ref[tiles - 1], pair_out, next_out)


def last_kernel(
    middle_ref,
    nu_ref,
    squares_ref,
    vorticity_ref,
    pair_ref,
    next_ref,
    beside_ref,
    column_ref,
    out_ref,
    padded_ref,
    ghost_ref,
):
    halo = Halo(
        middle_ref, pair_ref[...], next_ref[...], beside_ref, column_ref[0:8], padded_ref, ghost_ref
    )
    for row in range(nu_ref.shape[0]):
        rate = halo.rate(row, squares_ref[row], vorticity_ref[row])
        out_ref[row] = nu_ref[row] + time_step * rate


def swap_mask(block, mask):
    return lax.ppermute(block, "wrap", [(i, i ^ mask) for i in range(lax.axis_size("wrap"))])


def swap_next(block):
    devices = lax.axis_size("wrap")
    pairs = [(i, (i + 1) % devices) for i in range(1, devices, 2)]
    return lax.ppermute(block, "wrap", pairs + [(j, i) for i, j in pairs])


def swap_span(block):
    return lax.ppermute(block, "span", [(0, 1), (1, 0)])


def gather(chunks, pair, after, beside):
    devices = lax.axis_size("wrap")
    groups, rows, lanes = chunks.shape
    size = rows - 8
    members = [[low + (n << GROUP_BIT) for n in range(groups)] for low in range(devices // groups)]
    chunks = lax.all_to_all(chunks, "wrap", 0, 0, tiled=True, axis_index_groups=members)
    chunks, after, beside = lax.optimization_barrier((chunks, swap_next(after), swap_span(beside)))
    shard = chunks[:, :size].reshape(groups * size, lanes)
    opposite = groups - 1 - (lax.axis_index("wrap") >> GROUP_BIT)
    column = lax.dynamic_slice(chunks, (opposite, size, 0), (1, 8, lanes))[0]
    first = swap_mask(shard, Y_MASKS[0])
    second = swap_mask(jnp.concatenate([shard, column], 0), Y_MASKS[1])
    third = swap_mask(shard, Y_MASKS[2])
    shard = jnp.concatenate([pair, shard, first, second, third], 0)
    return shard, swap_mask(shard, 1), after, beside


def shards(cell_xyz, panel_xyz, panel_size, block_lists, nu_field, vorticity):
    devices = lax.axis_size("wrap")
    rows, span, cells = nu_field.shape
    own_blocks = panel_size.shape[0] // PBS
    tile = jax.ShapeDtypeStruct((span, cells), F32)
    field = jax.ShapeDtypeStruct(nu_field.shape, F32)
    side = jax.ShapeDtypeStruct((rows, cells), F32)
    edges = (tile, tile, side, jax.ShapeDtypeStruct((COLUMN_ROWS, cells), F32))
    scratch = [pltpu.VMEM((rows + 2, span, cells), F32), pltpu.VMEM(nu_field.shape, F32)]

    groups = devices >> GROUP_BIT
    chunks, pair, after, beside = pl.pallas_call(
        prep_kernel,
        out_shape=(jax.ShapeDtypeStruct((groups, 4 * own_blocks + 8, PBS), F32), tile, tile, side),
        in_specs=[pl.BlockSpec(memory_space=pltpu.HBM)] * 3,
        out_specs=(VMEM,) * 4,
        scratch_shapes=[
            pltpu.VMEM(panel_xyz.shape, F32),
            pltpu.VMEM((1,) + panel_size.shape, F32),
            pltpu.VMEM(nu_field.shape, F32),
            pltpu.SemaphoreType.DMA((3,)),
        ],
        compiler_params=pltpu.CompilerParams(vmem_limit_bytes=60 * 2**20),
        name="prep",
    )(panel_xyz, panel_size[None], nu_field)
    own, other, after, beside = gather(chunks, pair, after, beside)

    dist, squares, middle, pair, next_pair, sides, column = pl.pallas_call(
        main_kernel,
        out_shape=(field, field, field) + edges,
        in_specs=[SMEM] + [VMEM] * 7,
        out_specs=(VMEM,) * 7,
        scratch_shapes=[pltpu.VMEM((devices * own_blocks, FEATS, PBS), BF)] + scratch,
        compiler_params=pltpu.CompilerParams(vmem_limit_bytes=24 * 2**20),
        cost_estimate=pl.CostEstimate(
            flops=2 * 128 * rows * span * cells * block_lists.shape[2] * PBS,
            bytes_accessed=4 * 2**20,
            transcendentals=0,
        ),
        name="main",
    )(block_lists.reshape(-1), own, other, cell_xyz, nu_field, vorticity, after, beside)
    column = swap_mask(column, devices - 1)
    next_pair = swap_next(next_pair)
    sides = swap_span(sides)
    pair = swap_mask(pair, 1)

    nu_next = pl.pallas_call(
        last_kernel,
        out_shape=field,
        in_specs=[VMEM] * 8,
        out_specs=VMEM,
        scratch_shapes=scratch,
        compiler_params=pltpu.CompilerParams(vmem_limit_bytes=8 * 2**20),
        name="last",
    )(middle, nu_field, squares, vorticity, pair, next_pair, sides, column)
    return (nu_next, dist)


def solution(mesh):
    in_specs = (
        P(None, "wrap", "span", None),
        P(None, "wrap"),
        P("wrap"),
        P("wrap", "span", None),
        P("wrap", "span", None),
        P("wrap", "span", None),
    )
    out_specs = (P("wrap", "span", None), P("wrap", "span", None))
    return jax.shard_map(shards, mesh=mesh, in_specs=in_specs, out_specs=out_specs, check_vma=False)
```

```python
import functools

import jax
import jax.numpy as jnp
from jax import lax
from jax.experimental import pallas as pl
from jax.experimental.pallas import tpu as pltpu
from jax.sharding import PartitionSpec as P

BF = jnp.bfloat16
F32 = jnp.float32
PBS = 128
FEATS = 48
LINES_PER_STEP = 64
COLUMN_ROWS = 40
GROUP_BIT = 3
Y_MASKS = (2, 6, 4)

coef_cb1 = 0.1355
coef_cb2 = 0.622
coef_sigma = 2.0 / 3.0
coef_kappa = 0.41
coef_cw2 = 0.3
coef_cw3 = 2.0
viscous = 1.0
time_step = 0.03
coef_cw1 = coef_cb1 / coef_kappa**2 + (1.0 + coef_cb2) / coef_sigma

SMEM = pl.BlockSpec(memory_space=pltpu.SMEM)
VMEM = pl.BlockSpec(memory_space=pltpu.VMEM)


def tile_iota(dim):
    return lax.broadcasted_iota(jnp.int32, (8, 128), dim)


def split_rows(rows):
    high = rows.astype(BF).astype(F32)
    rest = rows - high
    mid = rest.astype(BF).astype(F32)
    return high, mid, rest - mid


def panel_features(rows):
    high, mid, low = split_rows(rows)
    return jnp.concatenate([high, high, high, mid, mid, low], 0).astype(BF)


def cell_features(rows):
    high, mid, low = split_rows(rows)
    return jnp.concatenate([high, mid, low, high, mid, high], 0).astype(BF)


def edge_row(value, low_span):
    return jnp.where(low_span, value[7:8], value[0:1])


def first_column(value):
    return jnp.broadcast_to(value[:, 0:1], (8, 128))


def even_place():
    return lax.rem(lax.axis_index("wrap"), 2) == 0


def missing_term(value, beside):
    change = beside - value
    flux = (viscous + value) * change + (0.5 * (1.0 + coef_cb2)) * change * change
    return (0.5 * time_step / coef_sigma) * flux


def prep_kernel(
    xyz_hbm,
    size_hbm,
    nu_hbm,
    chunks_ref,
    pair_ref,
    beside_ref,
    xyz_ref,
    size_ref,
    nu_ref,
    sems,
):
    pairs = ((xyz_hbm, xyz_ref), (size_hbm, size_ref), (nu_hbm, nu_ref))
    copies = [pltpu.make_async_copy(*pair, sems.at[n]) for n, pair in enumerate(pairs)]
    for copy in copies:
        copy.start()
    for copy in copies:
        copy.wait()
    parts = []
    for block in range(size_ref.shape[1] // PBS):
        lanes = slice(block * PBS, (block + 1) * PBS)
        xyz = xyz_ref[:, lanes]
        size = size_ref[:, lanes]
        parts += [xyz, jnp.sum(xyz * xyz, axis=0, keepdims=True) + size * size]
    low_span = lax.axis_index("span") == 0
    rows = nu_ref.shape[0]
    lane = tile_iota(1)
    column = jnp.zeros((8, 128), F32)
    for row in range(rows):
        value = nu_ref[row]
        beside_ref[row : row + 1, :] = edge_row(value, low_span)
        column = jnp.where(lane == row, first_column(value), column)
    pair_ref[...] = jnp.where(even_place(), nu_ref[rows - 1], nu_ref[0])
    chunk = jnp.concatenate(parts + [column], 0)
    for n in range(chunks_ref.shape[0]):
        chunks_ref[n] = chunk


class Halo:
    def __init__(self, nu_ref, pair, after, beside_ref, column, padded_ref, ghost_ref):
        devices = lax.axis_size("wrap")
        place = lax.axis_index("wrap")
        rows = nu_ref.shape[0]
        self.rows = rows
        self.low_span = lax.axis_index("span") == 0
        self.padded, self.ghost, self.beside = padded_ref, ghost_ref, beside_ref
        lower = jnp.where(even_place(), after, pair)
        upper = jnp.where(even_place(), pair, after)
        padded_ref[0] = jnp.where(place == 0, nu_ref[0], lower)
        padded_ref[rows + 1] = jnp.where(place == devices - 1, nu_ref[rows - 1], upper)
        in_wake = (place < devices // 4) | (place >= devices - devices // 4)
        self.in_wake = in_wake
        for row in range(rows):
            value = nu_ref[row]
            padded_ref[row + 1] = value
            partner = jnp.broadcast_to(column[:, rows - 1 - row : rows - row], (8, 128))
            ghost_ref[row] = jnp.where(in_wake, partner, -value)

    def rate(self, row, squares, vorticity):
        value = self.padded[row + 1]
        sub, lane = tile_iota(0), tile_iota(1)
        across = jnp.broadcast_to(self.beside[pl.ds(row, 1), :], (8, 128))
        span_low = jnp.where(self.low_span, value, across)
        span_high = jnp.where(self.low_span, across, value)
        others = (
            self.padded[row],
            self.padded[row + 2],
            jnp.where(sub == 0, span_low, pltpu.roll(value, 1, 0)),
            jnp.where(sub == 7, span_high, pltpu.roll(value, 7, 0)),
            jnp.where(lane == 0, self.ghost[row], pltpu.roll(value, 1, 1)),
            jnp.where(lane == 127, value, pltpu.roll(value, 127, 1)),
        )
        sums = jnp.zeros_like(value)
        squared = jnp.zeros_like(value)
        for other in others:
            change = other - value
            sums = sums + change
            squared = squared + change * change
        flux = (viscous + value) * sums + (0.5 * (1.0 + coef_cb2)) * squared
        scaled = coef_kappa**2 * squares
        modified = vorticity + value / scaled
        ratio = value / (modified * scaled)
        ratio2 = ratio * ratio
        shaped = ratio + coef_cw2 * (ratio2 * ratio2 * ratio2 - ratio)
        shaped2 = shaped * shaped
        base = (1.0 + coef_cw3**6) / (shaped2 * shaped2 * shaped2 + coef_cw3**6)
        factor = shaped * jnp.exp(jnp.log(base) * (1.0 / 6.0))
        return (
            flux / coef_sigma
            + coef_cb1 * modified * value
            - coef_cw1 * factor * value * value / squares
        )


def build_table(halves, table_ref):
    place = lax.axis_index("wrap")
    own_blocks = table_ref.shape[0] // lax.axis_size("wrap")
    groups = lax.axis_size("wrap") >> GROUP_BIT
    slots = groups * (len(Y_MASKS) + 1)

    def body(slot, carry):
        choice = slot // groups
        near = jnp.where(choice == 0, 0, Y_MASKS[0])
        for n in range(1, len(Y_MASKS)):
            near = jnp.where(choice == n + 1, Y_MASKS[n], near)
        low = (place & ((1 << GROUP_BIT) - 1)) ^ near
        skip = jnp.where(choice == 3, 16, 8)
        for half, ref in enumerate(halves):
            base = (((slot % groups) << GROUP_BIT) | (low ^ half)) * own_blocks
            for pair in range(own_blocks // 2):
                start = pl.multiple_of(slot * own_blocks * 4 + skip + pair * 8, 8)
                rows = ref[pl.ds(start, 8), :]
                table_ref[base + pair * 2] = panel_features(rows)
                table_ref[base + pair * 2 + 1] = panel_features(pltpu.roll(rows, 4, 0))
        return carry

    lax.fori_loop(0, slots, body, 0)


def nearest_tile(tile, list_ref, cell_ref, table_ref):
    sub = tile_iota(0)
    unit = jnp.where(sub == 3, 1.0, 0.0)
    xyz = [cell_ref[component, tile] for component in range(3)]
    twice = [-2.0 * part for part in xyz]
    found = []
    for line in range(8):
        rows = unit
        for component in range(3):
            spread = jnp.broadcast_to(twice[component][line : line + 1], (8, 128))
            rows = jnp.where(sub == component, spread, rows)
        cells = cell_features(rows).T
        nearest = None
        for slot in range(0, 8, 2):
            first = list_ref[(tile * 8 + line) * 8 + slot]
            second = list_ref[(tile * 8 + line) * 8 + slot + 1]
            panels = jnp.concatenate([table_ref[first], table_ref[second]], 1)
            value = jnp.dot(cells, panels, preferred_element_type=F32)
            value = jnp.minimum(value[:, :128], value[:, 128:])
            nearest = value if nearest is None else jnp.minimum(nearest, value)
        turned = jnp.min(nearest.T.reshape(16, 8, 128), axis=0)
        found.append(jnp.min(turned, axis=0, keepdims=True))
    norm = xyz[0] * xyz[0] + xyz[1] * xyz[1] + xyz[2] * xyz[2]
    return jnp.concatenate(found, 0) + norm


def main_kernel(
    list_ref,
    own_ref,
    other_ref,
    cell_ref,
    nu_ref,
    vorticity_ref,
    beside_ref,
    dist_ref,
    squares_ref,
    middle_ref,
    pair_out,
    next_out,
    beside_out,
    column_out,
    table_ref,
    padded_ref,
    ghost_ref,
):
    total = (other_ref.shape[0] - 16) // 4
    column = other_ref[3 * total + 8 : 3 * total + 16]
    pair = other_ref[0:8]
    tiles = nu_ref.shape[0]
    even = even_place()
    open_row = jnp.where(even, nu_ref[0], nu_ref[tiles - 1])
    halo = Halo(nu_ref, pair, open_row, beside_ref, column, padded_ref, ghost_ref)
    open_side = jnp.where(even, beside_ref[0:1], beside_ref[tiles - 1 : tiles])
    open_partner = jnp.where(even, column[:, tiles - 1 : tiles], column[:, 0:1])
    next_out[0:8] = open_row
    next_out[16:24] = jnp.broadcast_to(open_side, (8, 128))
    next_out[24:32] = jnp.broadcast_to(open_partner, (8, 128))
    build_table((own_ref, other_ref), table_ref)
    per_step = LINES_PER_STEP // 8

    def body(step, column):
        lane = tile_iota(1)
        for part in range(per_step):
            tile = step * per_step + part
            squares = nearest_tile(tile, list_ref, cell_ref, table_ref)
            squares_ref[tile] = squares
            dist_ref[tile] = jnp.sqrt(squares)
            rate = halo.rate(tile, squares, vorticity_ref[tile])
            middle = nu_ref[tile] + 0.5 * time_step * rate
            middle_ref[tile] = middle
            beside_out[pl.ds(tile, 1), :] = edge_row(middle, halo.low_span)
            column = jnp.where(lane == tile, first_column(middle), column)
        return column

    column = lax.fori_loop(0, tiles // per_step, body, jnp.zeros((8, 128), F32))
    for row in range(0, column_out.shape[0], 8):
        column_out[row : row + 8] = column
    first, last = middle_ref[0], middle_ref[tiles - 1]
    pair_out[...] = jnp.where(even, last, first)
    next_out[8:16] = jnp.where(even, first, last)


def last_kernel(
    middle_ref,
    nu_ref,
    squares_ref,
    vorticity_ref,
    pair_ref,
    mine_ref,
    theirs_ref,
    beside_ref,
    column_ref,
    out_ref,
    padded_ref,
    ghost_ref,
    side_ref,
):
    place = lax.axis_index("wrap")
    rows = nu_ref.shape[0]
    even = even_place()
    inner = (place > 0) & (place < lax.axis_size("wrap") - 1)
    value, partial, side, partner = (mine_ref[n : n + 8] for n in range(0, 32, 8))
    other, other_partial, other_side, other_partner = (theirs_ref[n : n + 8] for n in range(0, 32, 8))
    after = other_partial + missing_term(other, value)
    halo = Halo(
        middle_ref, pair_ref[...], after, beside_ref, column_ref[0:8], padded_ref, ghost_ref
    )
    side_ref[...] = beside_ref[...]
    halo.beside = side_ref
    fixed = partial + missing_term(value, other)
    side_term = missing_term(side, other_side)[0:1]
    partner_term = missing_term(partner, other_partner)
    for row, here in ((0, inner & even), (rows - 1, inner & ~even)):
        own = jnp.where(here, fixed, padded_ref[row + 1])
        padded_ref[row + 1] = own
        ghost = ghost_ref[row] + jnp.where(here, partner_term, 0.0)
        ghost_ref[row] = jnp.where(halo.in_wake, ghost, -own)
        side_ref[row : row + 1] = side_ref[row : row + 1] + jnp.where(here, side_term, 0.0)
    for row in range(rows):
        rate = halo.rate(row, squares_ref[row], vorticity_ref[row])
        out_ref[row] = nu_ref[row] + time_step * rate


def swap_mask(block, mask):
    return lax.ppermute(block, "wrap", [(i, i ^ mask) for i in range(lax.axis_size("wrap"))])


def swap_next(block):
    devices = lax.axis_size("wrap")
    pairs = [(i, (i + 1) % devices) for i in range(1, devices, 2)]
    return lax.ppermute(block, "wrap", pairs + [(j, i) for i, j in pairs])


def swap_span(block):
    return lax.ppermute(block, "span", [(0, 1), (1, 0)])


def gather(chunks, pair, beside):
    devices = lax.axis_size("wrap")
    groups, rows, lanes = chunks.shape
    size = rows - 8
    members = [[low + (n << GROUP_BIT) for n in range(groups)] for low in range(devices // groups)]
    chunks = lax.all_to_all(chunks, "wrap", 0, 0, tiled=True, axis_index_groups=members)
    chunks, beside = lax.optimization_barrier((chunks, swap_span(beside)))
    shard = chunks[:, :size].reshape(groups * size, lanes)
    opposite = groups - 1 - (lax.axis_index("wrap") >> GROUP_BIT)
    column = lax.dynamic_slice(chunks, (opposite, size, 0), (1, 8, lanes))[0]
    first = swap_mask(shard, Y_MASKS[0])
    second = swap_mask(jnp.concatenate([shard, column], 0), Y_MASKS[1])
    third = swap_mask(shard, Y_MASKS[2])
    shard = jnp.concatenate([pair, shard, first, second, third], 0)
    return shard, swap_mask(shard, 1), beside


def shards(cell_xyz, panel_xyz, panel_size, block_lists, nu_field, vorticity):
    devices = lax.axis_size("wrap")
    rows, span, cells = nu_field.shape
    own_blocks = panel_size.shape[0] // PBS
    tile = jax.ShapeDtypeStruct((span, cells), F32)
    field = jax.ShapeDtypeStruct(nu_field.shape, F32)
    side = jax.ShapeDtypeStruct((rows, cells), F32)
    opened = jax.ShapeDtypeStruct((32, cells), F32)
    edges = (tile, opened, side, jax.ShapeDtypeStruct((COLUMN_ROWS, cells), F32))
    scratch = [pltpu.VMEM((rows + 2, span, cells), F32), pltpu.VMEM(nu_field.shape, F32)]

    groups = devices >> GROUP_BIT
    chunks, pair, beside = pl.pallas_call(
        prep_kernel,
        out_shape=(jax.ShapeDtypeStruct((groups, 4 * own_blocks + 8, PBS), F32), tile, side),
        in_specs=[pl.BlockSpec(memory_space=pltpu.HBM)] * 3,
        out_specs=(VMEM,) * 3,
        scratch_shapes=[
            pltpu.VMEM(panel_xyz.shape, F32),
            pltpu.VMEM((1,) + panel_size.shape, F32),
            pltpu.VMEM(nu_field.shape, F32),
            pltpu.SemaphoreType.DMA((3,)),
        ],
        compiler_params=pltpu.CompilerParams(vmem_limit_bytes=60 * 2**20),
        name="prep",
    )(panel_xyz, panel_size[None], nu_field)
    own, other, beside = gather(chunks, pair, beside)

    dist, squares, middle, pair, mine, sides, column = pl.pallas_call(
        main_kernel,
        out_shape=(field, field, field) + edges,
        in_specs=[SMEM] + [VMEM] * 6,
        out_specs=(VMEM,) * 7,
        scratch_shapes=[pltpu.VMEM((devices * own_blocks, FEATS, PBS), BF)] + scratch,
        compiler_params=pltpu.CompilerParams(vmem_limit_bytes=24 * 2**20),
        cost_estimate=pl.CostEstimate(
            flops=2 * 128 * rows * span * cells * block_lists.shape[2] * PBS,
            bytes_accessed=4 * 2**20,
            transcendentals=0,
        ),
        name="main",
    )(block_lists.reshape(-1), own, other, cell_xyz, nu_field, vorticity, beside)
    column = swap_mask(column, devices - 1)
    theirs = swap_next(mine)
    sides = swap_span(sides)
    pair = swap_mask(pair, 1)

    nu_next = pl.pallas_call(
        last_kernel,
        out_shape=field,
        in_specs=[VMEM] * 9,
        out_specs=VMEM,
        scratch_shapes=scratch + [pltpu.VMEM(side.shape, F32)],
        compiler_params=pltpu.CompilerParams(vmem_limit_bytes=8 * 2**20),
        name="last",
    )(middle, nu_field, squares, vorticity, pair, mine, theirs, sides, column)
    return (nu_next, dist)


def solution(mesh):
    in_specs = (
        P(None, "wrap", "span", None),
        P(None, "wrap"),
        P("wrap"),
        P("wrap", "span", None),
        P("wrap", "span", None),
        P("wrap", "span", None),
    )
    out_specs = (P("wrap", "span", None), P("wrap", "span", None))
    return jax.shard_map(shards, mesh=mesh, in_specs=in_specs, out_specs=out_specs, check_vma=False)
```

```python
import functools

import jax
import jax.numpy as jnp
from jax import lax
from jax.experimental import pallas as pl
from jax.experimental.pallas import tpu as pltpu
from jax.sharding import PartitionSpec as P

BF = jnp.bfloat16
F32 = jnp.float32
PBS = 128
FEATS = 48
LINES_PER_STEP = 128
COLUMN_ROWS = 48
SIDE_ROWS = 40
GROUP_BIT = 3
Y_MASKS = (2, 6, 4)

coef_cb1 = 0.1355
coef_cb2 = 0.622
coef_sigma = 2.0 / 3.0
coef_kappa = 0.41
coef_cw2 = 0.3
coef_cw3 = 2.0
viscous = 1.0
time_step = 0.03
coef_cw1 = coef_cb1 / coef_kappa**2 + (1.0 + coef_cb2) / coef_sigma

SMEM = pl.BlockSpec(memory_space=pltpu.SMEM)
VMEM = pl.BlockSpec(memory_space=pltpu.VMEM)


def tile_iota(dim):
    return lax.broadcasted_iota(jnp.int32, (8, 128), dim)


def split_rows(rows):
    high = rows.astype(BF).astype(F32)
    rest = rows - high
    mid = rest.astype(BF).astype(F32)
    return high, mid, rest - mid


def panel_features(rows):
    high, mid, low = split_rows(rows)
    return jnp.concatenate([high, high, high, mid, mid, low], 0).astype(BF)


def cell_features(rows):
    high, mid, low = split_rows(rows)
    return jnp.concatenate([high, mid, low, high, mid, high], 0).astype(BF)


def edge_row(value, low_span):
    return jnp.where(low_span, value[7:8], value[0:1])


def first_column(value):
    return jnp.broadcast_to(value[:, 0:1], (8, 128))


def even_place():
    return lax.rem(lax.axis_index("wrap"), 2) == 0


def missing_term(value, beside):
    change = beside - value
    flux = (viscous + value) * change + (0.5 * (1.0 + coef_cb2)) * change * change
    return (0.5 * time_step / coef_sigma) * flux


def prep_kernel(
    xyz_hbm,
    size_hbm,
    nu_hbm,
    chunks_ref,
    pair_ref,
    beside_ref,
    xyz_ref,
    size_ref,
    nu_ref,
    sems,
):
    pairs = ((xyz_hbm, xyz_ref), (size_hbm, size_ref), (nu_hbm, nu_ref))
    copies = [pltpu.make_async_copy(*pair, sems.at[n]) for n, pair in enumerate(pairs)]
    for copy in copies:
        copy.start()
    for copy in copies:
        copy.wait()
    parts = []
    for block in range(size_ref.shape[1] // PBS):
        lanes = slice(block * PBS, (block + 1) * PBS)
        xyz = xyz_ref[:, lanes]
        size = size_ref[:, lanes]
        parts += [xyz, jnp.sum(xyz * xyz, axis=0, keepdims=True) + size * size]
    low_span = lax.axis_index("span") == 0
    rows = nu_ref.shape[0]
    lane = tile_iota(1)
    column = jnp.zeros((8, 128), F32)
    for row in range(rows):
        value = nu_ref[row]
        beside_ref[row : row + 1, :] = edge_row(value, low_span)
        column = jnp.where(lane == row, first_column(value), column)
    pair_ref[...] = jnp.where(even_place(), nu_ref[rows - 1], nu_ref[0])
    chunk = jnp.concatenate(parts + [column], 0)
    for n in range(chunks_ref.shape[0]):
        chunks_ref[n] = chunk


class Halo:
    def __init__(self, nu_ref, pair, after, beside_ref, column, padded_ref, ghost_ref):
        devices = lax.axis_size("wrap")
        place = lax.axis_index("wrap")
        rows = nu_ref.shape[0]
        self.rows = rows
        self.low_span = lax.axis_index("span") == 0
        self.padded, self.ghost, self.beside = padded_ref, ghost_ref, beside_ref
        lower = jnp.where(even_place(), after, pair)
        upper = jnp.where(even_place(), pair, after)
        padded_ref[0] = jnp.where(place == 0, nu_ref[0], lower)
        padded_ref[rows + 1] = jnp.where(place == devices - 1, nu_ref[rows - 1], upper)
        in_wake = (place < devices // 4) | (place >= devices - devices // 4)
        self.in_wake = in_wake
        for row in range(rows):
            value = nu_ref[row]
            padded_ref[row + 1] = value
            partner = jnp.broadcast_to(column[:, rows - 1 - row : rows - row], (8, 128))
            ghost_ref[row] = jnp.where(in_wake, partner, -value)

    def rate(self, row, squares, vorticity):
        value = self.padded[row + 1]
        sub, lane = tile_iota(0), tile_iota(1)
        across = jnp.broadcast_to(self.beside[pl.ds(row, 1), :], (8, 128))
        span_low = jnp.where(self.low_span, value, across)
        span_high = jnp.where(self.low_span, across, value)
        others = (
            self.padded[row],
            self.padded[row + 2],
            jnp.where(sub == 0, span_low, pltpu.roll(value, 1, 0)),
            jnp.where(sub == 7, span_high, pltpu.roll(value, 7, 0)),
            jnp.where(lane == 0, self.ghost[row], pltpu.roll(value, 1, 1)),
            jnp.where(lane == 127, value, pltpu.roll(value, 127, 1)),
        )
        sums = jnp.zeros_like(value)
        squared = jnp.zeros_like(value)
        for other in others:
            change = other - value
            sums = sums + change
            squared = squared + change * change
        flux = (viscous + value) * sums + (0.5 * (1.0 + coef_cb2)) * squared
        scaled = coef_kappa**2 * squares
        modified = vorticity + value / scaled
        ratio = value / (modified * scaled)
        ratio2 = ratio * ratio
        shaped = ratio + coef_cw2 * (ratio2 * ratio2 * ratio2 - ratio)
        shaped2 = shaped * shaped
        base = (1.0 + coef_cw3**6) / (shaped2 * shaped2 * shaped2 + coef_cw3**6)
        factor = shaped * jnp.exp(jnp.log(base) * (1.0 / 6.0))
        return (
            flux / coef_sigma
            + coef_cb1 * modified * value
            - coef_cw1 * factor * value * value / squares
        )


def build_table(halves, table_ref):
    place = lax.axis_index("wrap")
    own_blocks = table_ref.shape[0] // lax.axis_size("wrap")
    groups = lax.axis_size("wrap") >> GROUP_BIT
    slots = groups * (len(Y_MASKS) + 1)

    def body(slot, carry):
        choice = slot // groups
        near = jnp.where(choice == 0, 0, Y_MASKS[0])
        for n in range(1, len(Y_MASKS)):
            near = jnp.where(choice == n + 1, Y_MASKS[n], near)
        low = (place & ((1 << GROUP_BIT) - 1)) ^ near
        skip = jnp.where(choice == 3, 16, 8)
        for half, ref in enumerate(halves):
            base = (((slot % groups) << GROUP_BIT) | (low ^ half)) * own_blocks
            for pair in range(own_blocks // 2):
                start = pl.multiple_of(slot * own_blocks * 4 + skip + pair * 8, 8)
                rows = ref[pl.ds(start, 8), :]
                table_ref[base + pair * 2] = panel_features(rows)
                table_ref[base + pair * 2 + 1] = panel_features(pltpu.roll(rows, 4, 0))
        return carry

    lax.fori_loop(0, slots, body, 0, unroll=4)


def nearest_tile(tile, list_ref, cell_ref, table_ref):
    sub = tile_iota(0)
    unit = jnp.where(sub == 3, 1.0, 0.0)
    xyz = [cell_ref[component, tile] for component in range(3)]
    twice = [-2.0 * part for part in xyz]
    found = []
    for line in range(8):
        rows = unit
        for component in range(3):
            spread = jnp.broadcast_to(twice[component][line : line + 1], (8, 128))
            rows = jnp.where(sub == component, spread, rows)
        cells = cell_features(rows).T
        nearest = None
        for slot in range(0, 8, 2):
            first = list_ref[(tile * 8 + line) * 8 + slot]
            second = list_ref[(tile * 8 + line) * 8 + slot + 1]
            panels = jnp.concatenate([table_ref[first], table_ref[second]], 1)
            value = jnp.dot(cells, panels, preferred_element_type=F32)
            value = jnp.minimum(value[:, :128], value[:, 128:])
            nearest = value if nearest is None else jnp.minimum(nearest, value)
        turned = jnp.min(nearest.T.reshape(16, 8, 128), axis=0)
        found.append(jnp.min(turned, axis=0, keepdims=True))
    norm = xyz[0] * xyz[0] + xyz[1] * xyz[1] + xyz[2] * xyz[2]
    return jnp.concatenate(found, 0) + norm


def main_kernel(
    list_ref,
    own_ref,
    other_ref,
    cell_ref,
    nu_ref,
    vorticity_ref,
    beside_ref,
    dist_ref,
    squares_ref,
    middle_ref,
    pair_out,
    next_out,
    beside_out,
    column_out,
    table_ref,
    padded_ref,
    ghost_ref,
):
    total = (other_ref.shape[0] - 16) // 4
    column = other_ref[3 * total + 8 : 3 * total + 16]
    pair = other_ref[0:8]
    tiles = nu_ref.shape[0]
    even = even_place()
    open_row = jnp.where(even, nu_ref[0], nu_ref[tiles - 1])
    halo = Halo(nu_ref, pair, open_row, beside_ref, column, padded_ref, ghost_ref)
    open_side = jnp.where(even, beside_ref[0:1], beside_ref[tiles - 1 : tiles])
    open_partner = jnp.where(even, column[:, tiles - 1 : tiles], column[:, 0:1])
    next_out[0:8] = open_row
    next_out[16:24] = jnp.broadcast_to(open_side, (8, 128))
    next_out[24:32] = jnp.broadcast_to(open_partner, (8, 128))
    build_table((own_ref, other_ref), table_ref)
    per_step = LINES_PER_STEP // 8

    def body(step, column):
        lane = tile_iota(1)
        for part in range(per_step):
            tile = step * per_step + part
            squares = nearest_tile(tile, list_ref, cell_ref, table_ref)
            squares_ref[tile] = squares
            dist_ref[tile] = jnp.sqrt(squares)
            rate = halo.rate(tile, squares, vorticity_ref[tile])
            middle = nu_ref[tile] + 0.5 * time_step * rate
            middle_ref[tile] = middle
            beside_out[pl.ds(tile, 1), :] = edge_row(middle, halo.low_span)
            column = jnp.where(lane == tile, first_column(middle), column)
        return column

    column = lax.fori_loop(0, tiles // per_step, body, jnp.zeros((8, 128), F32))
    for row in range(0, column_out.shape[0], 8):
        column_out[row : row + 8] = column
    beside_out[tiles:] = jnp.zeros((beside_out.shape[0] - tiles, 128), F32)
    first, last = middle_ref[0], middle_ref[tiles - 1]
    pair_out[...] = jnp.where(even, last, first)
    next_out[8:16] = jnp.where(even, first, last)


def last_kernel(
    middle_ref,
    nu_ref,
    squares_ref,
    vorticity_ref,
    pair_ref,
    mine_ref,
    theirs_ref,
    beside_ref,
    column_ref,
    out_ref,
    padded_ref,
    ghost_ref,
    side_ref,
):
    place = lax.axis_index("wrap")
    rows = nu_ref.shape[0]
    even = even_place()
    inner = (place > 0) & (place < lax.axis_size("wrap") - 1)
    value, partial, side, partner = (mine_ref[n : n + 8] for n in range(0, 32, 8))
    other, other_partial, other_side, other_partner = (theirs_ref[n : n + 8] for n in range(0, 32, 8))
    after = other_partial + missing_term(other, value)
    halo = Halo(
        middle_ref, pair_ref[...], after, beside_ref, column_ref[0:8], padded_ref, ghost_ref
    )
    side_ref[...] = beside_ref[0:rows]
    halo.beside = side_ref
    fixed = partial + missing_term(value, other)
    side_term = missing_term(side, other_side)[0:1]
    partner_term = missing_term(partner, other_partner)
    for row, here in ((0, inner & even), (rows - 1, inner & ~even)):
        own = jnp.where(here, fixed, padded_ref[row + 1])
        padded_ref[row + 1] = own
        ghost = ghost_ref[row] + jnp.where(here, partner_term, 0.0)
        ghost_ref[row] = jnp.where(halo.in_wake, ghost, -own)
        side_ref[row : row + 1] = side_ref[row : row + 1] + jnp.where(here, side_term, 0.0)
    for row in range(rows):
        rate = halo.rate(row, squares_ref[row], vorticity_ref[row])
        out_ref[row] = nu_ref[row] + time_step * rate


def swap_mask(block, mask):
    return lax.ppermute(block, "wrap", [(i, i ^ mask) for i in range(lax.axis_size("wrap"))])


def swap_next(block):
    devices = lax.axis_size("wrap")
    pairs = [(i, (i + 1) % devices) for i in range(1, devices, 2)]
    return lax.ppermute(block, "wrap", pairs + [(j, i) for i, j in pairs])


def swap_span(block):
    return lax.ppermute(block, "span", [(0, 1), (1, 0)])


def gather(chunks, pair, beside):
    devices = lax.axis_size("wrap")
    groups, rows, lanes = chunks.shape
    size = rows - 8
    members = [[low + (n << GROUP_BIT) for n in range(groups)] for low in range(devices // groups)]
    chunks = lax.all_to_all(chunks, "wrap", 0, 0, tiled=True, axis_index_groups=members)
    chunks, beside = lax.optimization_barrier((chunks, swap_span(beside)))
    shard = chunks[:, :size].reshape(groups * size, lanes)
    opposite = groups - 1 - (lax.axis_index("wrap") >> GROUP_BIT)
    column = lax.dynamic_slice(chunks, (opposite, size, 0), (1, 8, lanes))[0]
    first = swap_mask(shard, Y_MASKS[0])
    second = swap_mask(jnp.concatenate([shard, column], 0), Y_MASKS[1])
    third = swap_mask(shard, Y_MASKS[2])
    shard = jnp.concatenate([pair, shard, first, second, third], 0)
    return shard, swap_mask(shard, 1), beside


def shards(cell_xyz, panel_xyz, panel_size, block_lists, nu_field, vorticity):
    devices = lax.axis_size("wrap")
    rows, span, cells = nu_field.shape
    own_blocks = panel_size.shape[0] // PBS
    tile = jax.ShapeDtypeStruct((span, cells), F32)
    field = jax.ShapeDtypeStruct(nu_field.shape, F32)
    side = jax.ShapeDtypeStruct((rows, cells), F32)
    opened = jax.ShapeDtypeStruct((32, cells), F32)
    edges = (
        tile,
        opened,
        jax.ShapeDtypeStruct((SIDE_ROWS, cells), F32),
        jax.ShapeDtypeStruct((COLUMN_ROWS, cells), F32),
    )
    scratch = [pltpu.VMEM((rows + 2, span, cells), F32), pltpu.VMEM(nu_field.shape, F32)]

    groups = devices >> GROUP_BIT
    chunks, pair, beside = pl.pallas_call(
        prep_kernel,
        out_shape=(jax.ShapeDtypeStruct((groups, 4 * own_blocks + 8, PBS), F32), tile, side),
        in_specs=[pl.BlockSpec(memory_space=pltpu.HBM)] * 3,
        out_specs=(VMEM,) * 3,
        scratch_shapes=[
            pltpu.VMEM(panel_xyz.shape, F32),
            pltpu.VMEM((1,) + panel_size.shape, F32),
            pltpu.VMEM(nu_field.shape, F32),
            pltpu.SemaphoreType.DMA((3,)),
        ],
        compiler_params=pltpu.CompilerParams(vmem_limit_bytes=60 * 2**20),
        name="prep",
    )(panel_xyz, panel_size[None], nu_field)
    own, other, beside = gather(chunks, pair, beside)

    dist, squares, middle, pair, mine, sides, column = pl.pallas_call(
        main_kernel,
        out_shape=(field, field, field) + edges,
        in_specs=[SMEM] + [VMEM] * 6,
        out_specs=(VMEM,) * 7,
        scratch_shapes=[pltpu.VMEM((devices * own_blocks, FEATS, PBS), BF)] + scratch,
        compiler_params=pltpu.CompilerParams(vmem_limit_bytes=24 * 2**20),
        cost_estimate=pl.CostEstimate(
            flops=2 * 128 * rows * span * cells * block_lists.shape[2] * PBS,
            bytes_accessed=4 * 2**20,
            transcendentals=0,
        ),
        name="main",
    )(block_lists.reshape(-1), own, other, cell_xyz, nu_field, vorticity, beside)
    column = swap_mask(column, devices - 1)
    theirs = swap_next(mine)
    sides = swap_span(sides)
    pair = swap_mask(pair, 1)

    nu_next = pl.pallas_call(
        last_kernel,
        out_shape=field,
        in_specs=[VMEM] * 9,
        out_specs=VMEM,
        scratch_shapes=scratch + [pltpu.VMEM(side.shape, F32)],
        compiler_params=pltpu.CompilerParams(vmem_limit_bytes=8 * 2**20),
        name="last",
    )(middle, nu_field, squares, vorticity, pair, mine, theirs, sides, column)
    return (nu_next, dist)


def solution(mesh):
    in_specs = (
        P(None, "wrap", "span", None),
        P(None, "wrap"),
        P("wrap"),
        P("wrap", "span", None),
        P("wrap", "span", None),
        P("wrap", "span", None),
    )
    out_specs = (P("wrap", "span", None), P("wrap", "span", None))
    return jax.shard_map(shards, mesh=mesh, in_specs=in_specs, out_specs=out_specs, check_vma=False)
```

```python
import functools

import jax
import jax.numpy as jnp
from jax import lax
from jax.experimental import pallas as pl
from jax.experimental.pallas import tpu as pltpu
from jax.sharding import PartitionSpec as P

BF = jnp.bfloat16
F32 = jnp.float32
PBS = 128
FEATS = 48
LINES_PER_STEP = 128
COLUMN_ROWS = 48
SIDE_ROWS = 40
GROUP_BIT = 3
Y_MASKS = (2, 6, 4)

coef_cb1 = 0.1355
coef_cb2 = 0.622
coef_sigma = 2.0 / 3.0
coef_kappa = 0.41
coef_cw2 = 0.3
coef_cw3 = 2.0
viscous = 1.0
time_step = 0.03
coef_cw1 = coef_cb1 / coef_kappa**2 + (1.0 + coef_cb2) / coef_sigma

SMEM = pl.BlockSpec(memory_space=pltpu.SMEM)
VMEM = pl.BlockSpec(memory_space=pltpu.VMEM)


def tile_iota(dim):
    return lax.broadcasted_iota(jnp.int32, (8, 128), dim)


def split_rows(rows):
    high = rows.astype(BF).astype(F32)
    rest = rows - high
    mid = rest.astype(BF).astype(F32)
    return high, mid, rest - mid


def panel_features(rows):
    high, mid, low = split_rows(rows)
    return jnp.concatenate([high, high, high, mid, mid, low], 0).astype(BF)


def cell_features(rows):
    high, mid, low = split_rows(rows)
    return jnp.concatenate([high, mid, low, high, mid, high], 0).astype(BF)


def edge_row(value, low_span):
    return jnp.where(low_span, value[7:8], value[0:1])


def first_column(value):
    return jnp.broadcast_to(value[:, 0:1], (8, 128))


def even_place():
    return lax.rem(lax.axis_index("wrap"), 2) == 0


def missing_term(value, beside):
    change = beside - value
    flux = (viscous + value) * change + (0.5 * (1.0 + coef_cb2)) * change * change
    return (0.5 * time_step / coef_sigma) * flux


def prep_kernel(
    xyz_hbm,
    size_hbm,
    nu_hbm,
    chunks_ref,
    pair_ref,
    beside_ref,
    xyz_ref,
    size_ref,
    nu_ref,
    sems,
):
    pairs = ((xyz_hbm, xyz_ref), (size_hbm, size_ref), (nu_hbm, nu_ref))
    copies = [pltpu.make_async_copy(*pair, sems.at[n]) for n, pair in enumerate(pairs)]
    for copy in copies:
        copy.start()
    for copy in copies:
        copy.wait()
    parts = []
    for block in range(size_ref.shape[1] // PBS):
        lanes = slice(block * PBS, (block + 1) * PBS)
        xyz = xyz_ref[:, lanes]
        size = size_ref[:, lanes]
        parts += [xyz, jnp.sum(xyz * xyz, axis=0, keepdims=True) + size * size]
    low_span = lax.axis_index("span") == 0
    rows = nu_ref.shape[0]
    lane = tile_iota(1)
    column = jnp.zeros((8, 128), F32)
    for row in range(rows):
        value = nu_ref[row]
        beside_ref[row : row + 1, :] = edge_row(value, low_span)
        column = jnp.where(lane == row, first_column(value), column)
    pair_ref[...] = jnp.where(even_place(), nu_ref[rows - 1], nu_ref[0])
    chunk = jnp.concatenate(parts + [column], 0)
    for n in range(chunks_ref.shape[0]):
        chunks_ref[n] = chunk


class Halo:
    def __init__(self, nu_ref, pair, after, beside_ref, column, padded_ref, ghost_ref):
        devices = lax.axis_size("wrap")
        place = lax.axis_index("wrap")
        rows = nu_ref.shape[0]
        self.rows = rows
        self.low_span = lax.axis_index("span") == 0
        self.padded, self.ghost, self.beside = padded_ref, ghost_ref, beside_ref
        lower = jnp.where(even_place(), after, pair)
        upper = jnp.where(even_place(), pair, after)
        padded_ref[0] = jnp.where(place == 0, nu_ref[0], lower)
        padded_ref[rows + 1] = jnp.where(place == devices - 1, nu_ref[rows - 1], upper)
        in_wake = (place < devices // 4) | (place >= devices - devices // 4)
        self.in_wake = in_wake
        for row in range(rows):
            value = nu_ref[row]
            padded_ref[row + 1] = value
            partner = jnp.broadcast_to(column[:, rows - 1 - row : rows - row], (8, 128))
            ghost_ref[row] = jnp.where(in_wake, partner, -value)

    def rate(self, row, squares, vorticity):
        value = self.padded[row + 1]
        sub, lane = tile_iota(0), tile_iota(1)
        across = jnp.broadcast_to(self.beside[pl.ds(row, 1), :], (8, 128))
        span_low = jnp.where(self.low_span, value, across)
        span_high = jnp.where(self.low_span, across, value)
        others = (
            self.padded[row],
            self.padded[row + 2],
            jnp.where(sub == 0, span_low, pltpu.roll(value, 1, 0)),
            jnp.where(sub == 7, span_high, pltpu.roll(value, 7, 0)),
            jnp.where(lane == 0, self.ghost[row], pltpu.roll(value, 1, 1)),
            jnp.where(lane == 127, value, pltpu.roll(value, 127, 1)),
        )
        sums = jnp.zeros_like(value)
        squared = jnp.zeros_like(value)
        for other in others:
            change = other - value
            sums = sums + change
            squared = squared + change * change
        flux = (viscous + value) * sums + (0.5 * (1.0 + coef_cb2)) * squared
        scaled = coef_kappa**2 * squares
        modified = vorticity + value / scaled
        ratio = value / (modified * scaled)
        ratio2 = ratio * ratio
        shaped = ratio + coef_cw2 * (ratio2 * ratio2 * ratio2 - ratio)
        shaped2 = shaped * shaped
        base = (1.0 + coef_cw3**6) / (shaped2 * shaped2 * shaped2 + coef_cw3**6)
        factor = shaped * jnp.exp(jnp.log(base) * (1.0 / 6.0))
        return (
            flux / coef_sigma
            + coef_cb1 * modified * value
            - coef_cw1 * factor * value * value / squares
        )


def build_table(halves, table_ref):
    place = lax.axis_index("wrap")
    own_blocks = table_ref.shape[0] // lax.axis_size("wrap")
    groups = lax.axis_size("wrap") >> GROUP_BIT
    low = place & ((1 << GROUP_BIT) - 1)

    def body(group, carry):
        for half, pieces in enumerate(halves):
            for ref, mask in zip(pieces, (0,) + Y_MASKS):
                base = ((group << GROUP_BIT) | (low ^ mask ^ half)) * own_blocks
                for pair in range(own_blocks // 2):
                    start = pl.multiple_of(group * own_blocks * 4 + pair * 8, 8)
                    rows = ref[pl.ds(start, 8), :]
                    table_ref[base + pair * 2] = panel_features(rows)
                    table_ref[base + pair * 2 + 1] = panel_features(pltpu.roll(rows, 4, 0))
        return carry

    lax.fori_loop(0, groups, body, 0)


def nearest_tile(tile, list_ref, cell_ref, table_ref):
    sub = tile_iota(0)
    unit = jnp.where(sub == 3, 1.0, 0.0)
    xyz = [cell_ref[component, tile] for component in range(3)]
    twice = [-2.0 * part for part in xyz]
    found = []
    for line in range(8):
        rows = unit
        for component in range(3):
            spread = jnp.broadcast_to(twice[component][line : line + 1], (8, 128))
            rows = jnp.where(sub == component, spread, rows)
        cells = cell_features(rows).T
        nearest = None
        for slot in range(0, 8, 2):
            first = list_ref[(tile * 8 + line) * 8 + slot]
            second = list_ref[(tile * 8 + line) * 8 + slot + 1]
            panels = jnp.concatenate([table_ref[first], table_ref[second]], 1)
            value = jnp.dot(cells, panels, preferred_element_type=F32)
            value = jnp.minimum(value[:, :128], value[:, 128:])
            nearest = value if nearest is None else jnp.minimum(nearest, value)
        turned = jnp.min(nearest.T.reshape(16, 8, 128), axis=0)
        found.append(jnp.min(turned, axis=0, keepdims=True))
    norm = xyz[0] * xyz[0] + xyz[1] * xyz[1] + xyz[2] * xyz[2]
    return jnp.concatenate(found, 0) + norm


def main_kernel(
    list_ref,
    own0_ref,
    own1_ref,
    own2_ref,
    own3_ref,
    other0_ref,
    other1_ref,
    other2_ref,
    other3_ref,
    cell_ref,
    nu_ref,
    vorticity_ref,
    beside_ref,
    dist_ref,
    squares_ref,
    middle_ref,
    pair_out,
    next_out,
    beside_out,
    column_out,
    table_ref,
    padded_ref,
    ghost_ref,
):
    total = own0_ref.shape[0]
    column = other2_ref[total : total + 8]
    pair = other0_ref[total : total + 8]
    tiles = nu_ref.shape[0]
    even = even_place()
    open_row = jnp.where(even, nu_ref[0], nu_ref[tiles - 1])
    halo = Halo(nu_ref, pair, open_row, beside_ref, column, padded_ref, ghost_ref)
    open_side = jnp.where(even, beside_ref[0:1], beside_ref[tiles - 1 : tiles])
    open_partner = jnp.where(even, column[:, tiles - 1 : tiles], column[:, 0:1])
    next_out[0:8] = open_row
    next_out[16:24] = jnp.broadcast_to(open_side, (8, 128))
    next_out[24:32] = jnp.broadcast_to(open_partner, (8, 128))
    own = (own0_ref, own1_ref, own2_ref, own3_ref)
    other = (other0_ref, other1_ref, other2_ref, other3_ref)
    build_table((own, other), table_ref)
    per_step = LINES_PER_STEP // 8

    def body(step, column):
        lane = tile_iota(1)
        for part in range(per_step):
            tile = step * per_step + part
            squares = nearest_tile(tile, list_ref, cell_ref, table_ref)
            squares_ref[tile] = squares
            dist_ref[tile] = jnp.sqrt(squares)
            rate = halo.rate(tile, squares, vorticity_ref[tile])
            middle = nu_ref[tile] + 0.5 * time_step * rate
            middle_ref[tile] = middle
            beside_out[pl.ds(tile, 1), :] = edge_row(middle, halo.low_span)
            column = jnp.where(lane == tile, first_column(middle), column)
        return column

    column = lax.fori_loop(0, tiles // per_step, body, jnp.zeros((8, 128), F32))
    for row in range(0, column_out.shape[0], 8):
        column_out[row : row + 8] = column
    beside_out[tiles:] = jnp.zeros((beside_out.shape[0] - tiles, 128), F32)
    first, last = middle_ref[0], middle_ref[tiles - 1]
    pair_out[...] = jnp.where(even, last, first)
    next_out[8:16] = jnp.where(even, first, last)


def last_kernel(
    middle_ref,
    nu_ref,
    squares_ref,
    vorticity_ref,
    pair_ref,
    mine_ref,
    theirs_ref,
    beside_ref,
    column_ref,
    out_ref,
    padded_ref,
    ghost_ref,
    side_ref,
):
    place = lax.axis_index("wrap")
    rows = nu_ref.shape[0]
    even = even_place()
    inner = (place > 0) & (place < lax.axis_size("wrap") - 1)
    value, partial, side, partner = (mine_ref[n : n + 8] for n in range(0, 32, 8))
    other, other_partial, other_side, other_partner = (theirs_ref[n : n + 8] for n in range(0, 32, 8))
    after = other_partial + missing_term(other, value)
    halo = Halo(
        middle_ref, pair_ref[...], after, beside_ref, column_ref[0:8], padded_ref, ghost_ref
    )
    side_ref[...] = beside_ref[0:rows]
    halo.beside = side_ref
    fixed = partial + missing_term(value, other)
    side_term = missing_term(side, other_side)[0:1]
    partner_term = missing_term(partner, other_partner)
    for row, here in ((0, inner & even), (rows - 1, inner & ~even)):
        own = jnp.where(here, fixed, padded_ref[row + 1])
        padded_ref[row + 1] = own
        ghost = ghost_ref[row] + jnp.where(here, partner_term, 0.0)
        ghost_ref[row] = jnp.where(halo.in_wake, ghost, -own)
        side_ref[row : row + 1] = side_ref[row : row + 1] + jnp.where(here, side_term, 0.0)
    for row in range(rows):
        rate = halo.rate(row, squares_ref[row], vorticity_ref[row])
        out_ref[row] = nu_ref[row] + time_step * rate


def swap_mask(block, mask):
    return lax.ppermute(block, "wrap", [(i, i ^ mask) for i in range(lax.axis_size("wrap"))])


def swap_next(block):
    devices = lax.axis_size("wrap")
    pairs = [(i, (i + 1) % devices) for i in range(1, devices, 2)]
    return lax.ppermute(block, "wrap", pairs + [(j, i) for i, j in pairs])


def swap_span(block):
    return lax.ppermute(block, "span", [(0, 1), (1, 0)])


def gather(chunks, pair, beside):
    devices = lax.axis_size("wrap")
    groups, rows, lanes = chunks.shape
    size = rows - 8
    members = [[low + (n << GROUP_BIT) for n in range(groups)] for low in range(devices // groups)]
    chunks = lax.all_to_all(chunks, "wrap", 0, 0, tiled=True, axis_index_groups=members)
    chunks, beside = lax.optimization_barrier((chunks, swap_span(beside)))
    shard = chunks[:, :size].reshape(groups * size, lanes)
    opposite = groups - 1 - (lax.axis_index("wrap") >> GROUP_BIT)
    column = lax.dynamic_slice(chunks, (opposite, size, 0), (1, 8, lanes))[0]
    own = [
        shard,
        swap_mask(shard, Y_MASKS[0]),
        swap_mask(jnp.concatenate([shard, column], 0), Y_MASKS[1]),
        swap_mask(shard, Y_MASKS[2]),
    ]
    other = [swap_mask(jnp.concatenate([shard, pair], 0), 1)]
    other += [swap_mask(piece, 1) for piece in own[1:]]
    return own, other, beside


def shards(cell_xyz, panel_xyz, panel_size, block_lists, nu_field, vorticity):
    devices = lax.axis_size("wrap")
    rows, span, cells = nu_field.shape
    own_blocks = panel_size.shape[0] // PBS
    tile = jax.ShapeDtypeStruct((span, cells), F32)
    field = jax.ShapeDtypeStruct(nu_field.shape, F32)
    side = jax.ShapeDtypeStruct((rows, cells), F32)
    opened = jax.ShapeDtypeStruct((32, cells), F32)
    edges = (
        tile,
        opened,
        jax.ShapeDtypeStruct((SIDE_ROWS, cells), F32),
        jax.ShapeDtypeStruct((COLUMN_ROWS, cells), F32),
    )
    scratch = [pltpu.VMEM((rows + 2, span, cells), F32), pltpu.VMEM(nu_field.shape, F32)]

    groups = devices >> GROUP_BIT
    chunks, pair, beside = pl.pallas_call(
        prep_kernel,
        out_shape=(jax.ShapeDtypeStruct((groups, 4 * own_blocks + 8, PBS), F32), tile, side),
        in_specs=[pl.BlockSpec(memory_space=pltpu.HBM)] * 3,
        out_specs=(VMEM,) * 3,
        scratch_shapes=[
            pltpu.VMEM(panel_xyz.shape, F32),
            pltpu.VMEM((1,) + panel_size.shape, F32),
            pltpu.VMEM(nu_field.shape, F32),
            pltpu.SemaphoreType.DMA((3,)),
        ],
        compiler_params=pltpu.CompilerParams(vmem_limit_bytes=60 * 2**20),
        name="prep",
    )(panel_xyz, panel_size[None], nu_field)
    own, other, beside = gather(chunks, pair, beside)

    dist, squares, middle, pair, mine, sides, column = pl.pallas_call(
        main_kernel,
        out_shape=(field, field, field) + edges,
        in_specs=[SMEM] + [VMEM] * 12,
        out_specs=(VMEM,) * 7,
        scratch_shapes=[pltpu.VMEM((devices * own_blocks, FEATS, PBS), BF)] + scratch,
        compiler_params=pltpu.CompilerParams(vmem_limit_bytes=24 * 2**20),
        cost_estimate=pl.CostEstimate(
            flops=2 * 128 * rows * span * cells * block_lists.shape[2] * PBS,
            bytes_accessed=4 * 2**20,
            transcendentals=0,
        ),
        name="main",
    )(block_lists.reshape(-1), *own, *other, cell_xyz, nu_field, vorticity, beside)
    column = swap_mask(column, devices - 1)
    theirs = swap_next(mine)
    sides = swap_span(sides)
    pair = swap_mask(pair, 1)

    nu_next = pl.pallas_call(
        last_kernel,
        out_shape=field,
        in_specs=[VMEM] * 9,
        out_specs=VMEM,
        scratch_shapes=scratch + [pltpu.VMEM(side.shape, F32)],
        compiler_params=pltpu.CompilerParams(vmem_limit_bytes=8 * 2**20),
        name="last",
    )(middle, nu_field, squares, vorticity, pair, mine, theirs, sides, column)
    return (nu_next, dist)


def solution(mesh):
    in_specs = (
        P(None, "wrap", "span", None),
        P(None, "wrap"),
        P("wrap"),
        P("wrap", "span", None),
        P("wrap", "span", None),
        P("wrap", "span", None),
    )
    out_specs = (P("wrap", "span", None), P("wrap", "span", None))
    return jax.shard_map(shards, mesh=mesh, in_specs=in_specs, out_specs=out_specs, check_vma=False)
```

```python
import functools

import jax
import jax.numpy as jnp
from jax import lax
from jax.experimental import pallas as pl
from jax.experimental.pallas import tpu as pltpu
from jax.sharding import PartitionSpec as P

BF = jnp.bfloat16
F32 = jnp.float32
PBS = 128
FEATS = 48
LINES_PER_STEP = 128
COLUMN_ROWS = 48
SIDE_ROWS = 40
GROUP_BIT = 3
Y_MASKS = (2, 6, 4)

coef_cb1 = 0.1355
coef_cb2 = 0.622
coef_sigma = 2.0 / 3.0
coef_kappa = 0.41
coef_cw2 = 0.3
coef_cw3 = 2.0
viscous = 1.0
time_step = 0.03
coef_cw1 = coef_cb1 / coef_kappa**2 + (1.0 + coef_cb2) / coef_sigma

SMEM = pl.BlockSpec(memory_space=pltpu.SMEM)
VMEM = pl.BlockSpec(memory_space=pltpu.VMEM)


def tile_iota(dim):
    return lax.broadcasted_iota(jnp.int32, (8, 128), dim)


def split_rows(rows):
    high = rows.astype(BF).astype(F32)
    rest = rows - high
    mid = rest.astype(BF).astype(F32)
    return high, mid, rest - mid


def panel_features(rows):
    high, mid, low = split_rows(rows)
    return jnp.concatenate([high, high, high, mid, mid, low], 0).astype(BF)


def cell_features(rows):
    high, mid, low = split_rows(rows)
    return jnp.concatenate([high, mid, low, high, mid, high], 0).astype(BF)


def edge_row(value, low_span):
    return jnp.where(low_span, value[7:8], value[0:1])


def first_column(value):
    return jnp.broadcast_to(value[:, 0:1], (8, 128))


def even_place():
    return lax.rem(lax.axis_index("wrap"), 2) == 0


def missing_term(value, beside):
    change = beside - value
    flux = (viscous + value) * change + (0.5 * (1.0 + coef_cb2)) * change * change
    return (0.5 * time_step / coef_sigma) * flux


def prep_kernel(
    xyz_hbm,
    size_hbm,
    nu_hbm,
    chunks_ref,
    pair_ref,
    beside_ref,
    xyz_ref,
    size_ref,
    nu_ref,
    sems,
):
    pairs = ((xyz_hbm, xyz_ref), (size_hbm, size_ref), (nu_hbm, nu_ref))
    copies = [pltpu.make_async_copy(*pair, sems.at[n]) for n, pair in enumerate(pairs)]
    for copy in copies:
        copy.start()
    for copy in copies:
        copy.wait()
    parts = []
    for block in range(size_ref.shape[1] // PBS):
        lanes = slice(block * PBS, (block + 1) * PBS)
        xyz = xyz_ref[:, lanes]
        size = size_ref[:, lanes]
        parts += [xyz, jnp.sum(xyz * xyz, axis=0, keepdims=True) + size * size]
    low_span = lax.axis_index("span") == 0
    rows = nu_ref.shape[0]
    lane = tile_iota(1)
    column = jnp.zeros((8, 128), F32)
    for row in range(rows):
        value = nu_ref[row]
        beside_ref[row : row + 1, :] = edge_row(value, low_span)
        column = jnp.where(lane == row, first_column(value), column)
    pair_ref[...] = jnp.where(even_place(), nu_ref[rows - 1], nu_ref[0])
    chunk = jnp.concatenate(parts + [column], 0)
    for n in range(chunks_ref.shape[0]):
        chunks_ref[n] = chunk


class Halo:
    def __init__(self, nu_ref, pair, after, beside_ref, column, padded_ref, ghost_ref):
        devices = lax.axis_size("wrap")
        place = lax.axis_index("wrap")
        rows = nu_ref.shape[0]
        self.rows = rows
        self.low_span = lax.axis_index("span") == 0
        self.padded, self.ghost, self.beside = padded_ref, ghost_ref, beside_ref
        lower = jnp.where(even_place(), after, pair)
        upper = jnp.where(even_place(), pair, after)
        padded_ref[0] = jnp.where(place == 0, nu_ref[0], lower)
        padded_ref[rows + 1] = jnp.where(place == devices - 1, nu_ref[rows - 1], upper)
        in_wake = (place < devices // 4) | (place >= devices - devices // 4)
        self.in_wake = in_wake
        for row in range(rows):
            value = nu_ref[row]
            padded_ref[row + 1] = value
            partner = jnp.broadcast_to(column[:, rows - 1 - row : rows - row], (8, 128))
            ghost_ref[row] = jnp.where(in_wake, partner, -value)

    def rate(self, row, squares, vorticity):
        value = self.padded[row + 1]
        sub, lane = tile_iota(0), tile_iota(1)
        across = jnp.broadcast_to(self.beside[pl.ds(row, 1), :], (8, 128))
        span_low = jnp.where(self.low_span, value, across)
        span_high = jnp.where(self.low_span, across, value)
        others = (
            self.padded[row],
            self.padded[row + 2],
            jnp.where(sub == 0, span_low, pltpu.roll(value, 1, 0)),
            jnp.where(sub == 7, span_high, pltpu.roll(value, 7, 0)),
            jnp.where(lane == 0, self.ghost[row], pltpu.roll(value, 1, 1)),
            jnp.where(lane == 127, value, pltpu.roll(value, 127, 1)),
        )
        sums = jnp.zeros_like(value)
        squared = jnp.zeros_like(value)
        for other in others:
            change = other - value
            sums = sums + change
            squared = squared + change * change
        flux = (viscous + value) * sums + (0.5 * (1.0 + coef_cb2)) * squared
        scaled = coef_kappa**2 * squares
        modified = vorticity + value / scaled
        ratio = value / (modified * scaled)
        ratio2 = ratio * ratio
        shaped = ratio + coef_cw2 * (ratio2 * ratio2 * ratio2 - ratio)
        shaped2 = shaped * shaped
        base = (1.0 + coef_cw3**6) / (shaped2 * shaped2 * shaped2 + coef_cw3**6)
        factor = shaped * jnp.exp(jnp.log(base) * (1.0 / 6.0))
        return (
            flux / coef_sigma
            + coef_cb1 * modified * value
            - coef_cw1 * factor * value * value / squares
        )


def build_table(halves, table_ref):
    place = lax.axis_index("wrap")
    own_blocks = table_ref.shape[0] // lax.axis_size("wrap")
    groups = lax.axis_size("wrap") >> GROUP_BIT
    low = place & ((1 << GROUP_BIT) - 1)

    def body(group, carry):
        for half, pieces in enumerate(halves):
            for ref, mask in zip(pieces, (0,) + Y_MASKS):
                base = ((group << GROUP_BIT) | (low ^ mask ^ half)) * own_blocks
                for pair in range(own_blocks // 2):
                    start = pl.multiple_of(group * own_blocks * 4 + pair * 8, 8)
                    rows = ref[pl.ds(start, 8), :]
                    table_ref[base + pair * 2] = panel_features(rows)
                    table_ref[base + pair * 2 + 1] = panel_features(pltpu.roll(rows, 4, 0))
        return carry

    lax.fori_loop(0, groups, body, 0)


def nearest_tile(tile, list_ref, cell_ref, table_ref):
    sub = tile_iota(0)
    unit = jnp.where(sub == 3, 1.0, 0.0)
    xyz = [cell_ref[component, tile] for component in range(3)]
    twice = [-2.0 * part for part in xyz]
    found = []
    for line in range(8):
        rows = unit
        for component in range(3):
            spread = jnp.broadcast_to(twice[component][line : line + 1], (8, 128))
            rows = jnp.where(sub == component, spread, rows)
        cells = cell_features(rows).T
        nearest = None
        for slot in range(0, 8, 2):
            first = list_ref[(tile * 8 + line) * 8 + slot]
            second = list_ref[(tile * 8 + line) * 8 + slot + 1]
            panels = jnp.concatenate([table_ref[first], table_ref[second]], 1)
            value = jnp.dot(cells, panels, preferred_element_type=F32)
            value = jnp.minimum(value[:, :128], value[:, 128:])
            nearest = value if nearest is None else jnp.minimum(nearest, value)
        turned = jnp.min(nearest.T.reshape(16, 8, 128), axis=0)
        found.append(jnp.min(turned, axis=0, keepdims=True))
    norm = xyz[0] * xyz[0] + xyz[1] * xyz[1] + xyz[2] * xyz[2]
    return jnp.concatenate(found, 0) + norm


def main_kernel(
    list_ref,
    own0_ref,
    own1_ref,
    own2_ref,
    own3_ref,
    other0_ref,
    other1_ref,
    other2_ref,
    other3_ref,
    cell_ref,
    nu_ref,
    vorticity_ref,
    beside_ref,
    dist_ref,
    squares_ref,
    middle_ref,
    pair_out,
    next_out,
    beside_out,
    column_out,
    table_ref,
    padded_ref,
    ghost_ref,
):
    total = own0_ref.shape[0]
    column = other2_ref[total : total + 8]
    pair = other0_ref[total : total + 8]
    tiles = nu_ref.shape[0]
    even = even_place()
    open_row = jnp.where(even, nu_ref[0], nu_ref[tiles - 1])
    halo = Halo(nu_ref, pair, open_row, beside_ref, column, padded_ref, ghost_ref)
    open_side = jnp.where(even, beside_ref[0:1], beside_ref[tiles - 1 : tiles])
    open_partner = jnp.where(even, column[:, tiles - 1 : tiles], column[:, 0:1])
    next_out[0:8] = open_row
    next_out[16:24] = jnp.broadcast_to(open_side, (8, 128))
    next_out[24:32] = jnp.broadcast_to(open_partner, (8, 128))
    own = (own0_ref, own1_ref, own2_ref, own3_ref)
    other = (other0_ref, other1_ref, other2_ref, other3_ref)
    build_table((own, other), table_ref)
    per_step = LINES_PER_STEP // 8

    def body(step, column):
        lane = tile_iota(1)
        for part in range(per_step):
            tile = step * per_step + part
            squares = nearest_tile(tile, list_ref, cell_ref, table_ref)
            squares_ref[tile] = squares
            dist_ref[tile] = jnp.sqrt(squares)
            rate = halo.rate(tile, squares, vorticity_ref[tile])
            middle = nu_ref[tile] + 0.5 * time_step * rate
            middle_ref[tile] = middle
            beside_out[pl.ds(tile, 1), :] = edge_row(middle, halo.low_span)
            column = jnp.where(lane == tile, first_column(middle), column)
        return column

    column = lax.fori_loop(0, tiles // per_step, body, jnp.zeros((8, 128), F32))
    for row in range(0, column_out.shape[0], 8):
        column_out[row : row + 8] = column
    beside_out[tiles:] = jnp.zeros((beside_out.shape[0] - tiles, 128), F32)
    first, last = middle_ref[0], middle_ref[tiles - 1]
    pair_out[...] = jnp.where(even, last, first)
    next_out[8:16] = jnp.where(even, first, last)


def last_kernel(
    middle_ref,
    nu_ref,
    squares_ref,
    vorticity_ref,
    pair_ref,
    mine_ref,
    theirs_ref,
    beside_ref,
    column_ref,
    out_ref,
    padded_ref,
    ghost_ref,
    side_ref,
):
    place = lax.axis_index("wrap")
    rows = nu_ref.shape[0]
    even = even_place()
    inner = (place > 0) & (place < lax.axis_size("wrap") - 1)
    value, partial, side, partner = (mine_ref[n : n + 8] for n in range(0, 32, 8))
    other, other_partial, other_side, other_partner = (theirs_ref[n : n + 8] for n in range(0, 32, 8))
    after = other_partial + missing_term(other, value)
    halo = Halo(
        middle_ref, pair_ref[...], after, beside_ref, column_ref[0:8], padded_ref, ghost_ref
    )
    side_ref[...] = beside_ref[0:rows]
    halo.beside = side_ref
    fixed = partial + missing_term(value, other)
    side_term = missing_term(side, other_side)[0:1]
    partner_term = missing_term(partner, other_partner)
    for row, here in ((0, inner & even), (rows - 1, inner & ~even)):
        own = jnp.where(here, fixed, padded_ref[row + 1])
        padded_ref[row + 1] = own
        ghost = ghost_ref[row] + jnp.where(here, partner_term, 0.0)
        ghost_ref[row] = jnp.where(halo.in_wake, ghost, -own)
        side_ref[row : row + 1] = side_ref[row : row + 1] + jnp.where(here, side_term, 0.0)
    for row in range(rows):
        rate = halo.rate(row, squares_ref[row], vorticity_ref[row])
        out_ref[row] = nu_ref[row] + time_step * rate


def swap_mask(block, mask):
    return lax.ppermute(block, "wrap", [(i, i ^ mask) for i in range(lax.axis_size("wrap"))])


def swap_next(block):
    devices = lax.axis_size("wrap")
    pairs = [(i, (i + 1) % devices) for i in range(1, devices, 2)]
    return lax.ppermute(block, "wrap", pairs + [(j, i) for i, j in pairs])


def swap_span(block):
    return lax.ppermute(block, "span", [(0, 1), (1, 0)])


def gather(chunks, pair, beside):
    devices = lax.axis_size("wrap")
    groups, rows, lanes = chunks.shape
    size = rows - 8
    members = [[low + (n << GROUP_BIT) for n in range(groups)] for low in range(devices // groups)]
    chunks = lax.all_to_all(chunks, "wrap", 0, 0, tiled=True, axis_index_groups=members)
    chunks, beside = lax.optimization_barrier((chunks, swap_span(beside)))
    shard = chunks[:, :size].reshape(groups * size, lanes)
    opposite = groups - 1 - (lax.axis_index("wrap") >> GROUP_BIT)
    column = lax.dynamic_slice(chunks, (opposite, size, 0), (1, 8, lanes))[0]
    own = [
        shard,
        swap_mask(shard, Y_MASKS[0]),
        swap_mask(jnp.concatenate([shard, column], 0), Y_MASKS[1]),
        swap_mask(shard, Y_MASKS[2]),
    ]
    other = [swap_mask(jnp.concatenate([shard, pair], 0), 1)]
    other += [swap_mask(piece, 1) for piece in own[1:]]
    return own, other, beside


def shards(cell_xyz, panel_xyz, panel_size, block_lists, nu_field, vorticity):
    devices = lax.axis_size("wrap")
    rows, span, cells = nu_field.shape
    own_blocks = panel_size.shape[0] // PBS
    tile = jax.ShapeDtypeStruct((span, cells), F32)
    field = jax.ShapeDtypeStruct(nu_field.shape, F32)
    side = jax.ShapeDtypeStruct((rows, cells), F32)
    opened = jax.ShapeDtypeStruct((32, cells), F32)
    edges = (
        tile,
        opened,
        jax.ShapeDtypeStruct((SIDE_ROWS, cells), F32),
        jax.ShapeDtypeStruct((COLUMN_ROWS, cells), F32),
    )
    scratch = [pltpu.VMEM((rows + 2, span, cells), F32), pltpu.VMEM(nu_field.shape, F32)]

    groups = devices >> GROUP_BIT
    inputs = (panel_xyz, panel_size[None], nu_field)
    chunks, pair, beside = pl.pallas_call(
        prep_kernel,
        out_shape=(jax.ShapeDtypeStruct((groups, 4 * own_blocks + 8, PBS), F32), tile, side),
        in_specs=[pl.BlockSpec(memory_space=pltpu.HBM)] * 3,
        out_specs=(VMEM,) * 3,
        scratch_shapes=[
            pltpu.VMEM(panel_xyz.shape, F32),
            pltpu.VMEM((1,) + panel_size.shape, F32),
            pltpu.VMEM(nu_field.shape, F32),
            pltpu.SemaphoreType.DMA((3,)),
        ],
        compiler_params=pltpu.CompilerParams(vmem_limit_bytes=4 * 2**20),
        name="prep",
    )(*(pltpu.with_memory_space_constraint(x, pltpu.HBM) for x in inputs))
    own, other, beside = gather(chunks, pair, beside)

    dist, squares, middle, pair, mine, sides, column = pl.pallas_call(
        main_kernel,
        out_shape=(field, field, field) + edges,
        in_specs=[SMEM] + [VMEM] * 12,
        out_specs=(VMEM,) * 7,
        scratch_shapes=[pltpu.VMEM((devices * own_blocks, FEATS, PBS), BF)] + scratch,
        compiler_params=pltpu.CompilerParams(vmem_limit_bytes=24 * 2**20),
        cost_estimate=pl.CostEstimate(
            flops=2 * 128 * rows * span * cells * block_lists.shape[2] * PBS,
            bytes_accessed=4 * 2**20,
            transcendentals=0,
        ),
        name="main",
    )(block_lists.reshape(-1), *own, *other, cell_xyz, nu_field, vorticity, beside)
    column = swap_mask(column, devices - 1)
    theirs = swap_next(mine)
    sides = swap_span(sides)
    pair = swap_mask(pair, 1)

    nu_next = pl.pallas_call(
        last_kernel,
        out_shape=field,
        in_specs=[VMEM] * 9,
        out_specs=VMEM,
        scratch_shapes=scratch + [pltpu.VMEM(side.shape, F32)],
        compiler_params=pltpu.CompilerParams(vmem_limit_bytes=8 * 2**20),
        name="last",
    )(middle, nu_field, squares, vorticity, pair, mine, theirs, sides, column)
    return (nu_next, dist)


def solution(mesh):
    in_specs = (
        P(None, "wrap", "span", None),
        P(None, "wrap"),
        P("wrap"),
        P("wrap", "span", None),
        P("wrap", "span", None),
        P("wrap", "span", None),
    )
    out_specs = (P("wrap", "span", None), P("wrap", "span", None))
    return jax.shard_map(shards, mesh=mesh, in_specs=in_specs, out_specs=out_specs, check_vma=False)
```

```python
import functools

import jax
import jax.numpy as jnp
from jax import lax
from jax.experimental import pallas as pl
from jax.experimental.pallas import tpu as pltpu
from jax.sharding import PartitionSpec as P

BF = jnp.bfloat16
F32 = jnp.float32
PBS = 128
FEATS = 48
LINES_PER_STEP = 128
NEXT_ROWS = 48
COLUMN_ROWS = 40
GROUP_BIT = 3
Y_MASKS = (2, 6, 4)

coef_cb1 = 0.1355
coef_cb2 = 0.622
coef_sigma = 2.0 / 3.0
coef_kappa = 0.41
coef_cw2 = 0.3
coef_cw3 = 2.0
viscous = 1.0
time_step = 0.03
coef_cw1 = coef_cb1 / coef_kappa**2 + (1.0 + coef_cb2) / coef_sigma

SMEM = pl.BlockSpec(memory_space=pltpu.SMEM)
VMEM = pl.BlockSpec(memory_space=pltpu.VMEM)


def tile_iota(dim):
    return lax.broadcasted_iota(jnp.int32, (8, 128), dim)


def split_rows(rows):
    high = rows.astype(BF).astype(F32)
    rest = rows - high
    mid = rest.astype(BF).astype(F32)
    return high, mid, rest - mid


def panel_features(rows):
    high, mid, low = split_rows(rows)
    return jnp.concatenate([high, high, high, mid, mid, low], 0).astype(BF)


def cell_features(rows):
    high, mid, low = split_rows(rows)
    return jnp.concatenate([high, mid, low, high, mid, high], 0).astype(BF)


def edge_row(value, low_span):
    return jnp.where(low_span, value[7:8], value[0:1])


def first_column(value):
    return jnp.broadcast_to(value[:, 0:1], (8, 128))


def even_place():
    return lax.rem(lax.axis_index("wrap"), 2) == 0


def missing_term(value, beside):
    change = beside - value
    flux = (viscous + value) * change + (0.5 * (1.0 + coef_cb2)) * change * change
    return (0.5 * time_step / coef_sigma) * flux


def prep_kernel(
    xyz_hbm,
    size_hbm,
    nu_hbm,
    chunks_ref,
    pair_ref,
    beside_ref,
    xyz_ref,
    size_ref,
    nu_ref,
    sems,
):
    pairs = ((xyz_hbm, xyz_ref), (size_hbm, size_ref), (nu_hbm, nu_ref))
    copies = [pltpu.make_async_copy(*pair, sems.at[n]) for n, pair in enumerate(pairs)]
    for copy in copies:
        copy.start()
    for copy in copies:
        copy.wait()
    parts = []
    for block in range(size_ref.shape[1] // PBS):
        lanes = slice(block * PBS, (block + 1) * PBS)
        xyz = xyz_ref[:, lanes]
        size = size_ref[:, lanes]
        parts += [xyz, jnp.sum(xyz * xyz, axis=0, keepdims=True) + size * size]
    low_span = lax.axis_index("span") == 0
    rows = nu_ref.shape[0]
    lane = tile_iota(1)
    column = jnp.zeros((8, 128), F32)
    for row in range(rows):
        value = nu_ref[row]
        beside_ref[row : row + 1, :] = edge_row(value, low_span)
        column = jnp.where(lane == row, first_column(value), column)
    pair_ref[...] = jnp.where(even_place(), nu_ref[rows - 1], nu_ref[0])
    chunk = jnp.concatenate(parts + [column], 0)
    for n in range(chunks_ref.shape[0]):
        chunks_ref[n] = chunk


class Halo:
    def __init__(self, nu_ref, pair, after, beside_ref, column, padded_ref, ghost_ref):
        devices = lax.axis_size("wrap")
        place = lax.axis_index("wrap")
        rows = nu_ref.shape[0]
        self.rows = rows
        self.low_span = lax.axis_index("span") == 0
        self.padded, self.ghost, self.beside = padded_ref, ghost_ref, beside_ref
        lower = jnp.where(even_place(), after, pair)
        upper = jnp.where(even_place(), pair, after)
        padded_ref[0] = jnp.where(place == 0, nu_ref[0], lower)
        padded_ref[rows + 1] = jnp.where(place == devices - 1, nu_ref[rows - 1], upper)
        in_wake = (place < devices // 4) | (place >= devices - devices // 4)
        self.in_wake = in_wake
        for row in range(rows):
            value = nu_ref[row]
            padded_ref[row + 1] = value
            partner = jnp.broadcast_to(column[:, rows - 1 - row : rows - row], (8, 128))
            ghost_ref[row] = jnp.where(in_wake, partner, -value)

    def rate(self, row, squares, vorticity):
        value = self.padded[row + 1]
        sub, lane = tile_iota(0), tile_iota(1)
        across = jnp.broadcast_to(self.beside[pl.ds(row, 1), :], (8, 128))
        span_low = jnp.where(self.low_span, value, across)
        span_high = jnp.where(self.low_span, across, value)
        others = (
            self.padded[row],
            self.padded[row + 2],
            jnp.where(sub == 0, span_low, pltpu.roll(value, 1, 0)),
            jnp.where(sub == 7, span_high, pltpu.roll(value, 7, 0)),
            jnp.where(lane == 0, self.ghost[row], pltpu.roll(value, 1, 1)),
            jnp.where(lane == 127, value, pltpu.roll(value, 127, 1)),
        )
        sums = jnp.zeros_like(value)
        squared = jnp.zeros_like(value)
        for other in others:
            change = other - value
            sums = sums + change
            squared = squared + change * change
        flux = (viscous + value) * sums + (0.5 * (1.0 + coef_cb2)) * squared
        scaled = coef_kappa**2 * squares
        modified = vorticity + value / scaled
        ratio = value / (modified * scaled)
        ratio2 = ratio * ratio
        shaped = ratio + coef_cw2 * (ratio2 * ratio2 * ratio2 - ratio)
        shaped2 = shaped * shaped
        base = (1.0 + coef_cw3**6) / (shaped2 * shaped2 * shaped2 + coef_cw3**6)
        factor = shaped * jnp.exp(jnp.log(base) * (1.0 / 6.0))
        return (
            flux / coef_sigma
            + coef_cb1 * modified * value
            - coef_cw1 * factor * value * value / squares
        )


def build_table(halves, table_ref):
    place = lax.axis_index("wrap")
    own_blocks = table_ref.shape[0] // lax.axis_size("wrap")
    groups = lax.axis_size("wrap") >> GROUP_BIT
    low = place & ((1 << GROUP_BIT) - 1)

    def body(group, carry):
        for half, pieces in enumerate(halves):
            for ref, mask in zip(pieces, (0,) + Y_MASKS):
                base = ((group << GROUP_BIT) | (low ^ mask ^ half)) * own_blocks
                for pair in range(own_blocks // 2):
                    start = pl.multiple_of(group * own_blocks * 4 + pair * 8, 8)
                    rows = ref[pl.ds(start, 8), :]
                    table_ref[base + pair * 2] = panel_features(rows)
                    table_ref[base + pair * 2 + 1] = panel_features(pltpu.roll(rows, 4, 0))
        return carry

    lax.fori_loop(0, groups, body, 0)


def nearest_tile(tile, list_ref, cell_ref, table_ref):
    sub = tile_iota(0)
    unit = jnp.where(sub == 3, 1.0, 0.0)
    xyz = [cell_ref[component, tile] for component in range(3)]
    twice = [-2.0 * part for part in xyz]
    found = []
    for line in range(8):
        rows = unit
        for component in range(3):
            spread = jnp.broadcast_to(twice[component][line : line + 1], (8, 128))
            rows = jnp.where(sub == component, spread, rows)
        cells = cell_features(rows).T
        nearest = None
        for slot in range(0, 8, 2):
            first = list_ref[(tile * 8 + line) * 8 + slot]
            second = list_ref[(tile * 8 + line) * 8 + slot + 1]
            panels = jnp.concatenate([table_ref[first], table_ref[second]], 1)
            value = jnp.dot(cells, panels, preferred_element_type=F32)
            value = jnp.minimum(value[:, :128], value[:, 128:])
            nearest = value if nearest is None else jnp.minimum(nearest, value)
        turned = jnp.min(nearest.T.reshape(16, 8, 128), axis=0)
        found.append(jnp.min(turned, axis=0, keepdims=True))
    norm = xyz[0] * xyz[0] + xyz[1] * xyz[1] + xyz[2] * xyz[2]
    return jnp.concatenate(found, 0) + norm


def main_kernel(
    list_ref,
    own0_ref,
    own1_ref,
    own2_ref,
    own3_ref,
    other0_ref,
    other1_ref,
    other2_ref,
    other3_ref,
    cell_ref,
    nu_ref,
    vorticity_ref,
    beside_ref,
    dist_ref,
    squares_ref,
    middle_ref,
    pair_out,
    next_out,
    beside_out,
    column_out,
    table_ref,
    padded_ref,
    ghost_ref,
):
    total = own0_ref.shape[0]
    column = other2_ref[total : total + 8]
    pair = other0_ref[total : total + 8]
    tiles = nu_ref.shape[0]
    even = even_place()
    open_row = jnp.where(even, nu_ref[0], nu_ref[tiles - 1])
    halo = Halo(nu_ref, pair, open_row, beside_ref, column, padded_ref, ghost_ref)
    open_side = jnp.where(even, beside_ref[0:1], beside_ref[tiles - 1 : tiles])
    open_partner = jnp.where(even, column[:, tiles - 1 : tiles], column[:, 0:1])
    next_out[0:8] = open_row
    next_out[16:24] = jnp.broadcast_to(open_side, (8, 128))
    next_out[24:32] = jnp.broadcast_to(open_partner, (8, 128))
    next_out[32:] = jnp.zeros((next_out.shape[0] - 32, 128), F32)
    own = (own0_ref, own1_ref, own2_ref, own3_ref)
    other = (other0_ref, other1_ref, other2_ref, other3_ref)
    build_table((own, other), table_ref)
    per_step = LINES_PER_STEP // 8

    def body(step, column):
        lane = tile_iota(1)
        for part in range(per_step):
            tile = step * per_step + part
            squares = nearest_tile(tile, list_ref, cell_ref, table_ref)
            squares_ref[tile] = squares
            dist_ref[tile] = jnp.sqrt(squares)
            rate = halo.rate(tile, squares, vorticity_ref[tile])
            middle = nu_ref[tile] + 0.5 * time_step * rate
            middle_ref[tile] = middle
            beside_out[pl.ds(tile, 1), :] = edge_row(middle, halo.low_span)
            column = jnp.where(lane == tile, first_column(middle), column)
        return column

    column = lax.fori_loop(0, tiles // per_step, body, jnp.zeros((8, 128), F32))
    for row in range(0, column_out.shape[0], 8):
        column_out[row : row + 8] = column
    first, last = middle_ref[0], middle_ref[tiles - 1]
    pair_out[...] = jnp.where(even, last, first)
    next_out[8:16] = jnp.where(even, first, last)


def last_kernel(
    middle_ref,
    nu_ref,
    squares_ref,
    vorticity_ref,
    pair_ref,
    mine_ref,
    theirs_ref,
    beside_ref,
    column_ref,
    out_ref,
    padded_ref,
    ghost_ref,
    side_ref,
):
    place = lax.axis_index("wrap")
    rows = nu_ref.shape[0]
    even = even_place()
    inner = (place > 0) & (place < lax.axis_size("wrap") - 1)
    value, partial, side, partner = (mine_ref[n : n + 8] for n in range(0, 32, 8))
    other, other_partial, other_side, other_partner = (theirs_ref[n : n + 8] for n in range(0, 32, 8))
    after = other_partial + missing_term(other, value)
    halo = Halo(
        middle_ref, pair_ref[...], after, beside_ref, column_ref[0:8], padded_ref, ghost_ref
    )
    side_ref[...] = beside_ref[...]
    halo.beside = side_ref
    fixed = partial + missing_term(value, other)
    side_term = missing_term(side, other_side)[0:1]
    partner_term = missing_term(partner, other_partner)
    for row, here in ((0, inner & even), (rows - 1, inner & ~even)):
        own = jnp.where(here, fixed, padded_ref[row + 1])
        padded_ref[row + 1] = own
        ghost = ghost_ref[row] + jnp.where(here, partner_term, 0.0)
        ghost_ref[row] = jnp.where(halo.in_wake, ghost, -own)
        side_ref[row : row + 1] = side_ref[row : row + 1] + jnp.where(here, side_term, 0.0)
    for row in range(rows):
        rate = halo.rate(row, squares_ref[row], vorticity_ref[row])
        out_ref[row] = nu_ref[row] + time_step * rate


def swap_mask(block, mask):
    return lax.ppermute(block, "wrap", [(i, i ^ mask) for i in range(lax.axis_size("wrap"))])


def swap_next(block):
    devices = lax.axis_size("wrap")
    pairs = [(i, i + 1) for i in range(1, devices - 1, 2)]
    pairs += [(j, i) for i, j in pairs] + [(0, 0), (devices - 1, devices - 1)]
    return lax.ppermute(block, "wrap", pairs)


def swap_span(block):
    return lax.ppermute(block, "span", [(0, 1), (1, 0)])


def gather(chunks, pair, beside):
    devices = lax.axis_size("wrap")
    groups, rows, lanes = chunks.shape
    size = rows - 8
    members = [[low + (n << GROUP_BIT) for n in range(groups)] for low in range(devices // groups)]
    chunks = lax.all_to_all(chunks, "wrap", 0, 0, tiled=True, axis_index_groups=members)
    chunks, beside = lax.optimization_barrier((chunks, swap_span(beside)))
    shard = chunks[:, :size].reshape(groups * size, lanes)
    opposite = groups - 1 - (lax.axis_index("wrap") >> GROUP_BIT)
    column = lax.dynamic_slice(chunks, (opposite, size, 0), (1, 8, lanes))[0]
    own = [
        shard,
        swap_mask(shard, Y_MASKS[0]),
        swap_mask(jnp.concatenate([shard, column], 0), Y_MASKS[1]),
        swap_mask(jnp.concatenate([shard, column, column], 0), Y_MASKS[2]),
    ]
    other = [swap_mask(jnp.concatenate([shard, pair], 0), 1)]
    other += [swap_mask(piece, 1) for piece in own[1:]]
    return own, other, beside


def shards(cell_xyz, panel_xyz, panel_size, block_lists, nu_field, vorticity):
    devices = lax.axis_size("wrap")
    rows, span, cells = nu_field.shape
    own_blocks = panel_size.shape[0] // PBS
    tile = jax.ShapeDtypeStruct((span, cells), F32)
    field = jax.ShapeDtypeStruct(nu_field.shape, F32)
    side = jax.ShapeDtypeStruct((rows, cells), F32)
    opened = jax.ShapeDtypeStruct((NEXT_ROWS, cells), F32)
    edges = (
        tile,
        opened,
        side,
        jax.ShapeDtypeStruct((COLUMN_ROWS, cells), F32),
    )
    scratch = [pltpu.VMEM((rows + 2, span, cells), F32), pltpu.VMEM(nu_field.shape, F32)]

    groups = devices >> GROUP_BIT
    inputs = (panel_xyz, panel_size[None], nu_field)
    chunks, pair, beside = pl.pallas_call(
        prep_kernel,
        out_shape=(jax.ShapeDtypeStruct((groups, 4 * own_blocks + 8, PBS), F32), tile, side),
        in_specs=[pl.BlockSpec(memory_space=pltpu.HBM)] * 3,
        out_specs=(VMEM,) * 3,
        scratch_shapes=[
            pltpu.VMEM(panel_xyz.shape, F32),
            pltpu.VMEM((1,) + panel_size.shape, F32),
            pltpu.VMEM(nu_field.shape, F32),
            pltpu.SemaphoreType.DMA((3,)),
        ],
        compiler_params=pltpu.CompilerParams(vmem_limit_bytes=4 * 2**20),
        name="prep",
    )(*(pltpu.with_memory_space_constraint(x, pltpu.HBM) for x in inputs))
    own, other, beside = gather(chunks, pair, beside)

    dist, squares, middle, pair, mine, sides, column = pl.pallas_call(
        main_kernel,
        out_shape=(field, field, field) + edges,
        in_specs=[SMEM] + [VMEM] * 12,
        out_specs=(VMEM,) * 7,
        scratch_shapes=[pltpu.VMEM((devices * own_blocks, FEATS, PBS), BF)] + scratch,
        compiler_params=pltpu.CompilerParams(vmem_limit_bytes=24 * 2**20),
        cost_estimate=pl.CostEstimate(
            flops=2 * 128 * rows * span * cells * block_lists.shape[2] * PBS,
            bytes_accessed=4 * 2**20,
            transcendentals=0,
        ),
        name="main",
    )(block_lists.reshape(-1), *own, *other, cell_xyz, nu_field, vorticity, beside)
    column = swap_mask(column, devices - 1)
    theirs = swap_next(mine)
    sides = swap_span(sides)
    pair = swap_mask(pair, 1)

    nu_next = pl.pallas_call(
        last_kernel,
        out_shape=field,
        in_specs=[VMEM] * 9,
        out_specs=VMEM,
        scratch_shapes=scratch + [pltpu.VMEM(side.shape, F32)],
        compiler_params=pltpu.CompilerParams(vmem_limit_bytes=8 * 2**20),
        name="last",
    )(middle, nu_field, squares, vorticity, pair, mine, theirs, sides, column)
    return (nu_next, dist)


def solution(mesh):
    in_specs = (
        P(None, "wrap", "span", None),
        P(None, "wrap"),
        P("wrap"),
        P("wrap", "span", None),
        P("wrap", "span", None),
        P("wrap", "span", None),
    )
    out_specs = (P("wrap", "span", None), P("wrap", "span", None))
    return jax.shard_map(shards, mesh=mesh, in_specs=in_specs, out_specs=out_specs, check_vma=False)
```

```python
import functools

import jax
import jax.numpy as jnp
from jax import lax
from jax.experimental import pallas as pl
from jax.experimental.pallas import tpu as pltpu
from jax.sharding import PartitionSpec as P

BF = jnp.bfloat16
F32 = jnp.float32
PBS = 128
FEATS = 48
LINES_PER_STEP = 128
COLUMN_ROWS = 48
SIDE_ROWS = 40
GROUP_BIT = 3
Y_MASKS = (2, 6, 4)

coef_cb1 = 0.1355
coef_cb2 = 0.622
coef_sigma = 2.0 / 3.0
coef_kappa = 0.41
coef_cw2 = 0.3
coef_cw3 = 2.0
viscous = 1.0
time_step = 0.03
coef_cw1 = coef_cb1 / coef_kappa**2 + (1.0 + coef_cb2) / coef_sigma

SMEM = pl.BlockSpec(memory_space=pltpu.SMEM)
VMEM = pl.BlockSpec(memory_space=pltpu.VMEM)


def tile_iota(dim):
    return lax.broadcasted_iota(jnp.int32, (8, 128), dim)


def split_rows(rows):
    high = rows.astype(BF).astype(F32)
    rest = rows - high
    mid = rest.astype(BF).astype(F32)
    return high, mid, rest - mid


def panel_features(rows):
    high, mid, low = split_rows(rows)
    return jnp.concatenate([high, high, high, mid, mid, low], 0).astype(BF)


def cell_features(rows):
    high, mid, low = split_rows(rows)
    return jnp.concatenate([high, mid, low, high, mid, high], 0).astype(BF)


def edge_row(value, low_span):
    return jnp.where(low_span, value[7:8], value[0:1])


def first_column(value):
    return jnp.broadcast_to(value[:, 0:1], (8, 128))


def even_place():
    return lax.rem(lax.axis_index("wrap"), 2) == 0


def missing_term(value, beside):
    change = beside - value
    flux = (viscous + value) * change + (0.5 * (1.0 + coef_cb2)) * change * change
    return (0.5 * time_step / coef_sigma) * flux


def prep_kernel(
    xyz_hbm,
    size_hbm,
    nu_hbm,
    chunks_ref,
    pair_ref,
    beside_ref,
    xyz_ref,
    size_ref,
    nu_ref,
    sems,
):
    pairs = ((xyz_hbm, xyz_ref), (size_hbm, size_ref), (nu_hbm, nu_ref))
    copies = [pltpu.make_async_copy(*pair, sems.at[n]) for n, pair in enumerate(pairs)]
    for copy in copies:
        copy.start()
    for copy in copies:
        copy.wait()
    parts = []
    for block in range(size_ref.shape[1] // PBS):
        lanes = slice(block * PBS, (block + 1) * PBS)
        xyz = xyz_ref[:, lanes]
        size = size_ref[:, lanes]
        parts += [xyz, jnp.sum(xyz * xyz, axis=0, keepdims=True) + size * size]
    low_span = lax.axis_index("span") == 0
    rows = nu_ref.shape[0]
    lane = tile_iota(1)
    column = jnp.zeros((8, 128), F32)
    for row in range(rows):
        value = nu_ref[row]
        beside_ref[row : row + 1, :] = edge_row(value, low_span)
        column = jnp.where(lane == row, first_column(value), column)
    pair_ref[...] = jnp.where(even_place(), nu_ref[rows - 1], nu_ref[0])
    chunk = jnp.concatenate(parts + [column], 0)
    for n in range(chunks_ref.shape[0]):
        chunks_ref[n] = chunk


class Halo:
    def __init__(self, nu_ref, pair, after, beside_ref, column, padded_ref, ghost_ref):
        devices = lax.axis_size("wrap")
        place = lax.axis_index("wrap")
        rows = nu_ref.shape[0]
        self.rows = rows
        self.low_span = lax.axis_index("span") == 0
        self.padded, self.ghost, self.beside = padded_ref, ghost_ref, beside_ref
        lower = jnp.where(even_place(), after, pair)
        upper = jnp.where(even_place(), pair, after)
        padded_ref[0] = jnp.where(place == 0, nu_ref[0], lower)
        padded_ref[rows + 1] = jnp.where(place == devices - 1, nu_ref[rows - 1], upper)
        in_wake = (place < devices // 4) | (place >= devices - devices // 4)
        self.in_wake = in_wake
        for row in range(rows):
            value = nu_ref[row]
            padded_ref[row + 1] = value
            partner = jnp.broadcast_to(column[:, rows - 1 - row : rows - row], (8, 128))
            ghost_ref[row] = jnp.where(in_wake, partner, -value)

    def rate(self, row, squares, vorticity):
        value = self.padded[row + 1]
        sub, lane = tile_iota(0), tile_iota(1)
        across = jnp.broadcast_to(self.beside[pl.ds(row, 1), :], (8, 128))
        span_low = jnp.where(self.low_span, value, across)
        span_high = jnp.where(self.low_span, across, value)
        others = (
            self.padded[row],
            self.padded[row + 2],
            jnp.where(sub == 0, span_low, pltpu.roll(value, 1, 0)),
            jnp.where(sub == 7, span_high, pltpu.roll(value, 7, 0)),
            jnp.where(lane == 0, self.ghost[row], pltpu.roll(value, 1, 1)),
            jnp.where(lane == 127, value, pltpu.roll(value, 127, 1)),
        )
        sums = jnp.zeros_like(value)
        squared = jnp.zeros_like(value)
        for other in others:
            change = other - value
            sums = sums + change
            squared = squared + change * change
        flux = (viscous + value) * sums + (0.5 * (1.0 + coef_cb2)) * squared
        scaled = coef_kappa**2 * squares
        modified = vorticity + value / scaled
        ratio = value / (modified * scaled)
        ratio2 = ratio * ratio
        shaped = ratio + coef_cw2 * (ratio2 * ratio2 * ratio2 - ratio)
        shaped2 = shaped * shaped
        base = (1.0 + coef_cw3**6) / (shaped2 * shaped2 * shaped2 + coef_cw3**6)
        factor = shaped * jnp.exp(jnp.log(base) * (1.0 / 6.0))
        return (
            flux / coef_sigma
            + coef_cb1 * modified * value
            - coef_cw1 * factor * value * value / squares
        )


def build_table(halves, table_ref):
    place = lax.axis_index("wrap")
    own_blocks = table_ref.shape[0] // lax.axis_size("wrap")
    groups = lax.axis_size("wrap") >> GROUP_BIT
    low = place & ((1 << GROUP_BIT) - 1)

    def body(group, carry):
        for half, pieces in enumerate(halves):
            for ref, mask in zip(pieces, (0,) + Y_MASKS):
                base = ((group << GROUP_BIT) | (low ^ mask ^ half)) * own_blocks
                for pair in range(own_blocks // 2):
                    start = pl.multiple_of(group * own_blocks * 4 + pair * 8, 8)
                    rows = ref[pl.ds(start, 8), :]
                    table_ref[base + pair * 2] = panel_features(rows)
                    table_ref[base + pair * 2 + 1] = panel_features(pltpu.roll(rows, 4, 0))
        return carry

    lax.fori_loop(0, groups, body, 0)


def nearest_tile(tile, list_ref, cell_ref, table_ref):
    sub = tile_iota(0)
    unit = jnp.where(sub == 3, 1.0, 0.0)
    xyz = [cell_ref[component, tile] for component in range(3)]
    twice = [-2.0 * part for part in xyz]
    found = []
    for line in range(8):
        rows = unit
        for component in range(3):
            spread = jnp.broadcast_to(twice[component][line : line + 1], (8, 128))
            rows = jnp.where(sub == component, spread, rows)
        cells = cell_features(rows).T
        nearest = None
        for slot in range(0, 8, 2):
            first = list_ref[(tile * 8 + line) * 8 + slot]
            second = list_ref[(tile * 8 + line) * 8 + slot + 1]
            panels = jnp.concatenate([table_ref[first], table_ref[second]], 1)
            value = jnp.dot(cells, panels, preferred_element_type=F32)
            value = jnp.minimum(value[:, :128], value[:, 128:])
            nearest = value if nearest is None else jnp.minimum(nearest, value)
        turned = jnp.min(nearest.T.reshape(16, 8, 128), axis=0)
        found.append(jnp.min(turned, axis=0, keepdims=True))
    norm = xyz[0] * xyz[0] + xyz[1] * xyz[1] + xyz[2] * xyz[2]
    return jnp.concatenate(found, 0) + norm


def main_kernel(
    list_ref,
    own0_ref,
    own1_ref,
    own2_ref,
    own3_ref,
    other0_ref,
    other1_ref,
    other2_ref,
    other3_ref,
    cell_ref,
    nu_ref,
    vorticity_ref,
    beside_ref,
    dist_ref,
    squares_ref,
    middle_ref,
    pair_out,
    next_out,
    beside_out,
    column_out,
    table_ref,
    padded_ref,
    ghost_ref,
):
    total = own0_ref.shape[0]
    column = other2_ref[total : total + 8]
    pair = other0_ref[total : total + 8]
    tiles = nu_ref.shape[0]
    even = even_place()
    open_row = jnp.where(even, nu_ref[0], nu_ref[tiles - 1])
    halo = Halo(nu_ref, pair, open_row, beside_ref, column, padded_ref, ghost_ref)
    open_side = jnp.where(even, beside_ref[0:1], beside_ref[tiles - 1 : tiles])
    open_partner = jnp.where(even, column[:, tiles - 1 : tiles], column[:, 0:1])
    next_out[0:8] = open_row
    next_out[16:24] = jnp.broadcast_to(open_side, (8, 128))
    next_out[24:32] = jnp.broadcast_to(open_partner, (8, 128))
    own = (own0_ref, own1_ref, own2_ref, own3_ref)
    other = (other0_ref, other1_ref, other2_ref, other3_ref)
    build_table((own, other), table_ref)
    per_step = LINES_PER_STEP // 8

    def body(step, column):
        lane = tile_iota(1)
        for part in range(per_step):
            tile = step * per_step + part
            squares = nearest_tile(tile, list_ref, cell_ref, table_ref)
            squares_ref[tile] = squares
            dist_ref[tile] = jnp.sqrt(squares)
            rate = halo.rate(tile, squares, vorticity_ref[tile])
            middle = nu_ref[tile] + 0.5 * time_step * rate
            middle_ref[tile] = middle
            beside_out[pl.ds(tile, 1), :] = edge_row(middle, halo.low_span)
            column = jnp.where(lane == tile, first_column(middle), column)
        return column

    column = lax.fori_loop(0, tiles // per_step, body, jnp.zeros((8, 128), F32))
    for row in range(0, column_out.shape[0], 8):
        column_out[row : row + 8] = column
    beside_out[tiles:] = jnp.zeros((beside_out.shape[0] - tiles, 128), F32)
    first, last = middle_ref[0], middle_ref[tiles - 1]
    pair_out[...] = jnp.where(even, last, first)
    next_out[8:16] = jnp.where(even, first, last)


def last_kernel(
    middle_ref,
    nu_ref,
    squares_ref,
    vorticity_ref,
    pair_ref,
    mine_ref,
    theirs_ref,
    beside_ref,
    column_ref,
    out_ref,
    padded_ref,
    ghost_ref,
    side_ref,
):
    place = lax.axis_index("wrap")
    rows = nu_ref.shape[0]
    even = even_place()
    inner = (place > 0) & (place < lax.axis_size("wrap") - 1)
    value, partial, side, partner = (mine_ref[n : n + 8] for n in range(0, 32, 8))
    other, other_partial, other_side, other_partner = (theirs_ref[n : n + 8] for n in range(0, 32, 8))
    after = other_partial + missing_term(other, value)
    halo = Halo(
        middle_ref, pair_ref[...], after, beside_ref, column_ref[0:8], padded_ref, ghost_ref
    )
    side_ref[...] = beside_ref[0:rows]
    halo.beside = side_ref
    fixed = partial + missing_term(value, other)
    side_term = missing_term(side, other_side)[0:1]
    partner_term = missing_term(partner, other_partner)
    for row, here in ((0, inner & even), (rows - 1, inner & ~even)):
        own = jnp.where(here, fixed, padded_ref[row + 1])
        padded_ref[row + 1] = own
        ghost = ghost_ref[row] + jnp.where(here, partner_term, 0.0)
        ghost_ref[row] = jnp.where(halo.in_wake, ghost, -own)
        side_ref[row : row + 1] = side_ref[row : row + 1] + jnp.where(here, side_term, 0.0)
    for row in range(rows):
        rate = halo.rate(row, squares_ref[row], vorticity_ref[row])
        out_ref[row] = nu_ref[row] + time_step * rate


def swap_mask(block, mask):
    return lax.ppermute(block, "wrap", [(i, i ^ mask) for i in range(lax.axis_size("wrap"))])


def swap_next(block):
    devices = lax.axis_size("wrap")
    pairs = [(i, (i + 1) % devices) for i in range(1, devices, 2)]
    return lax.ppermute(block, "wrap", pairs + [(j, i) for i, j in pairs])


def swap_span(block):
    return lax.ppermute(block, "span", [(0, 1), (1, 0)])


def gather(chunks, pair, beside):
    devices = lax.axis_size("wrap")
    groups, rows, lanes = chunks.shape
    size = rows - 8
    members = [[low + (n << GROUP_BIT) for n in range(groups)] for low in range(devices // groups)]
    chunks = lax.all_to_all(chunks, "wrap", 0, 0, tiled=True, axis_index_groups=members)
    chunks, beside = lax.optimization_barrier((chunks, swap_span(beside)))
    shard = chunks[:, :size].reshape(groups * size, lanes)
    opposite = groups - 1 - (lax.axis_index("wrap") >> GROUP_BIT)
    column = lax.dynamic_slice(chunks, (opposite, size, 0), (1, 8, lanes))[0]
    own = [
        shard,
        swap_mask(shard, Y_MASKS[0]),
        swap_mask(jnp.concatenate([shard, column], 0), Y_MASKS[1]),
        swap_mask(jnp.concatenate([shard, column, column], 0), Y_MASKS[2]),
    ]
    other = [swap_mask(jnp.concatenate([shard, pair], 0), 1)]
    other += [swap_mask(piece, 1) for piece in own[1:]]
    return own, other, beside


def shards(cell_xyz, panel_xyz, panel_size, block_lists, nu_field, vorticity):
    devices = lax.axis_size("wrap")
    rows, span, cells = nu_field.shape
    own_blocks = panel_size.shape[0] // PBS
    tile = jax.ShapeDtypeStruct((span, cells), F32)
    field = jax.ShapeDtypeStruct(nu_field.shape, F32)
    side = jax.ShapeDtypeStruct((rows, cells), F32)
    opened = jax.ShapeDtypeStruct((32, cells), F32)
    edges = (
        tile,
        opened,
        jax.ShapeDtypeStruct((SIDE_ROWS, cells), F32),
        jax.ShapeDtypeStruct((COLUMN_ROWS, cells), F32),
    )
    scratch = [pltpu.VMEM((rows + 2, span, cells), F32), pltpu.VMEM(nu_field.shape, F32)]

    groups = devices >> GROUP_BIT
    inputs = (panel_xyz, panel_size[None], nu_field)
    chunks, pair, beside = pl.pallas_call(
        prep_kernel,
        out_shape=(jax.ShapeDtypeStruct((groups, 4 * own_blocks + 8, PBS), F32), tile, side),
        in_specs=[pl.BlockSpec(memory_space=pltpu.HBM)] * 3,
        out_specs=(VMEM,) * 3,
        scratch_shapes=[
            pltpu.VMEM(panel_xyz.shape, F32),
            pltpu.VMEM((1,) + panel_size.shape, F32),
            pltpu.VMEM(nu_field.shape, F32),
            pltpu.SemaphoreType.DMA((3,)),
        ],
        compiler_params=pltpu.CompilerParams(vmem_limit_bytes=4 * 2**20),
        name="prep",
    )(*(pltpu.with_memory_space_constraint(x, pltpu.HBM) for x in inputs))
    own, other, beside = gather(chunks, pair, beside)

    dist, squares, middle, pair, mine, sides, column = pl.pallas_call(
        main_kernel,
        out_shape=(field, field, field) + edges,
        in_specs=[SMEM] + [VMEM] * 12,
        out_specs=(VMEM,) * 7,
        scratch_shapes=[pltpu.VMEM((devices * own_blocks, FEATS, PBS), BF)] + scratch,
        compiler_params=pltpu.CompilerParams(vmem_limit_bytes=24 * 2**20),
        cost_estimate=pl.CostEstimate(
            flops=2 * 128 * rows * span * cells * block_lists.shape[2] * PBS,
            bytes_accessed=4 * 2**20,
            transcendentals=0,
        ),
        name="main",
    )(block_lists.reshape(-1), *own, *other, cell_xyz, nu_field, vorticity, beside)
    column = swap_mask(column, devices - 1)
    theirs = swap_next(mine)
    sides = swap_span(sides)
    pair = swap_mask(pair, 1)

    nu_next = pl.pallas_call(
        last_kernel,
        out_shape=field,
        in_specs=[VMEM] * 9,
        out_specs=VMEM,
        scratch_shapes=scratch + [pltpu.VMEM(side.shape, F32)],
        compiler_params=pltpu.CompilerParams(vmem_limit_bytes=8 * 2**20),
        name="last",
    )(middle, nu_field, squares, vorticity, pair, mine, theirs, sides, column)
    return (nu_next, dist)


def solution(mesh):
    in_specs = (
        P(None, "wrap", "span", None),
        P(None, "wrap"),
        P("wrap"),
        P("wrap", "span", None),
        P("wrap", "span", None),
        P("wrap", "span", None),
    )
    out_specs = (P("wrap", "span", None), P("wrap", "span", None))
    return jax.shard_map(shards, mesh=mesh, in_specs=in_specs, out_specs=out_specs, check_vma=False)
```

```python
import functools

import jax
import jax.numpy as jnp
from jax import lax
from jax.experimental import pallas as pl
from jax.experimental.pallas import tpu as pltpu
from jax.sharding import PartitionSpec as P

BF = jnp.bfloat16
F32 = jnp.float32
PBS = 128
FEATS = 48
LINES_PER_STEP = 128
COLUMN_ROWS = 48
SIDE_ROWS = 40
GROUP_BIT = 3
Y_MASKS = (2, 6, 4)

coef_cb1 = 0.1355
coef_cb2 = 0.622
coef_sigma = 2.0 / 3.0
coef_kappa = 0.41
coef_cw2 = 0.3
coef_cw3 = 2.0
viscous = 1.0
time_step = 0.03
coef_cw1 = coef_cb1 / coef_kappa**2 + (1.0 + coef_cb2) / coef_sigma

SMEM = pl.BlockSpec(memory_space=pltpu.SMEM)
VMEM = pl.BlockSpec(memory_space=pltpu.VMEM)


def tile_iota(dim):
    return lax.broadcasted_iota(jnp.int32, (8, 128), dim)


def split_rows(rows):
    high = rows.astype(BF).astype(F32)
    rest = rows - high
    mid = rest.astype(BF).astype(F32)
    return high, mid, rest - mid


def panel_features(rows):
    high, mid, low = split_rows(rows)
    return jnp.concatenate([high, high, high, mid, mid, low], 0).astype(BF)


def cell_features(rows):
    high, mid, low = split_rows(rows)
    return jnp.concatenate([high, mid, low, high, mid, high], 0).astype(BF)


def edge_row(value, low_span):
    return jnp.where(low_span, value[7:8], value[0:1])


def first_column(value):
    return jnp.broadcast_to(value[:, 0:1], (8, 128))


def even_place():
    return lax.rem(lax.axis_index("wrap"), 2) == 0


def missing_term(value, beside):
    change = beside - value
    flux = (viscous + value) * change + (0.5 * (1.0 + coef_cb2)) * change * change
    return (0.5 * time_step / coef_sigma) * flux


def prep_kernel(
    xyz_hbm,
    size_hbm,
    nu_hbm,
    chunks_ref,
    pair_ref,
    beside_ref,
    xyz_ref,
    size_ref,
    nu_ref,
    sems,
):
    pairs = ((xyz_hbm, xyz_ref), (size_hbm, size_ref), (nu_hbm, nu_ref))
    copies = [pltpu.make_async_copy(*pair, sems.at[n]) for n, pair in enumerate(pairs)]
    for copy in copies:
        copy.start()
    for copy in copies:
        copy.wait()
    parts = []
    for block in range(size_ref.shape[1] // PBS):
        lanes = slice(block * PBS, (block + 1) * PBS)
        xyz = xyz_ref[:, lanes]
        size = size_ref[:, lanes]
        parts += [xyz, jnp.sum(xyz * xyz, axis=0, keepdims=True) + size * size]
    low_span = lax.axis_index("span") == 0
    rows = nu_ref.shape[0]
    lane = tile_iota(1)
    column = jnp.zeros((8, 128), F32)
    for row in range(rows):
        value = nu_ref[row]
        beside_ref[row : row + 1, :] = edge_row(value, low_span)
        column = jnp.where(lane == row, first_column(value), column)
    pair_ref[...] = jnp.where(even_place(), nu_ref[rows - 1], nu_ref[0])
    chunk = jnp.concatenate(parts + [column], 0)
    for n in range(chunks_ref.shape[0]):
        chunks_ref[n] = chunk


class Halo:
    def __init__(self, nu_ref, pair, after, beside_ref, column, padded_ref, ghost_ref):
        devices = lax.axis_size("wrap")
        place = lax.axis_index("wrap")
        rows = nu_ref.shape[0]
        self.rows = rows
        self.low_span = lax.axis_index("span") == 0
        self.padded, self.ghost, self.beside = padded_ref, ghost_ref, beside_ref
        lower = jnp.where(even_place(), after, pair)
        upper = jnp.where(even_place(), pair, after)
        padded_ref[0] = jnp.where(place == 0, nu_ref[0], lower)
        padded_ref[rows + 1] = jnp.where(place == devices - 1, nu_ref[rows - 1], upper)
        in_wake = (place < devices // 4) | (place >= devices - devices // 4)
        self.in_wake = in_wake
        for row in range(rows):
            value = nu_ref[row]
            padded_ref[row + 1] = value
            partner = jnp.broadcast_to(column[:, rows - 1 - row : rows - row], (8, 128))
            ghost_ref[row] = jnp.where(in_wake, partner, -value)

    def rate(self, row, squares, vorticity):
        value = self.padded[row + 1]
        sub, lane = tile_iota(0), tile_iota(1)
        across = jnp.broadcast_to(self.beside[pl.ds(row, 1), :], (8, 128))
        span_low = jnp.where(self.low_span, value, across)
        span_high = jnp.where(self.low_span, across, value)
        others = (
            self.padded[row],
            self.padded[row + 2],
            jnp.where(sub == 0, span_low, pltpu.roll(value, 1, 0)),
            jnp.where(sub == 7, span_high, pltpu.roll(value, 7, 0)),
            jnp.where(lane == 0, self.ghost[row], pltpu.roll(value, 1, 1)),
            jnp.where(lane == 127, value, pltpu.roll(value, 127, 1)),
        )
        sums = jnp.zeros_like(value)
        squared = jnp.zeros_like(value)
        for other in others:
            change = other - value
            sums = sums + change
            squared = squared + change * change
        flux = (viscous + value) * sums + (0.5 * (1.0 + coef_cb2)) * squared
        scaled = coef_kappa**2 * squares
        modified = vorticity + value / scaled
        ratio = value / (modified * scaled)
        ratio2 = ratio * ratio
        shaped = ratio + coef_cw2 * (ratio2 * ratio2 * ratio2 - ratio)
        shaped2 = shaped * shaped
        base = (1.0 + coef_cw3**6) / (shaped2 * shaped2 * shaped2 + coef_cw3**6)
        factor = shaped * jnp.exp(jnp.log(base) * (1.0 / 6.0))
        return (
            flux / coef_sigma
            + coef_cb1 * modified * value
            - coef_cw1 * factor * value * value / squares
        )


def build_table(halves, table_ref):
    place = lax.axis_index("wrap")
    own_blocks = table_ref.shape[0] // lax.axis_size("wrap")
    groups = lax.axis_size("wrap") >> GROUP_BIT
    low = place & ((1 << GROUP_BIT) - 1)

    def body(group, carry):
        for half, pieces in enumerate(halves):
            for ref, mask in zip(pieces, (0,) + Y_MASKS):
                base = ((group << GROUP_BIT) | (low ^ mask ^ half)) * own_blocks
                for pair in range(own_blocks // 2):
                    start = pl.multiple_of(group * own_blocks * 4 + pair * 8, 8)
                    rows = ref[pl.ds(start, 8), :]
                    table_ref[base + pair * 2] = panel_features(rows)
                    table_ref[base + pair * 2 + 1] = panel_features(pltpu.roll(rows, 4, 0))
        return carry

    lax.fori_loop(0, groups, body, 0)


def nearest_tile(tile, list_ref, cell_ref, table_ref):
    sub = tile_iota(0)
    unit = jnp.where(sub == 3, 1.0, 0.0)
    xyz = [cell_ref[component, tile] for component in range(3)]
    twice = [-2.0 * part for part in xyz]
    found = []
    for line in range(8):
        rows = unit
        for component in range(3):
            spread = jnp.broadcast_to(twice[component][line : line + 1], (8, 128))
            rows = jnp.where(sub == component, spread, rows)
        cells = cell_features(rows).T
        nearest = None
        for slot in range(0, 8, 2):
            first = list_ref[(tile * 8 + line) * 8 + slot]
            second = list_ref[(tile * 8 + line) * 8 + slot + 1]
            panels = jnp.concatenate([table_ref[first], table_ref[second]], 1)
            value = jnp.dot(cells, panels, preferred_element_type=F32)
            value = jnp.minimum(value[:, :128], value[:, 128:])
            nearest = value if nearest is None else jnp.minimum(nearest, value)
        turned = jnp.min(nearest.T.reshape(16, 8, 128), axis=0)
        found.append(jnp.min(turned, axis=0, keepdims=True))
    norm = xyz[0] * xyz[0] + xyz[1] * xyz[1] + xyz[2] * xyz[2]
    return jnp.concatenate(found, 0) + norm


def main_kernel(
    list_ref,
    own0_ref,
    own1_ref,
    own2_ref,
    own3_ref,
    other0_ref,
    other1_ref,
    other2_ref,
    other3_ref,
    cell_ref,
    nu_ref,
    vorticity_ref,
    beside_ref,
    squares_ref,
    middle_ref,
    pair_out,
    next_out,
    beside_out,
    column_out,
    table_ref,
    padded_ref,
    ghost_ref,
):
    total = own0_ref.shape[0]
    column = other2_ref[total : total + 8]
    pair = other0_ref[total : total + 8]
    tiles = nu_ref.shape[0]
    even = even_place()
    open_row = jnp.where(even, nu_ref[0], nu_ref[tiles - 1])
    halo = Halo(nu_ref, pair, open_row, beside_ref, column, padded_ref, ghost_ref)
    open_side = jnp.where(even, beside_ref[0:1], beside_ref[tiles - 1 : tiles])
    open_partner = jnp.where(even, column[:, tiles - 1 : tiles], column[:, 0:1])
    next_out[0:8] = open_row
    next_out[16:24] = jnp.broadcast_to(open_side, (8, 128))
    next_out[24:32] = jnp.broadcast_to(open_partner, (8, 128))
    own = (own0_ref, own1_ref, own2_ref, own3_ref)
    other = (other0_ref, other1_ref, other2_ref, other3_ref)
    build_table((own, other), table_ref)
    per_step = LINES_PER_STEP // 8

    def body(step, column):
        lane = tile_iota(1)
        for part in range(per_step):
            tile = step * per_step + part
            squares = nearest_tile(tile, list_ref, cell_ref, table_ref)
            squares_ref[tile] = squares
            rate = halo.rate(tile, squares, vorticity_ref[tile])
            middle = nu_ref[tile] + 0.5 * time_step * rate
            middle_ref[tile] = middle
            beside_out[pl.ds(tile, 1), :] = edge_row(middle, halo.low_span)
            column = jnp.where(lane == tile, first_column(middle), column)
        return column

    column = lax.fori_loop(0, tiles // per_step, body, jnp.zeros((8, 128), F32))
    for row in range(0, column_out.shape[0], 8):
        column_out[row : row + 8] = column
    beside_out[tiles:] = jnp.zeros((beside_out.shape[0] - tiles, 128), F32)
    first, last = middle_ref[0], middle_ref[tiles - 1]
    pair_out[...] = jnp.where(even, last, first)
    next_out[8:16] = jnp.where(even, first, last)


def last_kernel(
    middle_ref,
    nu_ref,
    squares_ref,
    vorticity_ref,
    pair_ref,
    mine_ref,
    theirs_ref,
    beside_ref,
    column_ref,
    out_ref,
    padded_ref,
    ghost_ref,
    side_ref,
):
    place = lax.axis_index("wrap")
    rows = nu_ref.shape[0]
    even = even_place()
    inner = (place > 0) & (place < lax.axis_size("wrap") - 1)
    value, partial, side, partner = (mine_ref[n : n + 8] for n in range(0, 32, 8))
    other, other_partial, other_side, other_partner = (theirs_ref[n : n + 8] for n in range(0, 32, 8))
    after = other_partial + missing_term(other, value)
    halo = Halo(
        middle_ref, pair_ref[...], after, beside_ref, column_ref[0:8], padded_ref, ghost_ref
    )
    side_ref[...] = beside_ref[0:rows]
    halo.beside = side_ref
    fixed = partial + missing_term(value, other)
    side_term = missing_term(side, other_side)[0:1]
    partner_term = missing_term(partner, other_partner)
    for row, here in ((0, inner & even), (rows - 1, inner & ~even)):
        own = jnp.where(here, fixed, padded_ref[row + 1])
        padded_ref[row + 1] = own
        ghost = ghost_ref[row] + jnp.where(here, partner_term, 0.0)
        ghost_ref[row] = jnp.where(halo.in_wake, ghost, -own)
        side_ref[row : row + 1] = side_ref[row : row + 1] + jnp.where(here, side_term, 0.0)
    for row in range(rows):
        rate = halo.rate(row, squares_ref[row], vorticity_ref[row])
        out_ref[row] = nu_ref[row] + time_step * rate


def swap_mask(block, mask):
    return lax.ppermute(block, "wrap", [(i, i ^ mask) for i in range(lax.axis_size("wrap"))])


def swap_next(block):
    devices = lax.axis_size("wrap")
    pairs = [(i, (i + 1) % devices) for i in range(1, devices, 2)]
    return lax.ppermute(block, "wrap", pairs + [(j, i) for i, j in pairs])


def swap_span(block):
    return lax.ppermute(block, "span", [(0, 1), (1, 0)])


def gather(chunks, pair, beside):
    devices = lax.axis_size("wrap")
    groups, rows, lanes = chunks.shape
    size = rows - 8
    members = [[low + (n << GROUP_BIT) for n in range(groups)] for low in range(devices // groups)]
    chunks = lax.all_to_all(chunks, "wrap", 0, 0, tiled=True, axis_index_groups=members)
    chunks, beside = lax.optimization_barrier((chunks, swap_span(beside)))
    shard = chunks[:, :size].reshape(groups * size, lanes)
    opposite = groups - 1 - (lax.axis_index("wrap") >> GROUP_BIT)
    column = lax.dynamic_slice(chunks, (opposite, size, 0), (1, 8, lanes))[0]
    own = [
        shard,
        swap_mask(shard, Y_MASKS[0]),
        swap_mask(jnp.concatenate([shard, column], 0), Y_MASKS[1]),
        swap_mask(jnp.concatenate([shard, column, column], 0), Y_MASKS[2]),
    ]
    other = [swap_mask(jnp.concatenate([shard, pair], 0), 1)]
    other += [swap_mask(piece, 1) for piece in own[1:]]
    return own, other, beside


def shards(cell_xyz, panel_xyz, panel_size, block_lists, nu_field, vorticity):
    devices = lax.axis_size("wrap")
    rows, span, cells = nu_field.shape
    own_blocks = panel_size.shape[0] // PBS
    tile = jax.ShapeDtypeStruct((span, cells), F32)
    field = jax.ShapeDtypeStruct(nu_field.shape, F32)
    side = jax.ShapeDtypeStruct((rows, cells), F32)
    opened = jax.ShapeDtypeStruct((32, cells), F32)
    edges = (
        tile,
        opened,
        jax.ShapeDtypeStruct((SIDE_ROWS, cells), F32),
        jax.ShapeDtypeStruct((COLUMN_ROWS, cells), F32),
    )
    scratch = [pltpu.VMEM((rows + 2, span, cells), F32), pltpu.VMEM(nu_field.shape, F32)]

    groups = devices >> GROUP_BIT
    inputs = (panel_xyz, panel_size[None], nu_field)
    chunks, pair, beside = pl.pallas_call(
        prep_kernel,
        out_shape=(jax.ShapeDtypeStruct((groups, 4 * own_blocks + 8, PBS), F32), tile, side),
        in_specs=[pl.BlockSpec(memory_space=pltpu.HBM)] * 3,
        out_specs=(VMEM,) * 3,
        scratch_shapes=[
            pltpu.VMEM(panel_xyz.shape, F32),
            pltpu.VMEM((1,) + panel_size.shape, F32),
            pltpu.VMEM(nu_field.shape, F32),
            pltpu.SemaphoreType.DMA((3,)),
        ],
        compiler_params=pltpu.CompilerParams(vmem_limit_bytes=4 * 2**20),
        name="prep",
    )(*(pltpu.with_memory_space_constraint(x, pltpu.HBM) for x in inputs))
    own, other, beside = gather(chunks, pair, beside)

    squares, middle, pair, mine, sides, column = pl.pallas_call(
        main_kernel,
        out_shape=(field, field) + edges,
        in_specs=[SMEM] + [VMEM] * 12,
        out_specs=(VMEM,) * 6,
        scratch_shapes=[pltpu.VMEM((devices * own_blocks, FEATS, PBS), BF)] + scratch,
        compiler_params=pltpu.CompilerParams(vmem_limit_bytes=24 * 2**20),
        cost_estimate=pl.CostEstimate(
            flops=2 * 128 * rows * span * cells * block_lists.shape[2] * PBS,
            bytes_accessed=4 * 2**20,
            transcendentals=0,
        ),
        name="main",
    )(block_lists.reshape(-1), *own, *other, cell_xyz, nu_field, vorticity, beside)
    column = swap_mask(column, devices - 1)
    theirs = swap_next(mine)
    sides = swap_span(sides)
    pair = swap_mask(pair, 1)

    nu_next = pl.pallas_call(
        last_kernel,
        out_shape=field,
        in_specs=[VMEM] * 9,
        out_specs=VMEM,
        scratch_shapes=scratch + [pltpu.VMEM(side.shape, F32)],
        compiler_params=pltpu.CompilerParams(vmem_limit_bytes=8 * 2**20),
        name="last",
    )(middle, nu_field, squares, vorticity, pair, mine, theirs, sides, column)
    return (nu_next, jnp.sqrt(squares))


def solution(mesh):
    in_specs = (
        P(None, "wrap", "span", None),
        P(None, "wrap"),
        P("wrap"),
        P("wrap", "span", None),
        P("wrap", "span", None),
        P("wrap", "span", None),
    )
    out_specs = (P("wrap", "span", None), P("wrap", "span", None))
    return jax.shard_map(shards, mesh=mesh, in_specs=in_specs, out_specs=out_specs, check_vma=False)
```

```python
import functools

import jax
import jax.numpy as jnp
from jax import lax
from jax.experimental import pallas as pl
from jax.experimental.pallas import tpu as pltpu
from jax.sharding import PartitionSpec as P

BF = jnp.bfloat16
F32 = jnp.float32
PBS = 128
FEATS = 48
LINES_PER_STEP = 128
COLUMN_ROWS = 48
SIDE_ROWS = 40
GROUP_BIT = 3
Y_MASKS = (2, 6, 4)

coef_cb1 = 0.1355
coef_cb2 = 0.622
coef_sigma = 2.0 / 3.0
coef_kappa = 0.41
coef_cw2 = 0.3
coef_cw3 = 2.0
viscous = 1.0
time_step = 0.03
coef_cw1 = coef_cb1 / coef_kappa**2 + (1.0 + coef_cb2) / coef_sigma

SMEM = pl.BlockSpec(memory_space=pltpu.SMEM)
VMEM = pl.BlockSpec(memory_space=pltpu.VMEM)


def tile_iota(dim):
    return lax.broadcasted_iota(jnp.int32, (8, 128), dim)


def split_rows(rows):
    high = rows.astype(BF).astype(F32)
    rest = rows - high
    mid = rest.astype(BF).astype(F32)
    return high, mid, rest - mid


def panel_features(rows):
    high, mid, low = split_rows(rows)
    return jnp.concatenate([high, high, high, mid, mid, low], 0).astype(BF)


def cell_features(rows):
    high, mid, low = split_rows(rows)
    return jnp.concatenate([high, mid, low, high, mid, high], 0).astype(BF)


def edge_row(value, low_span):
    return jnp.where(low_span, value[7:8], value[0:1])


def first_column(value):
    return jnp.broadcast_to(value[:, 0:1], (8, 128))


def even_place():
    return lax.rem(lax.axis_index("wrap"), 2) == 0


def missing_term(value, beside):
    change = beside - value
    flux = (viscous + value) * change + (0.5 * (1.0 + coef_cb2)) * change * change
    return (0.5 * time_step / coef_sigma) * flux


def prep_kernel(
    xyz_hbm,
    size_hbm,
    nu_hbm,
    chunks_ref,
    pair_ref,
    beside_ref,
    xyz_ref,
    size_ref,
    nu_ref,
    sems,
):
    pairs = ((xyz_hbm, xyz_ref), (size_hbm, size_ref), (nu_hbm, nu_ref))
    copies = [pltpu.make_async_copy(*pair, sems.at[n]) for n, pair in enumerate(pairs)]
    for copy in copies:
        copy.start()
    for copy in copies:
        copy.wait()
    parts = []
    for block in range(size_ref.shape[1] // PBS):
        lanes = slice(block * PBS, (block + 1) * PBS)
        xyz = xyz_ref[:, lanes]
        size = size_ref[:, lanes]
        parts += [xyz, jnp.sum(xyz * xyz, axis=0, keepdims=True) + size * size]
    low_span = lax.axis_index("span") == 0
    rows = nu_ref.shape[0]
    lane = tile_iota(1)
    column = jnp.zeros((8, 128), F32)
    for row in range(rows):
        value = nu_ref[row]
        beside_ref[row : row + 1, :] = edge_row(value, low_span)
        column = jnp.where(lane == row, first_column(value), column)
    pair_ref[...] = jnp.where(even_place(), nu_ref[rows - 1], nu_ref[0])
    chunk = jnp.concatenate(parts + [column], 0)
    for n in range(chunks_ref.shape[0]):
        chunks_ref[n] = chunk


class Halo:
    def __init__(self, nu_ref, pair, after, beside_ref, column, padded_ref, ghost_ref):
        devices = lax.axis_size("wrap")
        place = lax.axis_index("wrap")
        rows = nu_ref.shape[0]
        self.rows = rows
        self.low_span = lax.axis_index("span") == 0
        self.padded, self.ghost, self.beside = padded_ref, ghost_ref, beside_ref
        lower = jnp.where(even_place(), after, pair)
        upper = jnp.where(even_place(), pair, after)
        padded_ref[0] = jnp.where(place == 0, nu_ref[0], lower)
        padded_ref[rows + 1] = jnp.where(place == devices - 1, nu_ref[rows - 1], upper)
        in_wake = (place < devices // 4) | (place >= devices - devices // 4)
        self.in_wake = in_wake
        for row in range(rows):
            value = nu_ref[row]
            padded_ref[row + 1] = value
            partner = jnp.broadcast_to(column[:, rows - 1 - row : rows - row], (8, 128))
            ghost_ref[row] = jnp.where(in_wake, partner, -value)

    def rate(self, row, squares, vorticity):
        value = self.padded[row + 1]
        sub, lane = tile_iota(0), tile_iota(1)
        across = jnp.broadcast_to(self.beside[pl.ds(row, 1), :], (8, 128))
        span_low = jnp.where(self.low_span, value, across)
        span_high = jnp.where(self.low_span, across, value)
        others = (
            self.padded[row],
            self.padded[row + 2],
            jnp.where(sub == 0, span_low, pltpu.roll(value, 1, 0)),
            jnp.where(sub == 7, span_high, pltpu.roll(value, 7, 0)),
            jnp.where(lane == 0, self.ghost[row], pltpu.roll(value, 1, 1)),
            jnp.where(lane == 127, value, pltpu.roll(value, 127, 1)),
        )
        sums = jnp.zeros_like(value)
        squared = jnp.zeros_like(value)
        for other in others:
            change = other - value
            sums = sums + change
            squared = squared + change * change
        flux = (viscous + value) * sums + (0.5 * (1.0 + coef_cb2)) * squared
        scaled = coef_kappa**2 * squares
        modified = vorticity + value / scaled
        ratio = value / (modified * scaled)
        ratio2 = ratio * ratio
        shaped = ratio + coef_cw2 * (ratio2 * ratio2 * ratio2 - ratio)
        shaped2 = shaped * shaped
        base = (1.0 + coef_cw3**6) / (shaped2 * shaped2 * shaped2 + coef_cw3**6)
        factor = shaped * jnp.exp(jnp.log(base) * (1.0 / 6.0))
        return (
            flux / coef_sigma
            + coef_cb1 * modified * value
            - coef_cw1 * factor * value * value / squares
        )


def build_table(halves, table_ref):
    place = lax.axis_index("wrap")
    own_blocks = table_ref.shape[0] // lax.axis_size("wrap")
    groups = lax.axis_size("wrap") >> GROUP_BIT
    low = place & ((1 << GROUP_BIT) - 1)

    def body(group, carry):
        for half, pieces in enumerate(halves):
            for ref, mask in zip(pieces, (0,) + Y_MASKS):
                base = ((group << GROUP_BIT) | (low ^ mask ^ half)) * own_blocks
                for pair in range(own_blocks // 2):
                    start = pl.multiple_of(group * own_blocks * 4 + pair * 8, 8)
                    rows = ref[pl.ds(start, 8), :]
                    table_ref[base + pair * 2] = panel_features(rows)
                    table_ref[base + pair * 2 + 1] = panel_features(pltpu.roll(rows, 4, 0))
        return carry

    lax.fori_loop(0, groups, body, 0, unroll=2)


def nearest_tile(tile, list_ref, cell_ref, table_ref):
    sub = tile_iota(0)
    unit = jnp.where(sub == 3, 1.0, 0.0)
    xyz = [cell_ref[component, tile] for component in range(3)]
    twice = [-2.0 * part for part in xyz]
    found = []
    for line in range(8):
        rows = unit
        for component in range(3):
            spread = jnp.broadcast_to(twice[component][line : line + 1], (8, 128))
            rows = jnp.where(sub == component, spread, rows)
        cells = cell_features(rows).T
        nearest = None
        for slot in range(0, 8, 2):
            first = list_ref[(tile * 8 + line) * 8 + slot]
            second = list_ref[(tile * 8 + line) * 8 + slot + 1]
            panels = jnp.concatenate([table_ref[first], table_ref[second]], 1)
            value = jnp.dot(cells, panels, preferred_element_type=F32)
            value = jnp.minimum(value[:, :128], value[:, 128:])
            nearest = value if nearest is None else jnp.minimum(nearest, value)
        turned = jnp.min(nearest.T.reshape(16, 8, 128), axis=0)
        found.append(jnp.min(turned, axis=0, keepdims=True))
    norm = xyz[0] * xyz[0] + xyz[1] * xyz[1] + xyz[2] * xyz[2]
    return jnp.concatenate(found, 0) + norm


def main_kernel(
    list_ref,
    own0_ref,
    own1_ref,
    own2_ref,
    own3_ref,
    other0_ref,
    other1_ref,
    other2_ref,
    other3_ref,
    cell_ref,
    nu_ref,
    vorticity_ref,
    beside_ref,
    squares_ref,
    middle_ref,
    pair_out,
    next_out,
    beside_out,
    column_out,
    table_ref,
    padded_ref,
    ghost_ref,
):
    total = own0_ref.shape[0]
    column = other2_ref[total : total + 8]
    pair = other0_ref[total : total + 8]
    tiles = nu_ref.shape[0]
    even = even_place()
    open_row = jnp.where(even, nu_ref[0], nu_ref[tiles - 1])
    halo = Halo(nu_ref, pair, open_row, beside_ref, column, padded_ref, ghost_ref)
    open_side = jnp.where(even, beside_ref[0:1], beside_ref[tiles - 1 : tiles])
    open_partner = jnp.where(even, column[:, tiles - 1 : tiles], column[:, 0:1])
    next_out[0:8] = open_row
    next_out[16:24] = jnp.broadcast_to(open_side, (8, 128))
    next_out[24:32] = jnp.broadcast_to(open_partner, (8, 128))
    own = (own0_ref, own1_ref, own2_ref, own3_ref)
    other = (other0_ref, other1_ref, other2_ref, other3_ref)
    build_table((own, other), table_ref)
    per_step = LINES_PER_STEP // 8

    def body(step, column):
        lane = tile_iota(1)
        for part in range(per_step):
            tile = step * per_step + part
            squares = nearest_tile(tile, list_ref, cell_ref, table_ref)
            squares_ref[tile] = squares
            rate = halo.rate(tile, squares, vorticity_ref[tile])
            middle = nu_ref[tile] + 0.5 * time_step * rate
            middle_ref[tile] = middle
            beside_out[pl.ds(tile, 1), :] = edge_row(middle, halo.low_span)
            column = jnp.where(lane == tile, first_column(middle), column)
        return column

    column = lax.fori_loop(0, tiles // per_step, body, jnp.zeros((8, 128), F32))
    for row in range(0, column_out.shape[0], 8):
        column_out[row : row + 8] = column
    beside_out[tiles:] = jnp.zeros((beside_out.shape[0] - tiles, 128), F32)
    first, last = middle_ref[0], middle_ref[tiles - 1]
    pair_out[...] = jnp.where(even, last, first)
    next_out[8:16] = jnp.where(even, first, last)


def last_kernel(
    middle_ref,
    nu_ref,
    squares_ref,
    vorticity_ref,
    pair_ref,
    mine_ref,
    theirs_ref,
    beside_ref,
    column_ref,
    out_ref,
    padded_ref,
    ghost_ref,
    side_ref,
):
    place = lax.axis_index("wrap")
    rows = nu_ref.shape[0]
    even = even_place()
    inner = (place > 0) & (place < lax.axis_size("wrap") - 1)
    value, partial, side, partner = (mine_ref[n : n + 8] for n in range(0, 32, 8))
    other, other_partial, other_side, other_partner = (theirs_ref[n : n + 8] for n in range(0, 32, 8))
    after = other_partial + missing_term(other, value)
    halo = Halo(
        middle_ref, pair_ref[...], after, beside_ref, column_ref[0:8], padded_ref, ghost_ref
    )
    side_ref[...] = beside_ref[0:rows]
    halo.beside = side_ref
    fixed = partial + missing_term(value, other)
    side_term = missing_term(side, other_side)[0:1]
    partner_term = missing_term(partner, other_partner)
    for row, here in ((0, inner & even), (rows - 1, inner & ~even)):
        own = jnp.where(here, fixed, padded_ref[row + 1])
        padded_ref[row + 1] = own
        ghost = ghost_ref[row] + jnp.where(here, partner_term, 0.0)
        ghost_ref[row] = jnp.where(halo.in_wake, ghost, -own)
        side_ref[row : row + 1] = side_ref[row : row + 1] + jnp.where(here, side_term, 0.0)
    for row in range(rows):
        rate = halo.rate(row, squares_ref[row], vorticity_ref[row])
        out_ref[row] = nu_ref[row] + time_step * rate


def swap_mask(block, mask):
    return lax.ppermute(block, "wrap", [(i, i ^ mask) for i in range(lax.axis_size("wrap"))])


def swap_next(block):
    devices = lax.axis_size("wrap")
    pairs = [(i, (i + 1) % devices) for i in range(1, devices, 2)]
    return lax.ppermute(block, "wrap", pairs + [(j, i) for i, j in pairs])


def swap_span(block):
    return lax.ppermute(block, "span", [(0, 1), (1, 0)])


def gather(chunks, pair, beside):
    devices = lax.axis_size("wrap")
    groups, rows, lanes = chunks.shape
    size = rows - 8
    members = [[low + (n << GROUP_BIT) for n in range(groups)] for low in range(devices // groups)]
    chunks = lax.all_to_all(chunks, "wrap", 0, 0, tiled=True, axis_index_groups=members)
    chunks, beside = lax.optimization_barrier((chunks, swap_span(beside)))
    shard = chunks[:, :size].reshape(groups * size, lanes)
    opposite = groups - 1 - (lax.axis_index("wrap") >> GROUP_BIT)
    column = lax.dynamic_slice(chunks, (opposite, size, 0), (1, 8, lanes))[0]
    own = [
        shard,
        swap_mask(shard, Y_MASKS[0]),
        swap_mask(jnp.concatenate([shard, column], 0), Y_MASKS[1]),
        swap_mask(jnp.concatenate([shard, column, column], 0), Y_MASKS[2]),
    ]
    other = [swap_mask(jnp.concatenate([shard, pair], 0), 1)]
    other += [swap_mask(piece, 1) for piece in own[1:]]
    return own, other, beside


def shards(cell_xyz, panel_xyz, panel_size, block_lists, nu_field, vorticity):
    devices = lax.axis_size("wrap")
    rows, span, cells = nu_field.shape
    own_blocks = panel_size.shape[0] // PBS
    tile = jax.ShapeDtypeStruct((span, cells), F32)
    field = jax.ShapeDtypeStruct(nu_field.shape, F32)
    side = jax.ShapeDtypeStruct((rows, cells), F32)
    opened = jax.ShapeDtypeStruct((32, cells), F32)
    edges = (
        tile,
        opened,
        jax.ShapeDtypeStruct((SIDE_ROWS, cells), F32),
        jax.ShapeDtypeStruct((COLUMN_ROWS, cells), F32),
    )
    scratch = [pltpu.VMEM((rows + 2, span, cells), F32), pltpu.VMEM(nu_field.shape, F32)]

    groups = devices >> GROUP_BIT
    inputs = (panel_xyz, panel_size[None], nu_field)
    chunks, pair, beside = pl.pallas_call(
        prep_kernel,
        out_shape=(jax.ShapeDtypeStruct((groups, 4 * own_blocks + 8, PBS), F32), tile, side),
        in_specs=[pl.BlockSpec(memory_space=pltpu.HBM)] * 3,
        out_specs=(VMEM,) * 3,
        scratch_shapes=[
            pltpu.VMEM(panel_xyz.shape, F32),
            pltpu.VMEM((1,) + panel_size.shape, F32),
            pltpu.VMEM(nu_field.shape, F32),
            pltpu.SemaphoreType.DMA((3,)),
        ],
        compiler_params=pltpu.CompilerParams(vmem_limit_bytes=4 * 2**20),
        name="prep",
    )(*(pltpu.with_memory_space_constraint(x, pltpu.HBM) for x in inputs))
    own, other, beside = gather(chunks, pair, beside)

    squares, middle, pair, mine, sides, column = pl.pallas_call(
        main_kernel,
        out_shape=(field, field) + edges,
        in_specs=[SMEM] + [VMEM] * 12,
        out_specs=(VMEM,) * 6,
        scratch_shapes=[pltpu.VMEM((devices * own_blocks, FEATS, PBS), BF)] + scratch,
        compiler_params=pltpu.CompilerParams(vmem_limit_bytes=24 * 2**20),
        cost_estimate=pl.CostEstimate(
            flops=2 * 128 * rows * span * cells * block_lists.shape[2] * PBS,
            bytes_accessed=4 * 2**20,
            transcendentals=0,
        ),
        name="main",
    )(block_lists.reshape(-1), *own, *other, cell_xyz, nu_field, vorticity, beside)
    column = swap_mask(column, devices - 1)
    theirs = swap_next(mine)
    sides = swap_span(sides)
    pair = swap_mask(pair, 1)

    nu_next = pl.pallas_call(
        last_kernel,
        out_shape=field,
        in_specs=[VMEM] * 9,
        out_specs=VMEM,
        scratch_shapes=scratch + [pltpu.VMEM(side.shape, F32)],
        compiler_params=pltpu.CompilerParams(vmem_limit_bytes=8 * 2**20),
        name="last",
    )(middle, nu_field, squares, vorticity, pair, mine, theirs, sides, column)
    return (nu_next, jnp.sqrt(squares))


def solution(mesh):
    in_specs = (
        P(None, "wrap", "span", None),
        P(None, "wrap"),
        P("wrap"),
        P("wrap", "span", None),
        P("wrap", "span", None),
        P("wrap", "span", None),
    )
    out_specs = (P("wrap", "span", None), P("wrap", "span", None))
    return jax.shard_map(shards, mesh=mesh, in_specs=in_specs, out_specs=out_specs, check_vma=False)
```
